32 devices in a mesh: section: 2 (over y), dp: 16 (over z, x, core).
Axes of the slice: x: 2, y: 2, z: 4, core: 2. Of those that a mesh axis runs over, the one named last changes fastest.
Arguments:
- level_input: bfloat16 [4, 16, 64, 768], P(None, 'dp', 'section'), may hold values from -6 to 6
- cotangent: bfloat16 [4, 16, 64, 768], P(None, 'dp', 'section'), may hold values from -6 to 6
- class_table: bfloat16 [1000, 768], P(None, 'dp'), may hold values from -6 to 6
- conv_in: bfloat16 [2, 13824, 768], P('section', 'dp'), may hold values from -0.078125 to 0.078125
- conv_out: bfloat16 [2, 6912, 768], P('section', 'dp'), may hold values from -0.078125 to 0.078125
- embed_proj: bfloat16 [2, 768, 1536], P('section', 'dp'), may hold values from -0.21875 to 0.21875
- skip_proj: bfloat16 [2, 1536, 768], P('section', 'dp'), may hold values from -0.15625 to 0.15625
- qkv_proj: bfloat16 [2, 768, 2304], P('section', 'dp'), may hold values from -0.21875 to 0.21875
- out_proj: bfloat16 [2, 768, 768], P('section', 'dp'), may hold values from -0.625 to 0.625
- gains: bfloat16 [2, 3072], P('section', 'dp'), may hold values from 0.099609375 to 1.8984375
- biases: bfloat16 [2, 9216], P('section', 'dp'), may hold values from -3 to 3
- noise_pairs: int32 [4, 16, 2], P(None, 'dp'), may hold values from 0 to 39
- classes: int32 [4, 16], P(None, 'dp'), may hold values from 0 to 999
Outputs:
- level_output: bfloat16 [4, 16, 64, 768], P(None, 'dp', 'section')
- input_grad: float32 [4, 16, 64, 768], P(None, 'dp', 'section')
- class_table_grad: float32 [1000, 768], P(None, 'dp')
- conv_in_grad: float32 [2, 13824, 768], P('section', 'dp')
- conv_out_grad: float32 [2, 6912, 768], P('section', 'dp')
- embed_proj_grad: float32 [2, 768, 1536], P('section', 'dp')
- skip_proj_grad: float32 [2, 1536, 768], P('section', 'dp')
- qkv_proj_grad: float32 [2, 768, 2304], P('section', 'dp')
- out_proj_grad: float32 [2, 768, 768], P('section', 'dp')
- gains_grad: float32 [2, 3072], P('section', 'dp')
- biases_grad: float32 [2, 9216], P('section', 'dp')
The draws below stay inside these ranges and needn't reach their ends.
All inputs are finite; a program needn't handle non-finite values.
Results may differ from the reference program's by a relative error of at most 0.023.
Values may be sent and summed in bfloat16 or wider, within the bound.
No kernel may reach another device: no remote copies, remote signals or barrier semaphores. Data moves between devices by JAX's collectives and lax.ppermute only.
A program may use at most 256 MiB of HBM per device.

```python
import math
from functools import partial
import jax
import jax.numpy as jnp
from jax import lax

WIDTH = 768
EMBED = 768
CLASSES = 1000
HEAD_DIM = 64
GROUPS = 32
SIDE = 8
LEVELS = 40
MICRO = 4
SECTIONS = 2
IMAGES = 16
PIXELS = 64


def place_ends(values, own_key, least, largest):
    longest = values.shape.index(max(values.shape))
    spots = []
    for shift in (0, 1):
        where = [jax.random.randint(jax.random.fold_in(own_key, axis), (), 0, length) for axis, length in enumerate(values.shape)]
        where[longest] = (where[longest] + shift) % values.shape[longest]
        spots.append(tuple(where))
    return values.at[spots[0]].set(least).at[spots[1]].set(largest)


def with_spikes(values, own_key, source, target, parts, factor):
    owner, partner = [(jnp.arange(values.shape[axis_at]) // (values.shape[axis_at] // parts)).reshape([-1 if axis == axis_at else 1 for axis in range(values.ndim)]) for axis_at in (source, target)]
    chosen = jax.random.permutation(own_key, parts)[partner]
    strong = (owner == chosen) | (owner == (partner + parts // 2) % parts)
    return jnp.where(strong, factor * values, values)


def block_levels(rng, shape, split, least, high):
    level, own = 1.0, jax.random.fold_in(rng, 6)
    for position, shards_of in split:
        draws = jnp.exp(jax.random.uniform(jax.random.fold_in(own, position), (shards_of,), jnp.float32, least / len(split), high / len(split)))
        level = level * jnp.repeat(draws, shape[position] // shards_of).reshape([-1 if axis == position else 1 for axis in range(len(shape))])
    return level


def noise(key, dims, scale, most, split=(), kind=jnp.bfloat16):
    drawn = scale * jax.random.normal(key, dims, jnp.float32)
    if split:
        drawn = drawn * block_levels(key, dims, split, -0.22, 0.18)
    return jnp.clip(drawn, -most, most).astype(kind)


def bell_draw_with(own_key, extent, scale, reach, split, heavy, kind=jnp.bfloat16):
    values = scale * jax.random.normal(own_key, extent, jnp.float32)
    if split:
        values = values * block_levels(own_key, extent, split, -0.22, 0.18)
    return jnp.clip(with_spikes(values, jax.random.fold_in(own_key, 3), *heavy), -reach, reach).astype(kind)


def setup_inputs(seed: int = 0) -> dict:
    key_list = jax.random.split(jax.random.key(seed), 14)
    return {
        "level_input": noise(key_list[0], (MICRO, IMAGES, PIXELS, WIDTH), 1.0, 6.0, ((1, 16), (2, 2))),
        "cotangent": bell_draw_with(key_list[1], (MICRO, IMAGES, PIXELS, WIDTH), 1.0, 6.0, ((1, 16), (2, 2)), (1, 3, 16, 2.0)),
        "class_table": noise(key_list[2], (CLASSES, EMBED), 1.0, 6.0, ((1, 16),)),
        "conv_in": noise(key_list[3], (SECTIONS, 18 * WIDTH, WIDTH), (9 * WIDTH) ** -0.5, 0.078125, ((0, 2), (1, 16))),
        "conv_out": noise(key_list[4], (SECTIONS, 9 * WIDTH, WIDTH), (9 * WIDTH) ** -0.5, 0.078125, ((0, 2), (1, 16))),
        "embed_proj": noise(key_list[5], (SECTIONS, EMBED, 2 * WIDTH), EMBED ** -0.5, 0.21875, ((0, 2), (1, 16))),
        "skip_proj": noise(key_list[6], (SECTIONS, 2 * WIDTH, WIDTH), (2 * WIDTH) ** -0.5, 0.15625, ((0, 2), (1, 16))),
        "qkv_proj": noise(key_list[7], (SECTIONS, WIDTH, 3 * WIDTH), WIDTH ** -0.5, 0.21875, ((0, 2), (1, 16))),
        "out_proj": noise(key_list[8], (SECTIONS, WIDTH, WIDTH), (WIDTH // 8) ** -0.5, 0.625, ((0, 2), (1, 16))),
        "gains": jnp.clip(1.0 + 0.18 * jax.random.normal(key_list[9], (SECTIONS, 4 * WIDTH), jnp.float32), 0.099609375, 1.8984375).astype(jnp.bfloat16),
        "biases": noise(key_list[10], (SECTIONS, 12 * WIDTH), 0.3, 3.0, ((0, 2), (1, 16))),
        "noise_pairs": place_ends(jax.random.randint(key_list[11], (MICRO, IMAGES, 2), 0, LEVELS), jax.random.fold_in(key_list[11], 1), 0, LEVELS - 1).astype(jnp.int32),
        "classes": place_ends(jax.random.randint(key_list[12], (MICRO, IMAGES), 0, CLASSES), jax.random.fold_in(key_list[12], 1), 0, CLASSES - 1).astype(jnp.int32),
    }


@jax.custom_vjp
def low(v):
    return lax.optimization_barrier(v.astype(jnp.bfloat16)).astype(jnp.float32)

@jax.custom_vjp
def low_back(v):
    return v

def low_keep(v):
    return (low(v), None)

def low_pass(kept, grad):
    return (grad,)

def back_keep(v):
    return (v, None)

def back_low(kept, grad):
    return (low(grad),)
low.defvjp(low_keep, low_pass)
low_back.defvjp(back_keep, back_low)
EPS = 1e-05
SIGMA_LOW = 0.002
SIGMA_HIGH = 80.0

def precise(left_side, right_side):
    return jnp.dot(left_side, right_side, precision=lax.Precision.HIGHEST, preferred_element_type=jnp.float32)

def group_norm(values, gain_row, bias_row):
    images, pixels, channels = values.shape
    grouped = values.reshape(images, pixels, GROUPS, channels // GROUPS)
    centered = grouped - lax.optimization_barrier(jnp.mean(grouped, axis=(1, 3), keepdims=True))
    spread = lax.optimization_barrier(jnp.mean(centered * centered, axis=(1, 3), keepdims=True))
    normed = (centered * lax.rsqrt(spread + EPS)).reshape(images, pixels, channels)
    return normed * gain_row + bias_row

def columns(values):
    images, pixels, channels = values.shape
    planes = values.reshape(images, SIDE, SIDE, channels)
    padded = jnp.pad(planes, ((0, 0), (1, 1), (1, 1), (0, 0)))
    pieces = [padded[:, tap_row:tap_row + SIDE, tap_col:tap_col + SIDE, :] for tap_row in range(3) for tap_col in range(3)]
    return jnp.concatenate(pieces, axis=-1).reshape(images * pixels, 9 * channels)

def noise_features(pair_ids):
    fraction = pair_ids.astype(jnp.float32) / (LEVELS - 1)
    top_root = SIGMA_HIGH ** (1.0 / 7.0)
    bottom_root = SIGMA_LOW ** (1.0 / 7.0)
    sigmas = (top_root + fraction * (bottom_root - top_root)) ** 7
    log_scale = 250.0 * jnp.log(sigmas)
    quarter = EMBED // 4
    frequency = jnp.exp(-math.log(10000.0) * jnp.arange(quarter, dtype=jnp.float32) / quarter)
    angles = log_scale[..., None] * frequency
    return jnp.concatenate([jnp.cos(angles[..., 0, :]), jnp.sin(angles[..., 0, :]), jnp.cos(angles[..., 1, :]), jnp.sin(angles[..., 1, :])], axis=-1)

def section_layer(hidden, skipped, embedding, conv_in, conv_out, embed_proj, skip_proj, qkv_proj, out_proj, gains, biases, decoder):
    gain_rows = gains.reshape(4, WIDTH)
    bias_rows = biases.reshape(12, WIDTH)
    images = hidden.shape[0]
    row_count = images * PIXELS
    first_half = low(jax.nn.silu(group_norm(hidden, gain_rows[0], bias_rows[0])))
    if decoder:
        second_half = low(jax.nn.silu(group_norm(skipped, gain_rows[1], bias_rows[1])))
    else:
        second_half = jnp.zeros_like(first_half)
    joined = jnp.concatenate([first_half, second_half], axis=-1)
    conv_one = low_back(precise(columns(joined), conv_in) + bias_rows[2]).reshape(images, PIXELS, WIDTH)
    scale_shift = low_back(precise(low(embedding), embed_proj) + jnp.concatenate([bias_rows[3], bias_rows[4]]))
    normed = group_norm(conv_one, gain_rows[2], bias_rows[5])
    modulated = normed * (1.0 + scale_shift[:, None, :WIDTH]) + scale_shift[:, None, WIDTH:]
    middle = low(jax.nn.silu(modulated))
    conv_two = low_back(precise(columns(middle), conv_out) + bias_rows[6]).reshape(images, PIXELS, WIDTH)
    if decoder:
        paired = jnp.concatenate([hidden, skipped], axis=-1).reshape(row_count, 2 * WIDTH)
        residual = low_back(precise(paired, skip_proj) + bias_rows[7]).reshape(images, PIXELS, WIDTH) + conv_two
    else:
        residual = hidden + conv_two
    attend_in = low(group_norm(residual, gain_rows[3], bias_rows[8])).reshape(row_count, WIDTH)
    bias_qkv = jnp.concatenate([bias_rows[9], jnp.zeros_like(bias_rows[9]), bias_rows[10]])
    project = low(low_back(precise(attend_in, qkv_proj) + bias_qkv))
    head_count = WIDTH // HEAD_DIM
    queries = project[:, :WIDTH].reshape(images, PIXELS, head_count, HEAD_DIM)
    keys_h = project[:, WIDTH:2 * WIDTH].reshape(images, PIXELS, head_count, HEAD_DIM)
    values_h = project[:, 2 * WIDTH:].reshape(images, PIXELS, head_count, HEAD_DIM)
    scores = low_back(jnp.einsum('bqhd,bkhd->bhqk', queries, keys_h, precision=lax.Precision.HIGHEST) / math.sqrt(HEAD_DIM))
    attention = jax.nn.softmax(scores, axis=-1)
    mixed = jnp.einsum('bhqk,bkhd->bqhd', low(attention), values_h, precision=lax.Precision.HIGHEST).reshape(row_count, WIDTH)
    mixed = low(low_back(mixed))
    output = low_back(precise(mixed, out_proj) + bias_rows[11]).reshape(images, PIXELS, WIDTH)
    return residual + output

def forward(level_input, class_table, conv_in, conv_out, embed_proj, skip_proj, qkv_proj, out_proj, gains, biases, noise_pairs, classes):
    encoder_layer = jax.checkpoint(partial(section_layer, decoder=False))
    decoder_layer = jax.checkpoint(partial(section_layer, decoder=True))
    results = []
    for micro_index in range(MICRO):
        embedding = jax.nn.silu(noise_features(noise_pairs[micro_index]) + class_table[classes[micro_index]])
        hidden = level_input[micro_index]
        saved_skips = []
        for section_index in range(SECTIONS):
            if section_index >= SECTIONS // 2:
                skipped = low_back(saved_skips[SECTIONS - 1 - section_index])
                out_now = decoder_layer(hidden, skipped, embedding, conv_in[section_index], conv_out[section_index], embed_proj[section_index], skip_proj[section_index], qkv_proj[section_index], out_proj[section_index], gains[section_index], biases[section_index])
            else:
                out_now = encoder_layer(hidden, jnp.zeros_like(hidden), embedding, conv_in[section_index], conv_out[section_index], embed_proj[section_index], skip_proj[section_index], qkv_proj[section_index], out_proj[section_index], gains[section_index], biases[section_index])
            if section_index < SECTIONS - 1:
                carried = low(out_now)
                if section_index < SECTIONS // 2:
                    saved_skips.append(carried)
                hidden = low_back(carried)
            else:
                results.append(out_now)
    return jnp.stack(results)

def reference(level_input, cotangent, class_table, conv_in, conv_out, embed_proj, skip_proj, qkv_proj, out_proj, gains, biases, noise_pairs, classes):

    def wrapped(input_f, table_f, conv_in_f, conv_out_f, embed_f, skip_f, qkv_f, out_f, gains_f, biases_f):
        return forward(input_f, table_f, conv_in_f, conv_out_f, embed_f, skip_f, qkv_f, out_f, gains_f, biases_f, noise_pairs, classes)
    output, pullback = jax.vjp(wrapped, level_input.astype(jnp.float32), class_table.astype(jnp.float32), conv_in.astype(jnp.float32), conv_out.astype(jnp.float32), embed_proj.astype(jnp.float32), skip_proj.astype(jnp.float32), qkv_proj.astype(jnp.float32), out_proj.astype(jnp.float32), gains.astype(jnp.float32), biases.astype(jnp.float32))
    grads = pullback(cotangent.astype(jnp.float32))
    return (output.astype(jnp.bfloat16), grads[0], grads[1], grads[2], grads[3], grads[4], grads[5], grads[6], grads[7], grads[8], grads[9])
```

```python
from functools import partial
import math

import jax
import jax.numpy as jnp
import numpy as np
from jax import lax
from jax.experimental import pallas as pl
from jax.experimental.pallas import tpu as pltpu
from jax.sharding import PartitionSpec as P

WIDTH = 768
EMBED = 768
CLASSES = 1000
HEAD_DIM = 64
GROUPS = 32
SIDE = 8
LEVELS = 40
MICRO = 4
PIXELS = 64
TAPS = 9

EPS = 1e-05
SIGMA_LOW = 0.002
SIGMA_HIGH = 80.0

F32 = jnp.float32
BF16 = jnp.bfloat16
LANE = 128
CHUNKS = WIDTH // LANE
PER_GROUP = WIDTH // GROUPS
GROUP_SHARE = 1.0 / (PER_GROUP * PIXELS)
VMEM_LIMIT = 56 * 2**20

GAIN = 0
BIAS = 4

GROUP_OF = (np.arange(WIDTH)[:, None] // PER_GROUP == np.arange(LANE)[None, :]).astype(np.float32)


def lanes(chunk):
    return pl.ds(chunk * LANE, LANE)


def dot(left, right):
    return jnp.dot(left, right, preferred_element_type=F32)


def dot_nt(left, right):
    return lax.dot_general(left, right, (((1,), (1,)), ((), ())), preferred_element_type=F32)


def dot_tn(left, right):
    return lax.dot_general(left, right, (((0,), (0,)), ((), ())), preferred_element_type=F32)


def octet_sum(values, octets):
    width = values.shape[-1]
    partial_sums = values.reshape(SIDE, octets, width).sum(axis=0).reshape(octets // 8, 8, width)
    totals = jnp.sum(partial_sums, axis=1, keepdims=True)
    return jnp.broadcast_to(totals, partial_sums.shape).reshape(octets, width)


def over_rows(stat):
    octets, width = stat.shape
    return jnp.broadcast_to(stat[None], (SIDE, octets, width)).reshape(SIDE * octets, width)


def in_parts(values):
    first = values.astype(BF16)
    rest = values - first.astype(F32)
    second = rest.astype(BF16)
    third = (rest - second.astype(F32)).astype(BF16)
    return jnp.concatenate([first, second, third], axis=0)


def group_mean(sums, group_of, group_of_t):
    count = sums.shape[0]
    grouped = dot(in_parts(sums), group_of)
    grouped = (grouped[:count] + grouped[count : 2 * count] + grouped[2 * count :]) * GROUP_SHARE
    spread = dot(in_parts(grouped), group_of_t)
    return spread[:count] + spread[count : 2 * count] + spread[2 * count :]


def norm_stats(read, octets, group_of, group_of_t):
    sums = jnp.concatenate([octet_sum(read(c), octets) for c in range(CHUNKS)], axis=1)
    mean = group_mean(sums, group_of, group_of_t)
    squares = []
    for c in range(CHUNKS):
        centered = read(c) - over_rows(mean[:, c * LANE : (c + 1) * LANE])
        squares.append(octet_sum(centered * centered, octets))
    spread = group_mean(jnp.concatenate(squares, axis=1), group_of, group_of_t)
    return mean, lax.rsqrt(spread + EPS)


def normed_chunk(values, stat_ref, c):
    mean = stat_ref[0, :, lanes(c)]
    inv = stat_ref[1, :, lanes(c)]
    return (values - over_rows(mean)) * over_rows(inv)


def sigmoid(values):
    return 1.0 / (1.0 + jnp.exp(-values))


def silu_slope(values):
    gate = sigmoid(values)
    return gate * (1.0 + values * (1.0 - gate))


def put_shifted(planes, base, values, c, octets):
    rows = values.shape[0]
    column = lax.broadcasted_iota(jnp.int32, values.shape, 0) & 7
    before = jnp.where(column != 0, pltpu.roll(values, 1, 0), 0.0)
    after = jnp.where(column != 7, pltpu.roll(values, rows - 1, 0), 0.0)
    planes[base, pl.ds(octets, rows), lanes(c)] = before.astype(BF16)
    planes[base + 1, pl.ds(octets, rows), lanes(c)] = values.astype(BF16)
    planes[base + 2, pl.ds(octets, rows), lanes(c)] = after.astype(BF16)


def clear_edges(planes, octets):
    count, rows, width = planes.shape
    edge = jnp.zeros((count, octets, width), BF16)
    planes[:, pl.ds(0, octets), :] = edge
    planes[:, pl.ds(rows - octets, octets), :] = edge


def row_total(values):
    return jnp.sum(values, axis=0, keepdims=True)


def norm_back(read_grad, read_normed, gain_of, stat_ref, octets, tables, write, sums_out):
    group_of, group_of_t = tables
    first, second = [], []
    for c in range(CHUNKS):
        grad = read_grad(c)
        first.append(octet_sum(grad, octets))
        second.append(octet_sum(grad * read_normed(c), octets))
    first = jnp.concatenate(first, axis=1)
    second = jnp.concatenate(second, axis=1)
    sums_out(first, second)
    gain = gain_of(None)
    both = group_mean(jnp.concatenate([first * gain, second * gain], axis=0), group_of, group_of_t)
    for c in range(CHUNKS):
        part = slice(c * LANE, (c + 1) * LANE)
        inv = over_rows(stat_ref[1, :, lanes(c)])
        mean_one = over_rows(both[:octets, part])
        mean_two = over_rows(both[octets:, part])
        write(c, inv * (gain_of(c) * read_grad(c) - mean_one - read_normed(c) * mean_two))


def conv_in_forward(decoder, octets, *refs):
    if decoder:
        hidden, skipped, weights, params, group_of, group_of_t = refs[:6]
        conv_one, stat_h, stat_s, turned_h, turned_s, planes, held, sems = refs[6:]
        sides = ((hidden, stat_h, turned_h, 0), (skipped, stat_s, turned_s, 1))
    else:
        hidden, weights, params, group_of, group_of_t = refs[:5]
        conv_one, stat_h, turned_h, planes, held, sems = refs[5:]
        sides = ((hidden, stat_h, turned_h, 0),)
    span = WIDTH * len(sides)
    copies = [
        pltpu.make_async_copy(
            weights.at[pl.ds(tap * 2 * WIDTH, span)], held.at[pl.ds(tap * span, span)], sems.at[tap]
        )
        for tap in range(TAPS)
    ]
    for copy in copies:
        copy.start()
    rows = hidden.shape[0]
    tables = (group_of[...], group_of_t[...])
    clear_edges(planes, octets)
    for source, stat, turned, which in sides:
        mean, inv = norm_stats(lambda c: source[:, lanes(c)].astype(F32), octets, *tables)
        stat[0] = mean
        stat[1] = inv
        for c in range(CHUNKS):
            normed = normed_chunk(source[:, lanes(c)].astype(F32), stat, c)
            value = (
                normed * params[pl.ds(GAIN + which, 1), lanes(c)]
                + params[pl.ds(BIAS + which, 1), lanes(c)]
            )
            value = value * sigmoid(value)
            put_shifted(planes, 3 * which, value, c, octets)
            turned[lanes(c), :] = value.T.astype(BF16)
    for tap in range(TAPS):
        copies[tap].wait()
        for half in range(len(sides)):
            part = dot(
                planes[3 * half + tap % 3, pl.ds(octets * (tap // 3), rows), :],
                held[pl.ds(tap * span + half * WIDTH, WIDTH), :],
            )
            if tap == 0 and half == 0:
                conv_one[...] = part + params[pl.ds(BIAS + 2, 1), :]
            else:
                conv_one[...] += part


class Rest:
    def __init__(self, source, sems, pieces):
        self.source, self.sems, self.pieces = source, sems, pieces
        self.offset, self.waits = 0, {}

    def fetch(self, name, total, held, at_once=True):
        share = total // self.pieces
        copies = []
        for piece in range(self.pieces):
            copies.append(
                pltpu.make_async_copy(
                    self.source.at[piece, pl.ds(self.offset, share)],
                    held.at[pl.ds(piece * share, share)],
                    self.sems.at[len(self.waits), piece],
                )
            )
        self.waits[name] = (share, copies, [False] * self.pieces)
        self.offset += share
        if at_once:
            for copy in copies:
                copy.start()

    def need(self, name, stop):
        share, copies, done = self.waits[name]
        for piece, copy in enumerate(copies):
            if piece * share < stop and not done[piece]:
                copy.wait()
                done[piece] = True


def rest_rows():
    return {
        "conv_out": TAPS * WIDTH,
        "query": WIDTH,
        "key": WIDTH,
        "value": WIDTH,
        "out": WIDTH,
        "skip": 2 * WIDTH,
    }


def head_mask(rows):
    return lax.broadcasted_iota(jnp.int32, (rows, LANE), 1) < HEAD_DIM


def image_bias(rows, images):
    row_image = lax.rem(lax.shift_right_logical(lax.broadcasted_iota(jnp.int32, (rows, rows), 0), 3), images)
    column_image = lax.rem(lax.shift_right_logical(lax.broadcasted_iota(jnp.int32, (rows, rows), 1), 3), images)
    return jnp.where(row_image == column_image, 0.0, -1e30).astype(F32)


def attention_of(queries, keys, apart):
    scores = dot_nt(queries, keys) * (1.0 / math.sqrt(HEAD_DIM)) + apart
    weight = jnp.exp(scores - jnp.max(scores, axis=1, keepdims=True))
    return weight * (1.0 / jnp.sum(weight, axis=1, keepdims=True))


def block_forward(decoder, octets, pieces, *refs):
    if decoder:
        conv_one, hidden, skipped, modulation, rest, params, group_of, group_of_t = refs[:8]
        refs = refs[8:]
    else:
        conv_one, hidden, modulation, rest, params, group_of, group_of_t = refs[:7]
        refs = refs[7:]
    result, residual, stat_c, stat_r, attend, project, mixed, turned, planes, apart = refs[:10]
    held_conv, held_qkv, held_out, held_skip, sems = refs[10:]
    weights = Rest(rest, sems, pieces)
    weights.fetch("conv_out", TAPS * WIDTH, held_conv)
    for index, name in enumerate(("query", "key", "value")):
        weights.fetch(name, WIDTH, held_qkv.at[index])
    weights.fetch("out", WIDTH, held_out)
    if decoder:
        weights.fetch("skip", 2 * WIDTH, held_skip)
    rows = conv_one.shape[0]
    tables = (group_of[...], group_of_t[...])
    clear_edges(planes, octets)
    apart[...] = image_bias(rows, octets // 8)
    mean, inv = norm_stats(lambda c: conv_one[:, lanes(c)], octets, *tables)
    stat_c[0] = mean
    stat_c[1] = inv
    for c in range(CHUNKS):
        normed = (
            normed_chunk(conv_one[:, lanes(c)], stat_c, c) * params[pl.ds(GAIN + 2, 1), lanes(c)]
            + params[pl.ds(BIAS + 5, 1), lanes(c)]
        )
        scale = over_rows(modulation[:, lanes(c)])
        shift = over_rows(modulation[:, lanes(CHUNKS + c)])
        value = normed * (1.0 + scale) + shift
        value = value * sigmoid(value)
        put_shifted(planes, 0, value, c, octets)
        turned[lanes(c), :] = value.T.astype(BF16)
    for tap in range(TAPS):
        weights.need("conv_out", (tap + 1) * WIDTH)
        part = dot(
            planes[tap % 3, pl.ds(octets * (tap // 3), rows), :], held_conv[pl.ds(tap * WIDTH, WIDTH), :]
        )
        if tap == 0:
            residual[...] = part + params[pl.ds(BIAS + 6, 1), :]
        else:
            residual[...] += part
    if decoder:
        weights.need("skip", 2 * WIDTH)
        residual[...] += (
            dot(hidden[...], held_skip[pl.ds(0, WIDTH), :])
            + dot(skipped[...], held_skip[pl.ds(WIDTH, WIDTH), :])
            + params[pl.ds(BIAS + 7, 1), :]
        )
    else:
        residual[...] += hidden[...].astype(F32)
    mean, inv = norm_stats(lambda c: residual[:, lanes(c)], octets, *tables)
    stat_r[0] = mean
    stat_r[1] = inv
    for c in range(CHUNKS):
        attend[:, lanes(c)] = (
            normed_chunk(residual[:, lanes(c)], stat_r, c) * params[pl.ds(GAIN + 3, 1), lanes(c)]
            + params[pl.ds(BIAS + 8, 1), lanes(c)]
        ).astype(BF16)
    for index, (name, bias) in enumerate((("query", 9), ("key", None), ("value", 10))):
        weights.need(name, WIDTH)
        part = dot(attend[...], held_qkv[index])
        if bias is not None:
            part = part + params[pl.ds(BIAS + bias, 1), :]
        project[:, pl.ds(index * WIDTH, WIDTH)] = part.astype(BF16)
    left = head_mask(rows)
    for pair in range(CHUNKS):
        queries = project[:, lanes(pair)]
        keys_h = project[:, lanes(CHUNKS + pair)]
        values_h = project[:, lanes(2 * CHUNKS + pair)]
        parts = []
        for half in (left, jnp.logical_not(left)):
            chosen = jnp.where(half, queries, jnp.zeros_like(queries))
            attention = attention_of(chosen, keys_h, apart[...])
            parts.append(dot(attention.astype(BF16), values_h))
        mixed[:, lanes(pair)] = jnp.where(left, parts[0], parts[1]).astype(BF16)
    weights.need("out", WIDTH)
    result[...] = (
        residual[...] + dot(mixed[...], held_out[...]) + params[pl.ds(BIAS + 11, 1), :]
    ).astype(BF16)


def block_backward(decoder, octets, pieces, *refs):
    grad_out, project, residual, stat_r, conv_one, stat_c, modulation, rest, params, group_of, group_of_t = refs[:11]
    grad_top, grad_project, grad_resid, grad_resid_b, grad_conv_b, grad_mod, sums = refs[11:18]
    scratch, grad_mixed, planes, apart, held_conv, held_qkv, held_out, sems = refs[18:]
    weights = Rest(rest, sems, pieces)
    weights.fetch("conv_out", TAPS * WIDTH, held_conv, False)
    for index, name in enumerate(("query", "key", "value")):
        weights.fetch(name, WIDTH, held_qkv.at[index], False)
    weights.fetch("out", WIDTH, held_out, False)
    for name in ("out", "query", "key", "value", "conv_out"):
        for copy in weights.waits[name][1]:
            copy.start()
    rows = conv_one.shape[0]
    tables = (group_of[...], group_of_t[...])
    sums[...] = jnp.zeros(sums.shape, F32)
    clear_edges(planes, octets)
    apart[...] = image_bias(rows, octets // 8)

    def put_sum(row, c, values):
        sums[pl.ds(row, 1), lanes(c)] = row_total(values)

    top = grad_out[...].astype(BF16)
    grad_top[...] = top
    for c in range(CHUNKS):
        put_sum(BIAS + 11, c, grad_top[:, lanes(c)].astype(F32))
    weights.need("out", WIDTH)
    grad_mixed[...] = dot_nt(top, held_out[...]).astype(BF16)
    left = head_mask(rows)
    root = 1.0 / math.sqrt(HEAD_DIM)
    for pair in range(CHUNKS):
        queries = project[:, lanes(pair)]
        keys_h = project[:, lanes(CHUNKS + pair)]
        values_h = project[:, lanes(2 * CHUNKS + pair)]
        grads_h = grad_mixed[:, lanes(pair)]
        parts = []
        for half in (left, jnp.logical_not(left)):
            chosen = jnp.where(half, queries, jnp.zeros_like(queries))
            chosen_grad = jnp.where(half, grads_h, jnp.zeros_like(grads_h))
            attention = attention_of(chosen, keys_h, apart[...])
            grad_attention = dot_nt(chosen_grad, values_h)
            weighted = grad_attention * attention
            grad_scores = (weighted - attention * jnp.sum(weighted, axis=1, keepdims=True)).astype(BF16)
            parts.append(
                (
                    dot(grad_scores, keys_h) * root,
                    dot_tn(grad_scores, queries) * root,
                    dot_tn(attention.astype(BF16), grads_h),
                )
            )
        for index in range(3):
            joined = jnp.where(left, parts[0][index], parts[1][index]).astype(BF16)
            grad_project[:, lanes(index * CHUNKS + pair)] = joined
            if index == 0:
                put_sum(BIAS + 9, pair, joined.astype(F32))
            if index == 2:
                put_sum(BIAS + 10, pair, joined.astype(F32))
    for index, name in enumerate(("query", "key", "value")):
        weights.need(name, WIDTH)
        part = dot_nt(grad_project[:, pl.ds(index * WIDTH, WIDTH)], held_qkv[index])
        if index == 0:
            scratch[...] = part
        else:
            scratch[...] += part

    def gain_attend(c):
        return params[pl.ds(GAIN + 3, 1), :] if c is None else params[pl.ds(GAIN + 3, 1), lanes(c)]

    def sums_attend(first, second):
        sums[pl.ds(BIAS + 8, 1), :] = row_total(first) * 0.125
        sums[pl.ds(GAIN + 3, 1), :] = row_total(second) * 0.125

    def write_resid(c, grad):
        total = grad_out[:, lanes(c)].astype(F32) + grad
        grad_resid[:, lanes(c)] = total
        rounded = total.astype(BF16)
        grad_resid_b[:, lanes(c)] = rounded
        rounded = rounded.astype(F32)
        put_shifted(planes, 0, rounded, c, octets)
        put_sum(BIAS + 6, c, rounded)
        if decoder:
            put_sum(BIAS + 7, c, rounded)

    norm_back(
        lambda c: scratch[:, lanes(c)],
        lambda c: normed_chunk(residual[:, lanes(c)], stat_r, c),
        gain_attend,
        stat_r,
        octets,
        tables,
        write_resid,
        sums_attend,
    )
    for tap in range(TAPS):
        weights.need("conv_out", (tap + 1) * WIDTH)
        part = dot_nt(
            planes[2 - tap % 3, pl.ds(octets * (2 - tap // 3), rows), :],
            held_conv[pl.ds(tap * WIDTH, WIDTH), :],
        )
        if tap == 0:
            scratch[...] = part
        else:
            scratch[...] += part
    for c in range(CHUNKS):
        normed = (
            normed_chunk(conv_one[:, lanes(c)], stat_c, c) * params[pl.ds(GAIN + 2, 1), lanes(c)]
            + params[pl.ds(BIAS + 5, 1), lanes(c)]
        )
        scale = over_rows(modulation[:, lanes(c)])
        shift = over_rows(modulation[:, lanes(CHUNKS + c)])
        scratch[:, lanes(c)] = scratch[:, lanes(c)] * silu_slope(normed * (1.0 + scale) + shift)

    def gain_middle(c):
        if c is None:
            return params[pl.ds(GAIN + 2, 1), :] * (1.0 + modulation[:, pl.ds(0, WIDTH)])
        return over_rows(params[pl.ds(GAIN + 2, 1), lanes(c)] * (1.0 + modulation[:, lanes(c)]))

    def sums_middle(first, second):
        scaled = 1.0 + modulation[:, pl.ds(0, WIDTH)]
        sums[pl.ds(BIAS + 5, 1), :] = row_total(first * scaled) * 0.125
        sums[pl.ds(GAIN + 2, 1), :] = row_total(second * scaled) * 0.125
        grad_scale = (
            params[pl.ds(GAIN + 2, 1), :] * second + params[pl.ds(BIAS + 5, 1), :] * first
        ).astype(BF16)
        grad_shift = first.astype(BF16)
        grad_mod[:, pl.ds(0, WIDTH)] = grad_scale
        grad_mod[:, pl.ds(WIDTH, WIDTH)] = grad_shift
        sums[pl.ds(BIAS + 3, 1), :] = row_total(grad_scale.astype(F32)) * 0.125
        sums[pl.ds(BIAS + 4, 1), :] = row_total(grad_shift.astype(F32)) * 0.125

    def write_conv(c, grad):
        rounded = grad.astype(BF16)
        grad_conv_b[:, lanes(c)] = rounded
        put_sum(BIAS + 2, c, rounded.astype(F32))

    norm_back(
        lambda c: scratch[:, lanes(c)],
        lambda c: normed_chunk(conv_one[:, lanes(c)], stat_c, c),
        gain_middle,
        stat_c,
        octets,
        tables,
        write_conv,
        sums_middle,
    )


def conv_in_backward(decoder, octets, pieces, *refs):
    if decoder:
        grad_conv, hidden, skipped, stat_h, stat_s, grad_resid, grad_resid_b, weights, rest = refs[:9]
        params, group_of, group_of_t, grad_hidden, grad_skipped, sums = refs[9:15]
        scratch, planes, held, held_skip, sems, rest_sems = refs[15:]
        sides = ((hidden, stat_h, grad_hidden, 0), (skipped, stat_s, grad_skipped, 1))
    else:
        grad_conv, hidden, stat_h, grad_resid, weights, params, group_of, group_of_t = refs[:8]
        grad_hidden, sums, scratch, planes, held, sems = refs[8:]
        sides = ((hidden, stat_h, grad_hidden, 0),)
    span = WIDTH * len(sides)
    copies = [
        pltpu.make_async_copy(
            weights.at[pl.ds(tap * 2 * WIDTH, span)], held.at[pl.ds(tap * span, span)], sems.at[tap]
        )
        for tap in range(TAPS)
    ]
    for copy in copies:
        copy.start()
    if decoder:
        skip_weights = Rest(rest, rest_sems, pieces)
        skip_weights.offset = sum(
            count // pieces for name, count in rest_rows().items() if name != "skip"
        )
        skip_weights.fetch("skip", 2 * WIDTH, held_skip)
    rows = hidden.shape[0]
    tables = (group_of[...], group_of_t[...])
    sums[...] = jnp.zeros(sums.shape, F32)
    clear_edges(planes, octets)
    for c in range(CHUNKS):
        put_shifted(planes, 0, grad_conv[:, lanes(c)].astype(F32), c, octets)
    for tap in range(TAPS):
        copies[tap].wait()
        for _, _, _, half in sides:
            part = dot_nt(
                planes[2 - tap % 3, pl.ds(octets * (2 - tap // 3), rows), :],
                held[pl.ds(tap * span + half * WIDTH, WIDTH), :],
            )
            if tap == 0:
                scratch[half] = part
            else:
                scratch[half] += part
    if decoder:
        skip_weights.need("skip", 2 * WIDTH)
    for source, stat, target, which in sides:

        def normed_of(c, source=source, stat=stat):
            return normed_chunk(source[:, lanes(c)].astype(F32), stat, c)

        def gain_input(c, which=which):
            row = pl.ds(GAIN + which, 1)
            return params[row, :] if c is None else params[row, lanes(c)]

        for c in range(CHUNKS):
            value = normed_of(c) * gain_input(c) + params[pl.ds(BIAS + which, 1), lanes(c)]
            scratch[which, :, lanes(c)] = scratch[which, :, lanes(c)] * silu_slope(value)

        def sums_input(first, second, which=which):
            sums[pl.ds(BIAS + which, 1), :] = row_total(first) * 0.125
            sums[pl.ds(GAIN + which, 1), :] = row_total(second) * 0.125

        if decoder:
            target[...] = dot_nt(grad_resid_b[...], held_skip[pl.ds(which * WIDTH, WIDTH), :])

        def write_input(c, grad, target=target):
            if decoder:
                target[:, lanes(c)] += grad
            else:
                target[:, lanes(c)] = grad + grad_resid[:, lanes(c)]

        norm_back(
            lambda c, which=which: scratch[which, :, lanes(c)],
            normed_of,
            gain_input,
            stat,
            octets,
            tables,
            write_input,
            sums_input,
        )


def shape(dims, kind):
    return jax.ShapeDtypeStruct(dims, kind)


IN_VMEM = pl.BlockSpec(memory_space=pltpu.VMEM)
IN_HBM = pl.BlockSpec(memory_space=pl.ANY)


def call(body, operands, far, outputs, scratch, flops, name):
    moved = sum(int(np.prod(v.shape)) * v.dtype.itemsize for v in (*operands, *outputs))
    return pl.pallas_call(
        body,
        out_shape=outputs,
        in_specs=[IN_HBM if index in far else IN_VMEM for index in range(len(operands))],
        out_specs=[IN_VMEM] * len(outputs),
        scratch_shapes=scratch,
        compiler_params=pltpu.CompilerParams(vmem_limit_bytes=VMEM_LIMIT),
        cost_estimate=pl.CostEstimate(flops=flops, bytes_accessed=moved, transcendentals=0),
        name=name,
    )(*operands)


def run_conv_in(decoder, hidden, skipped, weights, params, tables):
    rows = hidden.shape[0]
    octets = rows // SIDE
    sides = 2 if decoder else 1
    inputs = [hidden, skipped] if decoder else [hidden]
    outputs = [shape((rows, WIDTH), F32)]
    outputs += [shape((2, octets, WIDTH), F32)] * sides
    outputs += [shape((WIDTH, rows), BF16)] * sides
    return call(
        partial(conv_in_forward, decoder, octets),
        [*inputs, weights, params, *tables],
        {len(inputs)},
        outputs,
        [
            pltpu.VMEM((3 * sides, rows + 2 * octets, WIDTH), BF16),
            pltpu.VMEM((sides * TAPS * WIDTH, WIDTH), BF16),
            pltpu.SemaphoreType.DMA((TAPS,)),
        ],
        2 * rows * sides * TAPS * WIDTH * WIDTH,
        "conv_in_forward",
    )


def run_block(decoder, conv_one, hidden, skipped, modulation, rest, params, tables):
    rows = hidden.shape[0]
    octets = rows // SIDE
    pieces = rest.shape[0]
    inputs = [conv_one, hidden, skipped] if decoder else [conv_one, hidden]
    outputs = [
        shape((rows, WIDTH), BF16),
        shape((rows, WIDTH), F32),
        shape((2, octets, WIDTH), F32),
        shape((2, octets, WIDTH), F32),
        shape((rows, WIDTH), BF16),
        shape((rows, 3 * WIDTH), BF16),
        shape((rows, WIDTH), BF16),
        shape((WIDTH, rows), BF16),
    ]
    return call(
        partial(block_forward, decoder, octets, pieces),
        [*inputs, modulation, rest, params, *tables],
        {len(inputs) + 1},
        outputs,
        [
            pltpu.VMEM((3, rows + 2 * octets, WIDTH), BF16),
            pltpu.VMEM((rows, rows), F32),
            pltpu.VMEM((TAPS * WIDTH, WIDTH), BF16),
            pltpu.VMEM((3, WIDTH, WIDTH), BF16),
            pltpu.VMEM((WIDTH, WIDTH), BF16),
            pltpu.VMEM((2 * WIDTH, WIDTH), BF16),
            pltpu.SemaphoreType.DMA((6, pieces)),
        ],
        2 * rows * (TAPS + 6) * WIDTH * WIDTH,
        "block_forward",
    )


def run_block_back(decoder, grad_out, project, residual, stat_r, conv_one, stat_c, modulation, rest, params, tables):
    rows = residual.shape[0]
    octets = rows // SIDE
    pieces = rest.shape[0]
    outputs = [
        shape((rows, WIDTH), BF16),
        shape((rows, 3 * WIDTH), BF16),
        shape((rows, WIDTH), F32),
        shape((rows, WIDTH), BF16),
        shape((rows, WIDTH), BF16),
        shape((octets, 2 * WIDTH), BF16),
        shape((16, WIDTH), F32),
    ]
    return call(
        partial(block_backward, decoder, octets, pieces),
        [grad_out, project, residual, stat_r, conv_one, stat_c, modulation, rest, params, *tables],
        {7},
        outputs,
        [
            pltpu.VMEM((rows, WIDTH), F32),
            pltpu.VMEM((rows, WIDTH), BF16),
            pltpu.VMEM((3, rows + 2 * octets, WIDTH), BF16),
            pltpu.VMEM((rows, rows), F32),
            pltpu.VMEM((TAPS * WIDTH, WIDTH), BF16),
            pltpu.VMEM((3, WIDTH, WIDTH), BF16),
            pltpu.VMEM((WIDTH, WIDTH), BF16),
            pltpu.SemaphoreType.DMA((6, pieces)),
        ],
        2 * rows * (TAPS + 6) * WIDTH * WIDTH,
        "block_backward",
    )


def run_conv_in_back(decoder, grad_conv, hidden, skipped, stat_h, stat_s, grad_resid, grad_resid_b, weights, rest, params, tables):
    rows = hidden.shape[0]
    octets = rows // SIDE
    sides = 2 if decoder else 1
    pieces = rest.shape[0]
    if decoder:
        inputs = [grad_conv, hidden, skipped, stat_h, stat_s, grad_resid, grad_resid_b, weights, rest]
        far = {7, 8}
    else:
        inputs = [grad_conv, hidden, stat_h, grad_resid, weights]
        far = {4}
    scratch = [
        pltpu.VMEM((sides, rows, WIDTH), F32),
        pltpu.VMEM((3, rows + 2 * octets, WIDTH), BF16),
        pltpu.VMEM((sides * TAPS * WIDTH, WIDTH), BF16),
    ]
    if decoder:
        scratch.append(pltpu.VMEM((2 * WIDTH, WIDTH), BF16))
    scratch.append(pltpu.SemaphoreType.DMA((TAPS,)))
    if decoder:
        scratch.append(pltpu.SemaphoreType.DMA((1, pieces)))
    return call(
        partial(conv_in_backward, decoder, octets, pieces),
        [*inputs, params, *tables],
        far,
        [shape((rows, WIDTH), F32)] * sides + [shape((16, WIDTH), F32)],
        scratch,
        2 * rows * sides * TAPS * WIDTH * WIDTH,
        "conv_in_backward",
    )


def tap_slices_kernel(rows_in, rows_out, octets, place, fields, cols_in, cols_out):
    lane = lax.broadcasted_iota(jnp.int32, (1, SIDE * octets), 1)
    grid_row = lax.div(lane, octets)
    grid_column = lane & 7
    for rows, base, channels, target in (
        (rows_in, 0, 2 * WIDTH, cols_in),
        (rows_out, 2 * WIDTH, WIDTH, cols_out),
    ):
        block = rows // TAPS
        per_tap = channels // block
        for index in range(TAPS):
            position = place[0] * TAPS + index
            tap = lax.div(position, per_tap)
            start = pl.multiple_of(base + lax.rem(position, per_tap) * block, 16)
            down = lax.div(tap, 3) - 1
            across = lax.rem(tap, 3) - 1
            values = fields[0, pl.ds(start, block), :].astype(F32)
            width = SIDE * octets
            moved = pltpu.roll(values, lax.rem(width - (octets * down + across), width), 1)
            inside = (
                (grid_row + down >= 0)
                & (grid_row + down < SIDE)
                & (grid_column + across >= 0)
                & (grid_column + across < 8)
            )
            target[pl.ds(index * block, block), :] = jnp.where(inside, moved, 0.0).astype(BF16)


def tap_slices_plain(fields, rows, base, channels, place, octets):
    pieces, _, width = fields.shape
    spots = place * rows + jnp.arange(rows)
    taps = spots // channels
    values = jnp.take(fields, base + spots % channels, axis=1)
    lane = jnp.arange(width)
    total = jnp.zeros_like(values)
    for tap in range(TAPS):
        down, across = tap // 3 - 1, tap % 3 - 1
        row, column = lane // octets + down, lane % 8 + across
        inside = (row >= 0) & (row < SIDE) & (column >= 0) & (column < 8)
        moved = jnp.roll(values, -(octets * down + across), axis=2)
        total = jnp.where((taps == tap)[None, :, None] & inside, moved, total)
    return total.transpose(1, 0, 2).reshape(rows, pieces * width)


def tap_slices(fields, rows_in, rows_out, place, octets):
    pieces, height, width = fields.shape
    if rows_in % (TAPS * 16) or rows_out % (TAPS * 16):
        return (
            tap_slices_plain(fields, rows_in, 0, 2 * WIDTH, place, octets),
            tap_slices_plain(fields, rows_out, 2 * WIDTH, WIDTH, place, octets),
        )
    return pl.pallas_call(
        partial(tap_slices_kernel, rows_in, rows_out, octets),
        grid_spec=pltpu.PrefetchScalarGridSpec(
            num_scalar_prefetch=1,
            grid=(pieces,),
            in_specs=[pl.BlockSpec((1, height, width), lambda piece, place: (piece, 0, 0))],
            out_specs=[
                pl.BlockSpec((rows_in, width), lambda piece, place: (0, piece)),
                pl.BlockSpec((rows_out, width), lambda piece, place: (0, piece)),
            ],
        ),
        out_shape=[
            shape((rows_in, pieces * width), BF16),
            shape((rows_out, pieces * width), BF16),
        ],
        compiler_params=pltpu.CompilerParams(vmem_limit_bytes=VMEM_LIMIT),
        cost_estimate=pl.CostEstimate(
            flops=0, bytes_accessed=4 * pieces * height * width, transcendentals=0
        ),
        name="tap_slices",
    )(place.reshape(1).astype(jnp.int32), fields)


def gather_doubling(value, axis):
    count, index = lax.axis_size(axis), lax.axis_index(axis)
    value = value[None]
    step = 1
    while step < count:
        other = lax.ppermute(value, axis, [(i, i ^ step) for i in range(count)])
        value = jnp.where(
            (index // step) % 2 == 0,
            jnp.concatenate([value, other], axis=0),
            jnp.concatenate([other, value], axis=0),
        )
        step *= 2
    return value


def scatter_halving(value, axis):
    count, index = lax.axis_size(axis), lax.axis_index(axis)
    step = count // 2
    while step:
        upper = (index // step) % 2 == 1
        keep = jnp.where(upper, value[step:], value[:step])
        send = jnp.where(upper, value[:step], value[step:])
        value = keep + lax.ppermute(send, axis, [(i, i ^ step) for i in range(count)])
        step //= 2
    return value[0]


def moved(value, source, target):
    return lax.ppermute(value, "section", [(source, target)])


def to_rows(value):
    micro, images, pixels, channels = value.shape
    count = micro * images
    return (
        value.reshape(count, pixels // 8, 8, channels).transpose(1, 0, 2, 3).reshape(-1, channels)
    )


def from_rows(value, images):
    count = MICRO * images
    channels = value.shape[-1]
    grid_rows = value.shape[0] // (8 * count)
    planes = value.reshape(grid_rows, count, 8, channels).transpose(1, 0, 2, 3)
    return planes.reshape(MICRO, images, grid_rows * 8, channels)


def noise_columns(pair_ids, columns):
    fraction = pair_ids.astype(F32) / (LEVELS - 1)
    top_root = SIGMA_HIGH ** (1.0 / 7.0)
    bottom_root = SIGMA_LOW ** (1.0 / 7.0)
    sigmas = (top_root + fraction * (bottom_root - top_root)) ** 7
    log_scale = 250.0 * jnp.log(sigmas)
    quarter = EMBED // 4
    kind = columns // quarter
    frequency = jnp.exp(-math.log(10000.0) * (columns % quarter).astype(F32) / quarter)
    angles = jnp.where(kind < 2, log_scale[:, :1], log_scale[:, 1:]) * frequency
    return jnp.where(kind % 2 == 0, jnp.cos(angles), jnp.sin(angles))


def on_device(
    level_input,
    cotangent,
    class_table,
    conv_in,
    conv_out,
    embed_proj,
    skip_proj,
    qkv_proj,
    out_proj,
    gains,
    biases,
    noise_pairs,
    classes,
):
    sections = lax.axis_size("section")
    section_id = lax.axis_index("section")
    shards = lax.axis_size("dp")
    shard_id = lax.axis_index("dp")
    images = level_input.shape[1]
    count = MICRO * images
    octets = 8 * count
    rows = SIDE * octets
    tables = (jnp.asarray(GROUP_OF, BF16), jnp.asarray(GROUP_OF.T, BF16))

    conv_in_full = lax.all_gather(conv_in[0], "dp", axis=0, tiled=True)
    qkv_parts = [qkv_proj[0][:, part * WIDTH : (part + 1) * WIDTH] for part in range(3)]
    rest_full = lax.all_gather(
        jnp.concatenate([conv_out[0], *qkv_parts, out_proj[0], skip_proj[0]], axis=0), "dp", axis=0
    )
    if any((total // shards) % 16 for total in rest_rows().values()):
        offset, whole = 0, []
        for total in rest_rows().values():
            share = total // shards
            whole.append(rest_full[:, offset : offset + share].reshape(total, WIDTH))
            offset += share
        rest_full = jnp.concatenate(whole, axis=0)[None]

    gain_share, bias_share = gains.shape[1], biases.shape[1]
    small = jnp.concatenate(
        [
            gains[0].astype(F32),
            biases[0].astype(F32),
            noise_pairs.reshape(-1).astype(F32),
            classes.reshape(-1).astype(F32),
        ]
    )
    spare = -small.shape[0] % LANE
    every = gather_doubling(jnp.pad(small, (0, spare))[None], "dp")[:, 0]
    cut = gain_share + bias_share
    params = jnp.concatenate(
        [every[:, :gain_share].reshape(4, WIDTH), every[:, gain_share:cut].reshape(12, WIDTH)],
        axis=0,
    )
    all_images = shards * count
    pair_ids = every[:, cut : cut + 2 * count].reshape(all_images, 2)
    class_ids = every[:, cut + 2 * count : cut + 3 * count].reshape(all_images).astype(jnp.int32)

    slice_width = class_table.shape[1]
    columns = shard_id * slice_width + jnp.arange(slice_width)[None, :]
    onehot = (class_ids[:, None] == jnp.arange(CLASSES)[None, :]).astype(BF16)
    pre = noise_columns(pair_ids, columns) + dot(onehot, class_table)
    embed_b = jax.nn.silu(pre).astype(BF16)
    shares = dot(embed_b, embed_proj[0]).reshape(shards, count, 2 * WIDTH)
    modulation = lax.all_to_all(shares, "dp", 0, 0).sum(axis=0)
    modulation = modulation + params[BIAS + 3 : BIAS + 5].reshape(1, 2 * WIDTH)
    modulation = jnp.repeat(modulation, 8, axis=0)

    level_own, top_own = to_rows(level_input), to_rows(cotangent)
    level_rows = jnp.concatenate(
        [level_own] + [moved(level_own, source, 0) for source in range(1, sections)], axis=0
    )
    top_rows = jnp.concatenate(
        [moved(top_own, source, sections - 1) for source in range(sections - 1)] + [top_own], axis=0
    )

    kept = []
    skips = {}
    hidden = level_rows
    result = None
    for tick in range(sections):
        decoder = tick >= sections // 2
        mirror = sections - 1 - tick
        skipped = skips[tick] if decoder else None
        outs = run_conv_in(decoder, hidden, skipped, conv_in_full, params, tables)
        if decoder:
            conv_one, stat_h, stat_s, turned_h, turned_s = outs
        else:
            conv_one, stat_h, turned_h = outs
            stat_s, turned_s = None, jnp.zeros_like(turned_h)
        result, residual, stat_c, stat_r, attend, project, mixed, turned_w = run_block(
            decoder, conv_one, hidden, skipped, modulation, rest_full, params, tables
        )
        kept.append(
            {
                "hidden": hidden,
                "skipped": skipped,
                "conv_one": conv_one,
                "stat_h": stat_h,
                "stat_s": stat_s,
                "stat_c": stat_c,
                "stat_r": stat_r,
                "residual": residual,
                "attend": attend,
                "project": project,
                "mixed": mixed,
                "fields": jnp.concatenate([turned_h, turned_s, turned_w], axis=0),
            }
        )
        if tick < sections - 1:
            hidden = moved(result, tick, tick + 1)
            if not decoder:
                skips[mirror] = hidden if mirror == tick + 1 else moved(result, tick, mirror)

    def own(values):
        chosen = values[0]
        for tick in range(1, sections):
            chosen = jnp.where(section_id == tick, values[tick], chosen)
        return chosen

    fields = lax.all_gather(own([entry["fields"] for entry in kept]), "dp", axis=0)
    cols_in, cols_out = tap_slices(fields, conv_in.shape[1], conv_out.shape[1], shard_id, octets)

    def to_owners(value, source):
        share = rows // sections
        pieces = [value[index * share : (index + 1) * share] for index in range(sections)]
        total = jnp.where(section_id == source, pieces[source], jnp.zeros_like(pieces[source]))
        for target in range(sections):
            if target != source:
                total = total + moved(pieces[target].astype(BF16), source, target).astype(value.dtype)
        return from_rows(total, images)

    level_output = to_owners(result, sections - 1)

    grads = [None] * sections
    skip_grads = {}
    grad_out = top_rows
    grad_hidden = None
    for tick in reversed(range(sections)):
        decoder = tick >= sections // 2
        mirror = sections - 1 - tick
        entry = kept[tick]
        if not decoder and tick in skip_grads:
            grad_out = grad_out.astype(F32) + skip_grads[tick].astype(F32)
        top, grad_project, grad_resid, grad_resid_b, grad_conv_b, grad_mod, sums_block = run_block_back(
            decoder,
            grad_out,
            entry["project"],
            entry["residual"],
            entry["stat_r"],
            entry["conv_one"],
            entry["stat_c"],
            modulation,
            rest_full,
            params,
            tables,
        )
        outs = run_conv_in_back(
            decoder,
            grad_conv_b,
            entry["hidden"],
            entry["skipped"],
            entry["stat_h"],
            entry["stat_s"],
            grad_resid,
            grad_resid_b,
            conv_in_full,
            rest_full,
            params,
            tables,
        )
        grad_hidden = outs[0]
        if decoder:
            if mirror == tick - 1:
                grad_out = moved((grad_hidden + outs[1]).astype(BF16), tick, mirror)
            else:
                skip_grads[mirror] = moved(outs[1].astype(BF16), tick, mirror)
        if tick > 0 and not (decoder and mirror == tick - 1):
            grad_out = moved(grad_hidden.astype(BF16), tick, tick - 1)
        grads[tick] = {
            "top": top,
            "project": grad_project,
            "resid": grad_resid_b,
            "conv": grad_conv_b,
            "mod": grad_mod.reshape(count, 8, 2 * WIDTH)[:, 0],
            "sums": sums_block + outs[-1],
        }
    input_grad = to_owners(grad_hidden, 0)

    def picked(name):
        return own([entry[name] for entry in grads])

    def kept_own(name):
        return own([entry[name] for entry in kept])

    is_decoder = section_id >= sections // 2
    resid_all = lax.all_gather(picked("resid"), "dp", axis=0, tiled=True)
    conv_all = lax.all_gather(picked("conv"), "dp", axis=0, tiled=True)
    conv_out_grad = dot(cols_out, resid_all)
    conv_in_grad = dot(cols_in, conv_all)

    resid_own = picked("resid")
    decoder_entries = [
        jnp.concatenate([entry["hidden"], entry["skipped"] if entry["skipped"] is not None else entry["hidden"]], axis=1)
        for entry in kept
    ]
    skip_part = dot_tn(own(decoder_entries), resid_own)
    skip_part = jnp.where(is_decoder, skip_part, 0.0).astype(BF16)
    qkv_part = dot_tn(kept_own("attend"), picked("project")).astype(BF16)
    out_part = dot_tn(kept_own("mixed"), picked("top")).astype(BF16)
    share = WIDTH // shards
    skip_split = skip_part.reshape(shards, 2, share, WIDTH)
    small_grads = lax.psum_scatter(
        jnp.concatenate(
            [
                qkv_part,
                out_part,
                skip_split[:, 0].reshape(WIDTH, WIDTH),
                skip_split[:, 1].reshape(WIDTH, WIDTH),
            ],
            axis=1,
        ),
        "dp",
        scatter_dimension=0,
        tiled=True,
    ).astype(F32)
    qkv_grad = small_grads[:, : 3 * WIDTH]
    out_grad = small_grads[:, 3 * WIDTH : 4 * WIDTH]
    skip_grad = jnp.concatenate(
        [small_grads[:, 4 * WIDTH : 5 * WIDTH], small_grads[:, 5 * WIDTH :]], axis=0
    )

    sums = picked("sums")
    summed = scatter_halving(
        jnp.concatenate(
            [sums[:4].reshape(shards, gain_share), sums[4:].reshape(shards, bias_share)], axis=1
        ),
        "dp",
    )
    gains_grad, biases_grad = summed[:gain_share], summed[gain_share:]

    mod_all = gather_doubling(picked("mod"), "dp").reshape(all_images, 2 * WIDTH)
    embed_grad = dot_tn(embed_b, mod_all)
    grad_embed = lax.psum(dot_nt(mod_all, embed_proj[0]), "section")
    grad_pre = jax.vjp(jax.nn.silu, pre)[1](grad_embed)[0]
    table_grad = lax.dot_general(
        onehot.astype(F32),
        grad_pre,
        (((0,), (0,)), ((), ())),
        precision=lax.Precision.HIGHEST,
        preferred_element_type=F32,
    )
    return (
        level_output,
        input_grad,
        table_grad,
        conv_in_grad[None],
        conv_out_grad[None],
        embed_grad[None],
        skip_grad[None],
        qkv_grad[None],
        out_grad[None],
        gains_grad[None],
        biases_grad[None],
    )


def solution(mesh):
    placed = (
        P(None, "dp", "section", None),
        P(None, "dp", "section", None),
        P(None, "dp"),
        P("section", "dp", None),
        P("section", "dp", None),
        P("section", "dp", None),
        P("section", "dp", None),
        P("section", "dp", None),
        P("section", "dp", None),
        P("section", "dp"),
        P("section", "dp"),
        P(None, "dp", None),
        P(None, "dp"),
    )
    return jax.shard_map(
        on_device,
        mesh=mesh,
        in_specs=placed,
        out_specs=(
            P(None, "dp", "section", None),
            P(None, "dp", "section", None),
            P(None, "dp"),
            P("section", "dp", None),
            P("section", "dp", None),
            P("section", "dp", None),
            P("section", "dp", None),
            P("section", "dp", None),
            P("section", "dp", None),
            P("section", "dp"),
            P("section", "dp"),
        ),
        check_vma=False,
    )
```

```python
from functools import partial
import math

import jax
import jax.numpy as jnp
import numpy as np
from jax import lax
from jax.experimental import pallas as pl
from jax.experimental.pallas import tpu as pltpu
from jax.sharding import PartitionSpec as P

WIDTH = 768
EMBED = 768
CLASSES = 1000
HEAD_DIM = 64
GROUPS = 32
SIDE = 8
LEVELS = 40
MICRO = 4
PIXELS = 64
TAPS = 9

EPS = 1e-05
SIGMA_LOW = 0.002
SIGMA_HIGH = 80.0

F32 = jnp.float32
BF16 = jnp.bfloat16
LANE = 128
CHUNKS = WIDTH // LANE
PER_GROUP = WIDTH // GROUPS
GROUP_SHARE = 1.0 / (PER_GROUP * PIXELS)
VMEM_LIMIT = 56 * 2**20

GAIN = 0
BIAS = 4

GROUP_OF = (np.arange(WIDTH)[:, None] // PER_GROUP == np.arange(LANE)[None, :]).astype(np.float32)


def lanes(chunk):
    return pl.ds(chunk * LANE, LANE)


def dot(left, right):
    return jnp.dot(left, right, preferred_element_type=F32)


def dot_nt(left, right):
    return lax.dot_general(left, right, (((1,), (1,)), ((), ())), preferred_element_type=F32)


def dot_tn(left, right):
    return lax.dot_general(left, right, (((0,), (0,)), ((), ())), preferred_element_type=F32)


def octet_sum(values, octets):
    width = values.shape[-1]
    partial_sums = values.reshape(SIDE, octets, width).sum(axis=0).reshape(octets // 8, 8, width)
    totals = jnp.sum(partial_sums, axis=1, keepdims=True)
    return jnp.broadcast_to(totals, partial_sums.shape).reshape(octets, width)


def over_rows(stat):
    octets, width = stat.shape
    return jnp.broadcast_to(stat[None], (SIDE, octets, width)).reshape(SIDE * octets, width)


def in_parts(values):
    first = values.astype(BF16)
    rest = values - first.astype(F32)
    second = rest.astype(BF16)
    third = (rest - second.astype(F32)).astype(BF16)
    return jnp.concatenate([first, second, third], axis=0)


def group_mean(sums, group_of, group_of_t):
    count = sums.shape[0]
    grouped = dot(in_parts(sums), group_of)
    grouped = (grouped[:count] + grouped[count : 2 * count] + grouped[2 * count :]) * GROUP_SHARE
    spread = dot(in_parts(grouped), group_of_t)
    return spread[:count] + spread[count : 2 * count] + spread[2 * count :]


def norm_stats(read, octets, group_of, group_of_t):
    sums = jnp.concatenate([octet_sum(read(c), octets) for c in range(CHUNKS)], axis=1)
    mean = group_mean(sums, group_of, group_of_t)
    squares = []
    for c in range(CHUNKS):
        centered = read(c) - over_rows(mean[:, c * LANE : (c + 1) * LANE])
        squares.append(octet_sum(centered * centered, octets))
    spread = group_mean(jnp.concatenate(squares, axis=1), group_of, group_of_t)
    return mean, lax.rsqrt(spread + EPS)


def normed_chunk(values, stat_ref, c):
    mean = stat_ref[0, :, lanes(c)]
    inv = stat_ref[1, :, lanes(c)]
    return (values - over_rows(mean)) * over_rows(inv)


def sigmoid(values):
    return 1.0 / (1.0 + jnp.exp(-values))


def silu_slope(values):
    gate = sigmoid(values)
    return gate * (1.0 + values * (1.0 - gate))


def put_shifted(planes, base, values, c, octets):
    rows = values.shape[0]
    column = lax.broadcasted_iota(jnp.int32, values.shape, 0) & 7
    before = jnp.where(column != 0, pltpu.roll(values, 1, 0), 0.0)
    after = jnp.where(column != 7, pltpu.roll(values, rows - 1, 0), 0.0)
    planes[base, pl.ds(octets, rows), lanes(c)] = before.astype(BF16)
    planes[base + 1, pl.ds(octets, rows), lanes(c)] = values.astype(BF16)
    planes[base + 2, pl.ds(octets, rows), lanes(c)] = after.astype(BF16)


def clear_edges(planes, octets):
    count, rows, width = planes.shape
    edge = jnp.zeros((count, octets, width), BF16)
    planes[:, pl.ds(0, octets), :] = edge
    planes[:, pl.ds(rows - octets, octets), :] = edge


def row_total(values):
    return jnp.sum(values, axis=0, keepdims=True)


def norm_back(read_grad, read_normed, gain_of, stat_ref, octets, tables, write, sums_out):
    group_of, group_of_t = tables
    first, second = [], []
    for c in range(CHUNKS):
        grad = read_grad(c)
        first.append(octet_sum(grad, octets))
        second.append(octet_sum(grad * read_normed(c), octets))
    first = jnp.concatenate(first, axis=1)
    second = jnp.concatenate(second, axis=1)
    sums_out(first, second)
    gain = gain_of(None)
    both = group_mean(jnp.concatenate([first * gain, second * gain], axis=0), group_of, group_of_t)
    for c in range(CHUNKS):
        part = slice(c * LANE, (c + 1) * LANE)
        inv = over_rows(stat_ref[1, :, lanes(c)])
        mean_one = over_rows(both[:octets, part])
        mean_two = over_rows(both[octets:, part])
        write(c, inv * (gain_of(c) * read_grad(c) - mean_one - read_normed(c) * mean_two))


def conv_in_forward(decoder, octets, *refs):
    if decoder:
        hidden, skipped, weights, modulation, params, group_of, group_of_t = refs[:7]
        conv_one, stat_c, middle, turned_w, stat_h, stat_s, turned_h, turned_s, planes, held, sems = refs[7:]
        sides = ((hidden, stat_h, turned_h, 0), (skipped, stat_s, turned_s, 1))
    else:
        hidden, weights, modulation, params, group_of, group_of_t = refs[:6]
        conv_one, stat_c, middle, turned_w, stat_h, turned_h, planes, held, sems = refs[6:]
        sides = ((hidden, stat_h, turned_h, 0),)
    span = WIDTH * len(sides)
    copies = [
        pltpu.make_async_copy(
            weights.at[pl.ds(tap * 2 * WIDTH, span)], held.at[pl.ds(tap * span, span)], sems.at[tap]
        )
        for tap in range(TAPS)
    ]
    for copy in copies:
        copy.start()
    rows = hidden.shape[0]
    tables = (group_of[...], group_of_t[...])
    clear_edges(planes, octets)
    for source, stat, turned, which in sides:
        mean, inv = norm_stats(lambda c: source[:, lanes(c)].astype(F32), octets, *tables)
        stat[0] = mean
        stat[1] = inv
        for c in range(CHUNKS):
            normed = normed_chunk(source[:, lanes(c)].astype(F32), stat, c)
            value = (
                normed * params[pl.ds(GAIN + which, 1), lanes(c)]
                + params[pl.ds(BIAS + which, 1), lanes(c)]
            )
            value = value * sigmoid(value)
            put_shifted(planes, 3 * which, value, c, octets)
            turned[lanes(c), :] = normed.T.astype(BF16)
    for tap in range(TAPS):
        copies[tap].wait()
        for half in range(len(sides)):
            part = dot(
                planes[3 * half + tap % 3, pl.ds(octets * (tap // 3), rows), :],
                held[pl.ds(tap * span + half * WIDTH, WIDTH), :],
            )
            if tap == 0 and half == 0:
                conv_one[...] = part + params[pl.ds(BIAS + 2, 1), :]
            else:
                conv_one[...] += part
    mean, inv = norm_stats(lambda c: conv_one[:, lanes(c)], octets, *tables)
    stat_c[0] = mean
    stat_c[1] = inv
    for c in range(CHUNKS):
        normed = (
            normed_chunk(conv_one[:, lanes(c)], stat_c, c) * params[pl.ds(GAIN + 2, 1), lanes(c)]
            + params[pl.ds(BIAS + 5, 1), lanes(c)]
        )
        scale = over_rows(modulation[:, lanes(c)])
        shift = over_rows(modulation[:, lanes(CHUNKS + c)])
        value = normed * (1.0 + scale) + shift
        value = value * sigmoid(value)
        middle[:, lanes(c)] = value.astype(BF16)
        turned_w[lanes(c), :] = value.T.astype(BF16)


REST = {
    "conv_out": TAPS * WIDTH,
    "query": WIDTH,
    "key": WIDTH,
    "value": WIDTH,
    "out": WIDTH,
    "skip": 2 * WIDTH,
}


class Rest:
    def __init__(self, source, sems, pieces):
        self.source, self.sems, self.pieces, self.waits = source, sems, pieces, {}

    def fetch(self, name, held):
        offset = 0
        for other, total in REST.items():
            share = total // self.pieces
            if other == name:
                break
            offset += share
        copies = []
        for piece in range(self.pieces):
            copies.append(
                pltpu.make_async_copy(
                    self.source.at[piece, pl.ds(offset, share)],
                    held.at[pl.ds(piece * share, share)],
                    self.sems.at[len(self.waits), piece],
                )
            )
            copies[-1].start()
        self.waits[name] = (share, copies, [False] * self.pieces)

    def need(self, name, stop):
        share, copies, done = self.waits[name]
        for piece, copy in enumerate(copies):
            if piece * share < stop and not done[piece]:
                copy.wait()
                done[piece] = True


def head_mask(rows):
    return lax.broadcasted_iota(jnp.int32, (rows, LANE), 1) < HEAD_DIM


def image_bias(rows, images):
    row_image = lax.rem(lax.shift_right_logical(lax.broadcasted_iota(jnp.int32, (rows, rows), 0), 3), images)
    column_image = lax.rem(lax.shift_right_logical(lax.broadcasted_iota(jnp.int32, (rows, rows), 1), 3), images)
    return jnp.where(row_image == column_image, 0.0, -1e30).astype(F32)


def attention_of(queries, keys, apart):
    scores = dot_nt(queries, keys) * (1.0 / math.sqrt(HEAD_DIM)) + apart
    weight = jnp.exp(scores - jnp.max(scores, axis=1, keepdims=True))
    return weight * (1.0 / jnp.sum(weight, axis=1, keepdims=True))


def block_forward(decoder, octets, pieces, *refs):
    if decoder:
        middle, hidden, skipped, rest, params, group_of, group_of_t = refs[:7]
        refs = refs[7:]
    else:
        middle, hidden, rest, params, group_of, group_of_t = refs[:6]
        refs = refs[6:]
    result, residual, stat_r, attend, project, mixed, planes, apart = refs[:8]
    held_conv, held_qkv, held_out, held_skip, sems = refs[8:]
    weights = Rest(rest, sems, pieces)
    weights.fetch("conv_out", held_conv)
    if decoder:
        weights.fetch("skip", held_skip)
    for index, name in enumerate(("query", "key", "value")):
        weights.fetch(name, held_qkv.at[index])
    weights.fetch("out", held_out)
    rows = middle.shape[0]
    tables = (group_of[...], group_of_t[...])
    clear_edges(planes, octets)
    for c in range(CHUNKS):
        put_shifted(planes, 0, middle[:, lanes(c)].astype(F32), c, octets)
    apart[...] = image_bias(rows, octets // 8)
    for tap in range(TAPS):
        weights.need("conv_out", (tap + 1) * WIDTH)
        part = dot(
            planes[tap % 3, pl.ds(octets * (tap // 3), rows), :], held_conv[pl.ds(tap * WIDTH, WIDTH), :]
        )
        if tap == 0:
            residual[...] = part + params[pl.ds(BIAS + 6, 1), :]
        else:
            residual[...] += part
    if decoder:
        weights.need("skip", 2 * WIDTH)
        residual[...] += (
            dot(hidden[...], held_skip[pl.ds(0, WIDTH), :])
            + dot(skipped[...], held_skip[pl.ds(WIDTH, WIDTH), :])
            + params[pl.ds(BIAS + 7, 1), :]
        )
    else:
        residual[...] += hidden[...].astype(F32)
    mean, inv = norm_stats(lambda c: residual[:, lanes(c)], octets, *tables)
    stat_r[0] = mean
    stat_r[1] = inv
    for c in range(CHUNKS):
        attend[:, lanes(c)] = (
            normed_chunk(residual[:, lanes(c)], stat_r, c) * params[pl.ds(GAIN + 3, 1), lanes(c)]
            + params[pl.ds(BIAS + 8, 1), lanes(c)]
        ).astype(BF16)
    for index, (name, bias) in enumerate((("query", 9), ("key", None), ("value", 10))):
        weights.need(name, WIDTH)
        part = dot(attend[...], held_qkv[index])
        if bias is not None:
            part = part + params[pl.ds(BIAS + bias, 1), :]
        project[:, pl.ds(index * WIDTH, WIDTH)] = part.astype(BF16)
    left = head_mask(rows)
    for pair in range(CHUNKS):
        queries = project[:, lanes(pair)]
        keys_h = project[:, lanes(CHUNKS + pair)]
        values_h = project[:, lanes(2 * CHUNKS + pair)]
        parts = []
        for half in (left, jnp.logical_not(left)):
            chosen = jnp.where(half, queries, jnp.zeros_like(queries))
            attention = attention_of(chosen, keys_h, apart[...])
            parts.append(dot(attention.astype(BF16), values_h))
        mixed[:, lanes(pair)] = jnp.where(left, parts[0], parts[1]).astype(BF16)
    weights.need("out", WIDTH)
    result[...] = (
        residual[...] + dot(mixed[...], held_out[...]) + params[pl.ds(BIAS + 11, 1), :]
    ).astype(BF16)


def attention_backward(decoder, octets, pieces, shards, chained, *refs):
    grad_out, project, residual, stat_r, attend, mixed, hidden, skipped, active, rest = refs[:10]
    params, group_of, group_of_t = refs[10:13]
    refs = refs[14:] if chained else refs[13:]
    grad_top, grad_project, grad_resid, grad_resid_b, sums, products = refs[:6]
    scratch, grad_mixed, apart, held_qkv, held_out, sems, built, built_sems = refs[6:]
    weights = Rest(rest, sems, pieces)
    weights.fetch("out", held_out)
    for index, name in enumerate(("query", "key", "value")):
        weights.fetch(name, held_qkv.at[index])
    rows = residual.shape[0]
    tables = (group_of[...], group_of_t[...])
    sums[...] = jnp.zeros(sums.shape, F32)
    apart[...] = image_bias(rows, octets // 8)
    leaving = []

    def leave(first, width):
        part = pl.ds(first * WIDTH, width * WIDTH)
        copy = pltpu.make_async_copy(built.at[:, part], products.at[:, part], built_sems.at[len(leaving)])
        leaving.append(copy)

        @pl.when(active[0] == 1)
        def _():
            copy.start()

    def put_sum(row, c, values):
        sums[pl.ds(row, 1), lanes(c)] = row_total(values)

    top = grad_out[...].astype(BF16)
    grad_top[...] = top
    for c in range(CHUNKS):
        put_sum(BIAS + 11, c, grad_top[:, lanes(c)].astype(F32))
    built[:, pl.ds(3 * WIDTH, WIDTH)] = dot_tn(mixed[...], top).astype(BF16)
    leave(3, 1)
    weights.need("out", WIDTH)
    grad_mixed[...] = dot_nt(top, held_out[...]).astype(BF16)
    left = head_mask(rows)
    root = 1.0 / math.sqrt(HEAD_DIM)
    for pair in range(CHUNKS):
        queries = project[:, lanes(pair)]
        keys_h = project[:, lanes(CHUNKS + pair)]
        values_h = project[:, lanes(2 * CHUNKS + pair)]
        grads_h = grad_mixed[:, lanes(pair)]
        parts = []
        for half in (left, jnp.logical_not(left)):
            chosen = jnp.where(half, queries, jnp.zeros_like(queries))
            chosen_grad = jnp.where(half, grads_h, jnp.zeros_like(grads_h))
            attention = attention_of(chosen, keys_h, apart[...])
            grad_attention = dot_nt(chosen_grad, values_h)
            weighted = grad_attention * attention
            grad_scores = (weighted - attention * jnp.sum(weighted, axis=1, keepdims=True)).astype(BF16)
            parts.append(
                (
                    dot(grad_scores, keys_h) * root,
                    dot_tn(grad_scores, queries) * root,
                    dot_tn(attention.astype(BF16), grads_h),
                )
            )
        for index in range(3):
            joined = jnp.where(left, parts[0][index], parts[1][index]).astype(BF16)
            grad_project[:, lanes(index * CHUNKS + pair)] = joined
            if index == 0:
                put_sum(BIAS + 9, pair, joined.astype(F32))
            if index == 2:
                put_sum(BIAS + 10, pair, joined.astype(F32))
    for index in range(3):
        columns = pl.ds(index * WIDTH, WIDTH)
        built[:, columns] = dot_tn(attend[...], grad_project[:, columns]).astype(BF16)
    leave(0, 3)
    for index, name in enumerate(("query", "key", "value")):
        weights.need(name, WIDTH)
        part = dot_nt(grad_project[:, pl.ds(index * WIDTH, WIDTH)], held_qkv[index])
        if index == 0:
            scratch[...] = part
        else:
            scratch[...] += part

    def gain_attend(c):
        return params[pl.ds(GAIN + 3, 1), :] if c is None else params[pl.ds(GAIN + 3, 1), lanes(c)]

    def sums_attend(first, second):
        sums[pl.ds(BIAS + 8, 1), :] = row_total(first) * 0.125
        sums[pl.ds(GAIN + 3, 1), :] = row_total(second) * 0.125

    def write_resid(c, grad):
        total = grad_out[:, lanes(c)].astype(F32) + grad
        grad_resid[:, lanes(c)] = total
        rounded = total.astype(BF16)
        grad_resid_b[:, lanes(c)] = rounded
        rounded = rounded.astype(F32)
        put_sum(BIAS + 6, c, rounded)
        if decoder:
            put_sum(BIAS + 7, c, rounded)

    norm_back(
        lambda c: scratch[:, lanes(c)],
        lambda c: normed_chunk(residual[:, lanes(c)], stat_r, c),
        gain_attend,
        stat_r,
        octets,
        tables,
        write_resid,
        sums_attend,
    )
    share = WIDTH // shards
    for side, source in enumerate((hidden, skipped)):
        first = side * shards // 2
        if decoder:
            part = dot_tn(source[...], grad_resid_b[...]).astype(BF16)
        else:
            part = jnp.zeros((WIDTH, WIDTH), BF16)
        for index in range(shards // 2):
            target = pl.ds((first + index) * share, share)
            for half in range(2):
                built[target, pl.ds((4 + half) * WIDTH, WIDTH)] = part[
                    (2 * index + half) * share : (2 * index + half + 1) * share
                ]
    leave(4, 2)

    @pl.when(active[0] == 1)
    def _():
        for copy in leaving:
            copy.wait()


def middle_backward(octets, pieces, *refs):
    grad_resid_b, conv_one, stat_c, modulation, rest, params, group_of, group_of_t = refs[:8]
    grad_conv_b, grad_mod, sums, scratch, planes, held_conv, sems = refs[8:]
    weights = Rest(rest, sems, pieces)
    weights.fetch("conv_out", held_conv)
    rows = conv_one.shape[0]
    tables = (group_of[...], group_of_t[...])
    sums[...] = jnp.zeros(sums.shape, F32)
    clear_edges(planes, octets)
    for c in range(CHUNKS):
        put_shifted(planes, 0, grad_resid_b[:, lanes(c)].astype(F32), c, octets)
    for tap in range(TAPS):
        weights.need("conv_out", (tap + 1) * WIDTH)
        part = dot_nt(
            planes[2 - tap % 3, pl.ds(octets * (2 - tap // 3), rows), :],
            held_conv[pl.ds(tap * WIDTH, WIDTH), :],
        )
        if tap == 0:
            scratch[...] = part
        else:
            scratch[...] += part
    for c in range(CHUNKS):
        normed = (
            normed_chunk(conv_one[:, lanes(c)], stat_c, c) * params[pl.ds(GAIN + 2, 1), lanes(c)]
            + params[pl.ds(BIAS + 5, 1), lanes(c)]
        )
        scale = over_rows(modulation[:, lanes(c)])
        shift = over_rows(modulation[:, lanes(CHUNKS + c)])
        scratch[:, lanes(c)] = scratch[:, lanes(c)] * silu_slope(normed * (1.0 + scale) + shift)

    def gain_middle(c):
        if c is None:
            return params[pl.ds(GAIN + 2, 1), :] * (1.0 + modulation[:, pl.ds(0, WIDTH)])
        return over_rows(params[pl.ds(GAIN + 2, 1), lanes(c)] * (1.0 + modulation[:, lanes(c)]))

    def sums_middle(first, second):
        scaled = 1.0 + modulation[:, pl.ds(0, WIDTH)]
        sums[pl.ds(BIAS + 5, 1), :] = row_total(first * scaled) * 0.125
        sums[pl.ds(GAIN + 2, 1), :] = row_total(second * scaled) * 0.125
        grad_scale = (
            params[pl.ds(GAIN + 2, 1), :] * second + params[pl.ds(BIAS + 5, 1), :] * first
        ).astype(BF16)
        grad_shift = first.astype(BF16)
        grad_mod[:, pl.ds(0, WIDTH)] = grad_scale
        grad_mod[:, pl.ds(WIDTH, WIDTH)] = grad_shift
        sums[pl.ds(BIAS + 3, 1), :] = row_total(grad_scale.astype(F32)) * 0.125
        sums[pl.ds(BIAS + 4, 1), :] = row_total(grad_shift.astype(F32)) * 0.125

    def write_conv(c, grad):
        rounded = grad.astype(BF16)
        grad_conv_b[:, lanes(c)] = rounded
        sums[pl.ds(BIAS + 2, 1), lanes(c)] = row_total(rounded.astype(F32))

    norm_back(
        lambda c: scratch[:, lanes(c)],
        lambda c: normed_chunk(conv_one[:, lanes(c)], stat_c, c),
        gain_middle,
        stat_c,
        octets,
        tables,
        write_conv,
        sums_middle,
    )


def conv_in_backward(decoder, joined, octets, pieces, *refs):
    if decoder:
        grad_conv, hidden, skipped, stat_h, stat_s, grad_resid, grad_resid_b, weights, rest = refs[:9]
        params, group_of, group_of_t = refs[9:12]
        grad_hidden, grad_skipped, sums = refs[12:15] if not joined else (refs[15], refs[15], refs[13])
        scratch, planes, held, held_skip, sems, rest_sems = refs[15:] if not joined else refs[14:15] + refs[16:]
        sides = ((hidden, stat_h, grad_hidden, 0), (skipped, stat_s, grad_skipped, 1))
    else:
        grad_conv, hidden, stat_h, grad_resid, weights, params, group_of, group_of_t = refs[:8]
        grad_hidden, sums, scratch, planes, held, sems = refs[8:]
        sides = ((hidden, stat_h, grad_hidden, 0),)
    span = WIDTH * len(sides)
    copies = [
        pltpu.make_async_copy(
            weights.at[pl.ds(tap * 2 * WIDTH, span)], held.at[pl.ds(tap * span, span)], sems.at[tap]
        )
        for tap in range(TAPS)
    ]
    for copy in copies:
        copy.start()
    if decoder:
        skip_weights = Rest(rest, rest_sems, pieces)
        skip_weights.fetch("skip", held_skip)
    rows = hidden.shape[0]
    tables = (group_of[...], group_of_t[...])
    sums[...] = jnp.zeros(sums.shape, F32)
    clear_edges(planes, octets)
    for c in range(CHUNKS):
        put_shifted(planes, 0, grad_conv[:, lanes(c)].astype(F32), c, octets)
    for tap in range(TAPS):
        copies[tap].wait()
        for _, _, _, half in sides:
            part = dot_nt(
                planes[2 - tap % 3, pl.ds(octets * (2 - tap // 3), rows), :],
                held[pl.ds(tap * span + half * WIDTH, WIDTH), :],
            )
            if tap == 0:
                scratch[half] = part
            else:
                scratch[half] += part
    if decoder:
        skip_weights.need("skip", 2 * WIDTH)
    for source, stat, target, which in sides:

        def normed_of(c, source=source, stat=stat):
            return normed_chunk(source[:, lanes(c)].astype(F32), stat, c)

        def gain_input(c, which=which):
            row = pl.ds(GAIN + which, 1)
            return params[row, :] if c is None else params[row, lanes(c)]

        for c in range(CHUNKS):
            value = normed_of(c) * gain_input(c) + params[pl.ds(BIAS + which, 1), lanes(c)]
            scratch[which, :, lanes(c)] = scratch[which, :, lanes(c)] * silu_slope(value)

        def sums_input(first, second, which=which):
            sums[pl.ds(BIAS + which, 1), :] = row_total(first) * 0.125
            sums[pl.ds(GAIN + which, 1), :] = row_total(second) * 0.125

        if decoder:
            part = dot_nt(grad_resid_b[...], held_skip[pl.ds(which * WIDTH, WIDTH), :])
            if joined and which:
                target[...] += part
            else:
                target[...] = part

        def write_input(c, grad, target=target):
            if decoder:
                target[:, lanes(c)] += grad
            else:
                target[:, lanes(c)] = grad + grad_resid[:, lanes(c)]

        norm_back(
            lambda c, which=which: scratch[which, :, lanes(c)],
            normed_of,
            gain_input,
            stat,
            octets,
            tables,
            write_input,
            sums_input,
        )
    if joined:
        refs[12][...] = grad_hidden[...].astype(BF16)


def shape(dims, kind):
    return jax.ShapeDtypeStruct(dims, kind)


IN_VMEM = pl.BlockSpec(memory_space=pltpu.VMEM)
IN_HBM = pl.BlockSpec(memory_space=pl.ANY)
IN_SMEM = pl.BlockSpec(memory_space=pltpu.SMEM)


def call(body, operands, places, outputs, scratch, flops, name, out_places=None, aliases=None):
    moved = sum(int(np.prod(v.shape)) * v.dtype.itemsize for v in (*operands, *outputs))
    return pl.pallas_call(
        body,
        out_shape=outputs,
        in_specs=[places.get(index, IN_VMEM) for index in range(len(operands))],
        out_specs=[(out_places or {}).get(index, IN_VMEM) for index in range(len(outputs))],
        scratch_shapes=scratch,
        input_output_aliases=aliases or {},
        compiler_params=pltpu.CompilerParams(vmem_limit_bytes=VMEM_LIMIT),
        cost_estimate=pl.CostEstimate(flops=flops, bytes_accessed=moved, transcendentals=0),
        name=name,
    )(*operands)


def run_conv_in(decoder, hidden, skipped, weights, modulation, params, tables):
    rows = hidden.shape[0]
    octets = rows // SIDE
    sides = 2 if decoder else 1
    inputs = [hidden, skipped] if decoder else [hidden]
    outputs = [
        shape((rows, WIDTH), F32),
        shape((2, octets, WIDTH), F32),
        shape((rows, WIDTH), BF16),
        shape((WIDTH, rows), BF16),
    ]
    outputs += [shape((2, octets, WIDTH), F32)] * sides
    outputs += [shape((WIDTH, rows), BF16)] * sides
    return call(
        partial(conv_in_forward, decoder, octets),
        [*inputs, weights, modulation, params, *tables],
        {len(inputs): IN_HBM},
        outputs,
        [
            pltpu.VMEM((3 * sides, rows + 2 * octets, WIDTH), BF16),
            pltpu.VMEM((sides * TAPS * WIDTH, WIDTH), BF16),
            pltpu.SemaphoreType.DMA((TAPS,)),
        ],
        2 * rows * sides * TAPS * WIDTH * WIDTH,
        "conv_in_forward",
    )


def run_block(decoder, middle, hidden, skipped, rest, params, tables):
    rows = hidden.shape[0]
    octets = rows // SIDE
    pieces = rest.shape[0]
    inputs = [middle, hidden, skipped] if decoder else [middle, hidden]
    outputs = [
        shape((rows, WIDTH), BF16),
        shape((rows, WIDTH), F32),
        shape((2, octets, WIDTH), F32),
        shape((rows, WIDTH), BF16),
        shape((rows, 3 * WIDTH), BF16),
        shape((rows, WIDTH), BF16),
    ]
    return call(
        partial(block_forward, decoder, octets, pieces),
        [*inputs, rest, params, *tables],
        {len(inputs): IN_HBM},
        outputs,
        [
            pltpu.VMEM((3, rows + 2 * octets, WIDTH), BF16),
            pltpu.VMEM((rows, rows), F32),
            pltpu.VMEM((TAPS * WIDTH, WIDTH), BF16),
            pltpu.VMEM((3, WIDTH, WIDTH), BF16),
            pltpu.VMEM((WIDTH, WIDTH), BF16),
            pltpu.VMEM((2 * WIDTH, WIDTH), BF16),
            pltpu.SemaphoreType.DMA((6, pieces)),
        ],
        2 * rows * (TAPS + 6) * WIDTH * WIDTH,
        "block_forward",
    )


def run_attention_back(decoder, shards, grad_out, entry, active, rest, params, tables, before):
    rows = entry["residual"].shape[0]
    octets = rows // SIDE
    pieces = rest.shape[0]
    skipped = entry["skipped"] if decoder else entry["hidden"]
    operands = [
        grad_out,
        entry["project"],
        entry["residual"],
        entry["stat_r"],
        entry["attend"],
        entry["mixed"],
        entry["hidden"],
        skipped,
        active,
        rest,
        params,
        *tables,
    ]
    places = {8: IN_SMEM, 9: IN_HBM}
    aliases = {}
    if before is not None:
        places[len(operands)] = IN_HBM
        aliases = {len(operands): 5}
        operands.append(before)
    return call(
        partial(attention_backward, decoder, octets, pieces, shards, before is not None),
        operands,
        places,
        [
            shape((rows, WIDTH), BF16),
            shape((rows, 3 * WIDTH), BF16),
            shape((rows, WIDTH), F32),
            shape((rows, WIDTH), BF16),
            shape((16, WIDTH), F32),
            shape((WIDTH, 6 * WIDTH), BF16),
        ],
        [
            pltpu.VMEM((rows, WIDTH), F32),
            pltpu.VMEM((rows, WIDTH), BF16),
            pltpu.VMEM((rows, rows), F32),
            pltpu.VMEM((3, WIDTH, WIDTH), BF16),
            pltpu.VMEM((WIDTH, WIDTH), BF16),
            pltpu.SemaphoreType.DMA((4, pieces)),
            pltpu.VMEM((WIDTH, 6 * WIDTH), BF16),
            pltpu.SemaphoreType.DMA((3,)),
        ],
        2 * rows * 14 * WIDTH * WIDTH,
        "attention_backward",
        out_places={5: IN_HBM},
        aliases=aliases,
    )


def run_middle_back(grad_resid_b, conv_one, stat_c, modulation, rest, params, tables):
    rows = conv_one.shape[0]
    octets = rows // SIDE
    pieces = rest.shape[0]
    return call(
        partial(middle_backward, octets, pieces),
        [grad_resid_b, conv_one, stat_c, modulation, rest, params, *tables],
        {4: IN_HBM},
        [
            shape((rows, WIDTH), BF16),
            shape((octets, 2 * WIDTH), BF16),
            shape((16, WIDTH), F32),
        ],
        [
            pltpu.VMEM((rows, WIDTH), F32),
            pltpu.VMEM((3, rows + 2 * octets, WIDTH), BF16),
            pltpu.VMEM((TAPS * WIDTH, WIDTH), BF16),
            pltpu.SemaphoreType.DMA((1, pieces)),
        ],
        2 * rows * TAPS * WIDTH * WIDTH,
        "middle_backward",
    )


def run_conv_in_back(decoder, grad_conv, hidden, skipped, stat_h, stat_s, grad_resid, grad_resid_b, weights, rest, params, tables, joined):
    rows = hidden.shape[0]
    octets = rows // SIDE
    sides = 2 if decoder else 1
    pieces = rest.shape[0]
    if decoder:
        inputs = [grad_conv, hidden, skipped, stat_h, stat_s, grad_resid, grad_resid_b, weights, rest]
        far = {7: IN_HBM, 8: IN_HBM}
    else:
        inputs = [grad_conv, hidden, stat_h, grad_resid, weights]
        far = {4: IN_HBM}
    scratch = [
        pltpu.VMEM((sides, rows, WIDTH), F32),
        pltpu.VMEM((3, rows + 2 * octets, WIDTH), BF16),
        pltpu.VMEM((sides * TAPS * WIDTH, WIDTH), BF16),
    ]
    outputs = [shape((rows, WIDTH), F32)] * sides
    if joined:
        outputs = [shape((rows, WIDTH), BF16)]
        scratch.insert(1, pltpu.VMEM((rows, WIDTH), F32))
    if decoder:
        scratch.append(pltpu.VMEM((2 * WIDTH, WIDTH), BF16))
    scratch.append(pltpu.SemaphoreType.DMA((TAPS,)))
    if decoder:
        scratch.append(pltpu.SemaphoreType.DMA((1, pieces)))
    return call(
        partial(conv_in_backward, decoder, joined, octets, pieces),
        [*inputs, params, *tables],
        far,
        outputs + [shape((16, WIDTH), F32)],
        scratch,
        2 * rows * sides * TAPS * WIDTH * WIDTH,
        "conv_in_backward",
    )


def tap_slices_kernel(rows_in, rows_out, octets, place, order, fields, affine, cols_in, cols_out):
    _, height, width = fields.shape
    lane = lax.broadcasted_iota(jnp.int32, (1, width), 1)
    grid_row = lax.div(lane, octets)
    grid_column = lane & 7
    second = height - 2 * WIDTH
    for rows, channels, target in ((rows_in, 2 * WIDTH, cols_in), (rows_out, WIDTH, cols_out)):
        block = rows // TAPS
        per_tap = channels // block
        for index in range(TAPS):
            position = place[0] * TAPS + index
            tap = lax.div(position, per_tap)
            start = pl.multiple_of(lax.rem(position, per_tap) * block, 16)
            down = lax.div(tap, 3) - 1
            across = lax.rem(tap, 3) - 1
            inside = (
                (grid_row + down >= 0)
                & (grid_row + down < SIDE)
                & (grid_column + across >= 0)
                & (grid_column + across < 8)
            )
            back = lax.rem(width - (octets * down + across), width)
            if target is cols_in:
                side = lax.div(start, WIDTH)
                spot = pl.multiple_of(start - side * (WIDTH - second), 16)
                inside = inside & (lane >= lax.mul(side, 1 - place[1]) * width)
            else:
                spot = pl.multiple_of(start + height - WIDTH, 16)
            values = fields[0, pl.ds(spot, block), :].astype(F32)
            if target is cols_in:
                values = values * affine[pl.ds(start, block), 0:1] + affine[pl.ds(start, block), 1:2]
                values = values * sigmoid(values)
            turned = jnp.where(inside, pltpu.roll(values, back, 1), 0.0).astype(BF16)
            target[pl.ds(index * block, block), :] = turned


def tap_slices_plain(fields, rows, channels, place, octets):
    pieces, _, width = fields.shape
    spots = place * rows + jnp.arange(rows)
    taps = spots // channels
    values = jnp.take(fields, spots % channels, axis=1)
    lane = jnp.arange(width)
    total = jnp.zeros_like(values)
    for tap in range(TAPS):
        down, across = tap // 3 - 1, tap % 3 - 1
        row, column = lane // octets + down, lane % 8 + across
        inside = (row >= 0) & (row < SIDE) & (column >= 0) & (column < 8)
        moved = jnp.roll(values, -(octets * down + across), axis=2)
        total = jnp.where((taps == tap)[None, :, None] & inside, moved, total)
    return total.transpose(1, 0, 2).reshape(rows, pieces * width)


def tap_slices(fields, order, affine, rows_in, rows_out, place, decoder, octets):
    _, height, width = fields.shape
    pieces = order.shape[0]
    if rows_in % (TAPS * 16) or rows_out % (TAPS * 16):
        fields = jnp.take(fields, order, axis=0)
        sides = jnp.concatenate([fields[:, :WIDTH], fields[:, height - 2 * WIDTH : height - WIDTH]], axis=1)
        sides = sides.astype(F32) * affine[:, :1] + affine[:, 1:]
        keep = (jnp.arange(2 * WIDTH)[:, None] < WIDTH) | decoder
        sides = jnp.where(keep, jax.nn.silu(sides), 0.0).astype(BF16)
        return (
            tap_slices_plain(sides, rows_in, 2 * WIDTH, place, octets),
            tap_slices_plain(fields[:, height - WIDTH :], rows_out, WIDTH, place, octets),
        )
    return pl.pallas_call(
        partial(tap_slices_kernel, rows_in, rows_out, octets),
        grid_spec=pltpu.PrefetchScalarGridSpec(
            num_scalar_prefetch=2,
            grid=(pieces,),
            in_specs=[
                pl.BlockSpec((1, height, width), lambda piece, place, order: (order[piece], 0, 0)),
                pl.BlockSpec((2 * WIDTH, 2), lambda piece, place, order: (0, 0)),
            ],
            out_specs=[
                pl.BlockSpec((rows_in, width), lambda piece, place, order: (0, piece)),
                pl.BlockSpec((rows_out, width), lambda piece, place, order: (0, piece)),
            ],
        ),
        out_shape=[shape((rows, pieces * width), BF16) for rows in (rows_in, rows_out)],
        compiler_params=pltpu.CompilerParams(vmem_limit_bytes=VMEM_LIMIT),
        cost_estimate=pl.CostEstimate(
            flops=0, bytes_accessed=4 * pieces * height * width, transcendentals=0
        ),
        name="tap_slices",
    )(jnp.stack([place, decoder.astype(jnp.int32)]).astype(jnp.int32), order, fields, affine)


def grad_step_kernel(count, sides, *refs):
    factors, blocks, targets = refs[:sides], refs[sides : sides + count], refs[-sides:]
    totals = refs[sides + count : len(refs) - sides]
    depth = factors[0].shape[1] // count
    for side in range(sides):
        cols = factors[side]
        rows = cols.shape[0]
        tile = rows // 3 if rows % 48 == 0 else rows
        for start in range(0, rows, tile):
            total = totals[side][pl.ds(start, tile), :] if totals else None
            for number in range(count):
                part = dot(
                    cols[pl.ds(start, tile), pl.ds(number * depth, depth)],
                    blocks[number][pl.ds(side * depth, depth), :],
                )
                total = part if total is None else total + part
            targets[side][pl.ds(start, tile), :] = total


def grad_step(cols_out, cols_in, blocks, *totals):
    operands = [cols_out, cols_in, *blocks]
    aliases = {}
    if totals[0] is not None:
        aliases = {len(operands): 0, len(operands) + 1: 1}
        operands += totals
    return call(
        partial(grad_step_kernel, len(blocks), 2),
        operands,
        {},
        [shape((cols.shape[0], WIDTH), F32) for cols in (cols_out, cols_in)],
        [],
        2 * (cols_out.shape[0] + cols_in.shape[0]) * cols_in.shape[1] * WIDTH,
        "grad_step",
        aliases=aliases,
    )


class Doubling:
    def __init__(self, value, axis):
        self.axis, self.value, self.distance = axis, value[None], 1

    def step(self):
        count, index = lax.axis_size(self.axis), lax.axis_index(self.axis)
        if self.distance < count:
            pairs = [(i, i ^ self.distance) for i in range(count)]
            other = lax.ppermute(self.value, self.axis, pairs)
            self.value = jnp.where(
                (index // self.distance) % 2 == 0,
                jnp.concatenate([self.value, other], axis=0),
                jnp.concatenate([other, self.value], axis=0),
            )
            self.distance *= 2

    def finish(self):
        while self.distance < lax.axis_size(self.axis):
            self.step()
        return self.value


class Halving:
    def __init__(self, value, axis):
        self.axis, self.value, self.distance = axis, value, lax.axis_size(axis) // 2

    def step(self):
        count, index, distance = lax.axis_size(self.axis), lax.axis_index(self.axis), self.distance
        if distance:
            upper = (index // distance) % 2 == 1
            keep = jnp.where(upper, self.value[distance:], self.value[:distance])
            send = jnp.where(upper, self.value[:distance], self.value[distance:])
            pairs = [(i, i ^ distance) for i in range(count)]
            self.value = keep + lax.ppermute(send, self.axis, pairs)
            self.distance //= 2

    def finish(self):
        while self.distance:
            self.step()
        return self.value[0]


class Ring:
    def __init__(self, value, axis):
        self.axis = axis
        self.count = lax.axis_size(axis)
        self.stride = self.count // 4
        self.values, self.rows, self.steps = [value], [], []

    def turn(self):
        around = [(i, (i + self.stride) % self.count) for i in range(self.count)]
        self.values.append(lax.ppermute(self.values[-1], self.axis, around))
        return self.values[-1]

    def spread(self):
        stride = self.stride
        beside = [(i, i // stride * stride + (i + 2) % stride) for i in range(self.count)]
        row = [self.values[len(self.rows)]]
        for _ in range(stride // 2 - 1):
            row.append(lax.ppermute(row[-1], self.axis, beside))
        self.rows.append(row)
        return row[1:]

    def share(self, step):
        row = self.rows[step]
        core = [(i, i ^ 1) for i in range(self.count)]
        self.steps.append(row + [lax.ppermute(part, self.axis, core) for part in row])

    def order(self, step):
        index, stride = lax.axis_index(self.axis), self.stride
        quarter = (index // stride + 4 - step) % 4 * stride
        sources = []
        for core in range(2):
            for beside in range(stride // 2):
                sources.append(quarter + (index % stride + stride - 2 * beside) % stride // 2 * 2 + (index + core) % 2)
        return jnp.stack(sources).astype(jnp.int32)


def together(*values):
    return lax.optimization_barrier(values)


def moved(value, source, target):
    return lax.ppermute(value, "section", [(source, target)])


def to_rows(value):
    micro, images, pixels, channels = value.shape
    count = micro * images
    return (
        value.reshape(count, pixels // 8, 8, channels).transpose(1, 0, 2, 3).reshape(-1, channels)
    )


def from_rows(value, images):
    count = MICRO * images
    channels = value.shape[-1]
    grid_rows = value.shape[0] // (8 * count)
    planes = value.reshape(grid_rows, count, 8, channels).transpose(1, 0, 2, 3)
    return planes.reshape(MICRO, images, grid_rows * 8, channels)


def noise_columns(pair_ids, columns):
    fraction = pair_ids.astype(F32) / (LEVELS - 1)
    top_root = SIGMA_HIGH ** (1.0 / 7.0)
    bottom_root = SIGMA_LOW ** (1.0 / 7.0)
    sigmas = (top_root + fraction * (bottom_root - top_root)) ** 7
    log_scale = 250.0 * jnp.log(sigmas)
    quarter = EMBED // 4
    kind = columns // quarter
    frequency = jnp.exp(-math.log(10000.0) * (columns % quarter).astype(F32) / quarter)
    angles = jnp.where(kind < 2, log_scale[:, :1], log_scale[:, 1:]) * frequency
    return jnp.where(kind % 2 == 0, jnp.cos(angles), jnp.sin(angles))


def on_device(
    level_input,
    cotangent,
    class_table,
    conv_in,
    conv_out,
    embed_proj,
    skip_proj,
    qkv_proj,
    out_proj,
    gains,
    biases,
    noise_pairs,
    classes,
):
    sections = lax.axis_size("section")
    section_id = lax.axis_index("section")
    shards = lax.axis_size("dp")
    shard_id = lax.axis_index("dp")
    images = level_input.shape[1]
    count = MICRO * images
    octets = 8 * count
    rows = SIDE * octets
    tables = (jnp.asarray(GROUP_OF, BF16), jnp.asarray(GROUP_OF.T, BF16))

    conv_in_full = lax.all_gather(conv_in[0], "dp", axis=0, tiled=True)
    qkv_parts = [qkv_proj[0][:, part * WIDTH : (part + 1) * WIDTH] for part in range(3)]
    rest_full = lax.all_gather(
        jnp.concatenate([conv_out[0], *qkv_parts, out_proj[0], skip_proj[0]], axis=0), "dp", axis=0
    )
    if any((total // shards) % 16 for total in REST.values()):
        offset, whole = 0, []
        for total in REST.values():
            share = total // shards
            whole.append(rest_full[:, offset : offset + share].reshape(total, WIDTH))
            offset += share
        rest_full = jnp.concatenate(whole, axis=0)[None]

    gain_share, bias_share = gains.shape[1], biases.shape[1]
    small = jnp.concatenate(
        [
            gains[0].astype(F32),
            biases[0].astype(F32),
            noise_pairs.reshape(-1).astype(F32),
            classes.reshape(-1).astype(F32),
        ]
    )
    spare = -small.shape[0] % LANE
    every = Doubling(jnp.pad(small, (0, spare))[None], "dp").finish()[:, 0]
    cut = gain_share + bias_share
    params = jnp.concatenate(
        [every[:, :gain_share].reshape(4, WIDTH), every[:, gain_share:cut].reshape(12, WIDTH)],
        axis=0,
    )
    all_images = shards * count
    pair_ids = every[:, cut : cut + 2 * count].reshape(all_images, 2)
    class_ids = every[:, cut + 2 * count : cut + 3 * count].reshape(all_images).astype(jnp.int32)

    slice_width = class_table.shape[1]
    columns = shard_id * slice_width + jnp.arange(slice_width)[None, :]
    onehot = (class_ids[:, None] == jnp.arange(CLASSES)[None, :]).astype(BF16)
    pre = noise_columns(pair_ids, columns) + dot(onehot, class_table)
    embed_b = jax.nn.silu(pre).astype(BF16)
    shares = dot(embed_b, embed_proj[0]).reshape(shards, count, 2 * WIDTH)
    modulation = lax.all_to_all(shares, "dp", 0, 0).sum(axis=0)
    modulation = modulation + params[BIAS + 3 : BIAS + 5].reshape(1, 2 * WIDTH)
    modulation = jnp.repeat(modulation, 8, axis=0)

    level_own, top_own = to_rows(level_input), to_rows(cotangent)
    level_rows = jnp.concatenate(
        [level_own] + [moved(level_own, source, 0) for source in range(1, sections)], axis=0
    )
    top_rows = jnp.concatenate(
        [moved(top_own, source, sections - 1) for source in range(sections - 1)] + [top_own], axis=0
    )

    kept = []
    skips = {}
    hidden = level_rows
    result = None
    for tick in range(sections):
        decoder = tick >= sections // 2
        mirror = sections - 1 - tick
        skipped = skips[tick] if decoder else None
        outs = run_conv_in(decoder, hidden, skipped, conv_in_full, modulation, params, tables)
        conv_one, stat_c, middle, turned_w = outs[:4]
        if decoder:
            stat_h, stat_s, turned_h, turned_s = outs[4:]
        else:
            stat_h, turned_h = outs[4:]
            stat_s, turned_s = None, turned_h
        result, residual, stat_r, attend, project, mixed = run_block(
            decoder, middle, hidden, skipped, rest_full, params, tables
        )
        kept.append(
            {
                "hidden": hidden,
                "skipped": skipped,
                "conv_one": conv_one,
                "stat_h": stat_h,
                "stat_s": stat_s,
                "stat_c": stat_c,
                "stat_r": stat_r,
                "residual": residual,
                "attend": attend,
                "project": project,
                "mixed": mixed,
                "fields": jnp.concatenate(
                    [turned_h, turned_w] if sections == 2 else [turned_h, turned_s, turned_w], axis=0
                ),
            }
        )
        if tick < sections - 1:
            hidden = moved(result, tick, tick + 1)
            if not decoder:
                skips[mirror] = hidden if mirror == tick + 1 else moved(result, tick, mirror)

    def own(values):
        chosen = values[0]
        for tick in range(1, sections):
            chosen = jnp.where(section_id == tick, values[tick], chosen)
        return chosen

    is_decoder = section_id >= sections // 2
    fields = lax.all_gather(own([entry["fields"] for entry in kept]), "dp", axis=0)

    def to_owners(value, source):
        share = rows // sections
        pieces = [value[index * share : (index + 1) * share] for index in range(sections)]
        total = jnp.where(section_id == source, pieces[source], jnp.zeros_like(pieces[source]))
        for target in range(sections):
            if target != source:
                total = total + moved(pieces[target].astype(BF16), source, target).astype(value.dtype)
        return from_rows(total, images)


    grads = [None] * sections
    skip_grads = {}
    grad_out = top_rows
    grad_hidden = None
    products = None
    for tick in reversed(range(sections)):
        decoder = tick >= sections // 2
        mirror = sections - 1 - tick
        entry = kept[tick]
        if not decoder and tick in skip_grads:
            grad_out = grad_out.astype(F32) + skip_grads[tick].astype(F32)
        joined = decoder and mirror == tick - 1
        active = (section_id == tick).astype(jnp.int32).reshape(1)
        top, grad_project, grad_resid, grad_resid_b, sums_attend, products = run_attention_back(
            decoder, shards, grad_out, entry, active, rest_full, params, tables, products
        )
        grad_conv_b, grad_mod, sums_middle = run_middle_back(
            grad_resid_b, entry["conv_one"], entry["stat_c"], modulation, rest_full, params, tables
        )
        grads[tick] = {
            "rows": [
                grad_resid_b,
                grad_conv_b,
                jnp.pad(
                    grad_mod.reshape(count, 8, 2 * WIDTH)[:, 0].reshape(2 * count, WIDTH),
                    ((0, -2 * count % 16), (0, 0)),
                ),
            ],
        }

        def finish_tick(decoder=decoder, joined=joined, entry=entry):
            return run_conv_in_back(
                decoder,
                grad_conv_b,
                entry["hidden"],
                entry["skipped"],
                entry["stat_h"],
                entry["stat_s"],
                grad_resid,
                grad_resid_b,
                conv_in_full,
                rest_full,
                params,
                tables,
                joined,
            )

        sums = sums_attend + sums_middle
        if tick == 0:
            grads[tick]["sums"] = sums
            break
        outs = finish_tick()
        grads[tick]["sums"] = sums + outs[-1]
        if joined:
            grad_out = moved(outs[0], tick, mirror)
        else:
            if decoder:
                skip_grads[mirror] = moved(outs[1].astype(BF16), tick, mirror)
            grad_out = moved(outs[0].astype(BF16), tick, tick - 1)

    def picked(name):
        return own([entry[name] for entry in grads])

    products, fields = together(products, fields)
    small_grads = lax.psum_scatter(products, "dp", scatter_dimension=0, tiled=True)
    affine = jnp.stack([params[GAIN : GAIN + 2].reshape(-1), params[BIAS : BIAS + 2].reshape(-1)], axis=1)

    def cols_of(step):
        return tap_slices(
            fields,
            ring.order(step),
            affine,
            conv_in.shape[1],
            conv_out.shape[1],
            shard_id,
            is_decoder,
            octets,
        )[::-1]

    ring = Ring(own([jnp.concatenate(entry["rows"], axis=0) for entry in grads]), "dp")
    cols, totals = [], (None, None)

    ring.turn()
    ring.spread()
    outs = finish_tick()
    cols.append(cols_of(0))
    ring.values, ring.rows, cols, fields, result, grads[0]["sums"], input_rows = together(
        ring.values, ring.rows, cols, fields, result, grads[0]["sums"] + outs[-1], outs[0]
    )
    sums = picked("sums")
    halves = Halving(
        jnp.concatenate([sums[:4].reshape(shards, gain_share), sums[4:].reshape(shards, bias_share)], axis=1),
        "dp",
    )
    halves.step()
    ring.turn()
    ring.spread()
    ring.share(0)
    cols += [cols_of(1), cols_of(2)]
    ring.values, ring.rows, ring.steps, cols, fields, result, input_rows, halves.value = together(
        ring.values, ring.rows, ring.steps, cols, fields, result, input_rows, halves.value
    )
    halves.step()
    ring.turn()
    ring.spread()
    ring.share(1)
    cols.append(cols_of(3))
    totals = grad_step(*cols[0], ring.steps[0], *totals)
    ring.values, ring.rows, ring.steps, cols, result, input_rows, halves.value, totals = together(
        ring.values, ring.rows, ring.steps, cols, result, input_rows, halves.value, totals
    )
    halves.step()
    level_output = to_owners(result, sections - 1)
    input_grad = to_owners(input_rows, 0)
    ring.spread()
    ring.share(2)
    totals = grad_step(*cols[1], ring.steps[1], *totals)
    ring.rows, ring.steps, cols, halves.value, totals, level_output, input_grad = together(
        ring.rows, ring.steps, cols, halves.value, totals, level_output, input_grad
    )
    halves.step()
    ring.share(3)
    totals = grad_step(*cols[2], ring.steps[2], *totals)
    ring.steps, cols, halves.value, totals = together(ring.steps, cols, halves.value, totals)
    conv_out_grad, conv_in_grad = grad_step(*cols[3], ring.steps[3], *totals)
    summed = halves.finish()
    gains_grad, biases_grad = summed[:gain_share], summed[gain_share:]

    order = jnp.concatenate([ring.order(step) for step in range(4)])
    spot = 2 * rows
    mods = jnp.concatenate(
        [block[spot : spot + 2 * count] for step in ring.steps for block in step], axis=0
    ).reshape(all_images, 2 * WIDTH)

    def in_order(values):
        return jnp.take(values.reshape(shards, count, -1), order, axis=0).reshape(all_images, -1)

    embed_grad = dot_tn(in_order(embed_b), mods)
    grad_embed = dot_nt(mods, embed_proj[0])
    if sections == 2:
        grad_embed = grad_embed + lax.ppermute(grad_embed, "section", [(0, 1), (1, 0)])
    else:
        grad_embed = lax.psum(grad_embed, "section")
    grad_pre = jax.vjp(jax.nn.silu, in_order(pre))[1](grad_embed)[0]
    table_grad = lax.dot_general(
        in_order(onehot).astype(F32),
        grad_pre,
        (((0,), (0,)), ((), ())),
        precision=lax.Precision.HIGHEST,
        preferred_element_type=F32,
    )

    small_grads = small_grads.astype(F32)
    qkv_grad = small_grads[:, : 3 * WIDTH]
    out_grad = small_grads[:, 3 * WIDTH : 4 * WIDTH]
    skip_grad = jnp.concatenate(
        [small_grads[:, 4 * WIDTH : 5 * WIDTH], small_grads[:, 5 * WIDTH :]], axis=0
    )
    return (
        level_output,
        input_grad,
        table_grad,
        conv_in_grad[None],
        conv_out_grad[None],
        embed_grad[None],
        skip_grad[None],
        qkv_grad[None],
        out_grad[None],
        gains_grad[None],
        biases_grad[None],
    )


def solution(mesh):
    placed = (
        P(None, "dp", "section", None),
        P(None, "dp", "section", None),
        P(None, "dp"),
        P("section", "dp", None),
        P("section", "dp", None),
        P("section", "dp", None),
        P("section", "dp", None),
        P("section", "dp", None),
        P("section", "dp", None),
        P("section", "dp"),
        P("section", "dp"),
        P(None, "dp", None),
        P(None, "dp"),
    )
    return jax.shard_map(
        on_device,
        mesh=mesh,
        in_specs=placed,
        out_specs=(
            P(None, "dp", "section", None),
            P(None, "dp", "section", None),
            P(None, "dp"),
            P("section", "dp", None),
            P("section", "dp", None),
            P("section", "dp", None),
            P("section", "dp", None),
            P("section", "dp", None),
            P("section", "dp", None),
            P("section", "dp"),
            P("section", "dp"),
        ),
        check_vma=False,
    )
```

```python
import math
from functools import partial

import jax
import jax.numpy as jnp
import numpy as np
from jax import lax
from jax.experimental import pallas as pl
from jax.experimental.pallas import tpu as pltpu
from jax.sharding import PartitionSpec as P

WIDTH = 768
EMBED = 768
CLASSES = 1000
HEAD_DIM = 64
GROUPS = 32
SIDE = 8
LEVELS = 40
MICRO = 4
PIXELS = 64
TAPS = 9

EPS = 1e-05
SIGMA_LOW = 0.002
SIGMA_HIGH = 80.0

ACTIVE = "active"
ATTEND = "attend"
BEFORE = "before_"
BLOCK = "block_"
COLS_NAME = "cols"
COLS = "cols_"
COLUMNS_W = "columns_w"
CONV_IN = "conv_in"
CONV_ONE = "conv_one"
CONV_OUT = "conv_out"
DP = "dp"
FIELDS = "fields"
GRAD_HIDDEN = "grad_hidden"
GRAD_JOINED = "grad_joined"
GRAD_OUT = "grad_out"
GRAD_RESID = "grad_resid"
GRAD_RESID_B = "grad_resid_b"
GRAD_SKIPPED = "grad_skipped"
HELD = "held_"
HIDDEN = "hidden"
KEY = "key"
MIDDLE = "middle"
MIXED = "mixed"
MODULATION = "modulation"
OUT_NAME = "out"
OUT = "out_"
OUT_SEMS = "out_sems"
PAYLOAD = "payload"
PLANES = "planes"
PRIOR = "prior_"
PRODUCTS = "products"
PROJECT = "project"
QUERY = "query"
RESIDUAL = "residual"
RESULT = "result"
SECTION = "section"
SKIP = "skip"
SKIPPED = "skipped"
SOURCE = "source_"
STAT_C = "stat_c"
STAT_H = "stat_h"
STAT_R = "stat_r"
STAT_S = "stat_s"
SUMS = "sums"
TAKEN = "taken"
TOTAL = "total_"
VALUE = "value"

F32 = jnp.float32
BF16 = jnp.bfloat16
LANE = 128
CHUNKS = WIDTH // LANE
PER_GROUP = WIDTH // GROUPS
GROUP_SHARE = 1.0 / (PER_GROUP * PIXELS)
VMEM_LIMIT = 60 * 2**20

GAIN = 0
BIAS = 4

GROUP_OF = (np.arange(WIDTH)[:, None] // PER_GROUP == np.arange(LANE)[None, :]).astype(np.float32)


def lanes(chunk):
    return pl.ds(chunk * LANE, LANE)


def dot(left, right):
    return jnp.dot(left, right, preferred_element_type=F32)


def dot_nt(left, right):
    return lax.dot_general(left, right, (((1,), (1,)), ((), ())), preferred_element_type=F32)


def dot_tn(left, right):
    return lax.dot_general(left, right, (((0,), (0,)), ((), ())), preferred_element_type=F32)


def octet_sum(values, octets):
    width = values.shape[-1]
    partial_sums = values.reshape(SIDE, octets, width).sum(axis=0).reshape(octets // 8, 8, width)
    totals = jnp.sum(partial_sums, axis=1, keepdims=True)
    return jnp.broadcast_to(totals, partial_sums.shape).reshape(octets, width)


def over_rows(stat):
    octets, width = stat.shape
    return jnp.broadcast_to(stat[None], (SIDE, octets, width)).reshape(SIDE * octets, width)


def in_parts(values):
    first = values.astype(BF16)
    rest = values - first.astype(F32)
    second = rest.astype(BF16)
    third = (rest - second.astype(F32)).astype(BF16)
    return jnp.concatenate([first, second, third], axis=0)


def group_mean(sums, group_of, group_of_t):
    count = sums.shape[0]
    grouped = dot(in_parts(sums), group_of)
    grouped = (grouped[:count] + grouped[count : 2 * count] + grouped[2 * count :]) * GROUP_SHARE
    spread = dot(in_parts(grouped), group_of_t)
    return spread[:count] + spread[count : 2 * count] + spread[2 * count :]


def norm_stats(read, octets, group_of, group_of_t):
    sums = jnp.concatenate([octet_sum(read(c), octets) for c in range(CHUNKS)], axis=1)
    mean = group_mean(sums, group_of, group_of_t)
    squares = []
    for c in range(CHUNKS):
        centered = read(c) - over_rows(mean[:, c * LANE : (c + 1) * LANE])
        squares.append(octet_sum(centered * centered, octets))
    spread = group_mean(jnp.concatenate(squares, axis=1), group_of, group_of_t)
    return mean, lax.rsqrt(spread + EPS)


def normed_chunk(values, stat_ref, c):
    mean = stat_ref[0, :, lanes(c)]
    inv = stat_ref[1, :, lanes(c)]
    return (values - over_rows(mean)) * over_rows(inv)


def sigmoid(values):
    return 1.0 / (1.0 + jnp.exp(-values))


def silu_slope(values):
    gate = sigmoid(values)
    return gate * (1.0 + values * (1.0 - gate))


def put_shifted(planes, base, values, c, octets):
    rows = values.shape[0]
    column = lax.broadcasted_iota(jnp.int32, values.shape, 0) & 7
    before = jnp.where(column != 0, pltpu.roll(values, 1, 0), 0.0)
    after = jnp.where(column != 7, pltpu.roll(values, rows - 1, 0), 0.0)
    planes[base, pl.ds(octets, rows), lanes(c)] = before.astype(BF16)
    planes[base + 1, pl.ds(octets, rows), lanes(c)] = values.astype(BF16)
    planes[base + 2, pl.ds(octets, rows), lanes(c)] = after.astype(BF16)


def clear_edges(planes, octets):
    count, rows, width = planes.shape
    edge = jnp.zeros((count, octets, width), BF16)
    planes[:, pl.ds(0, octets), :] = edge
    planes[:, pl.ds(rows - octets, octets), :] = edge


def row_total(values):
    return jnp.sum(values, axis=0, keepdims=True)


def norm_back(read_grad, read_normed, gain_of, stat_ref, octets, tables, write, sums_out):
    group_of, group_of_t = tables
    first, second = [], []
    for c in range(CHUNKS):
        grad = read_grad(c)
        first.append(octet_sum(grad, octets))
        second.append(octet_sum(grad * read_normed(c), octets))
    first = jnp.concatenate(first, axis=1)
    second = jnp.concatenate(second, axis=1)
    sums_out(first, second)
    gain = gain_of(None)
    both = group_mean(jnp.concatenate([first * gain, second * gain], axis=0), group_of, group_of_t)
    for c in range(CHUNKS):
        part = slice(c * LANE, (c + 1) * LANE)
        inv = over_rows(stat_ref[1, :, lanes(c)])
        mean_one = over_rows(both[:octets, part])
        mean_two = over_rows(both[octets:, part])
        write(c, inv * (gain_of(c) * read_grad(c) - mean_one - read_normed(c) * mean_two))


class Weights:
    def __init__(self, sources, plan, sems):
        self.sources, self.plan, self.sems, self.waits, self.used = sources, plan, sems, {}, 0

    def fetch(self, name, held):
        self.waits[name] = []
        for source, piece, row, target, count in self.plan[name]:
            copy = pltpu.make_async_copy(
                self.sources[source].at[piece, pl.ds(row, count)],
                held.at[pl.ds(target, count)],
                self.sems.at[self.used],
            )
            copy.start()
            self.used += 1
            self.waits[name].append([target, copy])

    def need(self, name, stop):
        for entry in self.waits[name]:
            if entry[0] < stop and entry[1] is not None:
                entry[1].wait()
                entry[1] = None


def copies_of(plan, *names):
    return pltpu.SemaphoreType.DMA((sum(len(plan[name]) for name in names),))


SMALL = (QUERY, KEY, VALUE, OUT_NAME)


def held_at(r, name):
    if name in SMALL[:3]:
        return r.held_qkv.at[SMALL.index(name)]
    return getattr(r, HELD + name)


def held_scratch(decoder, names):
    sizes = {CONV_IN: (1 + decoder) * TAPS * WIDTH, CONV_OUT: TAPS * WIDTH, OUT_NAME: WIDTH, SKIP: 2 * WIDTH}
    scratch = {HELD + name: pltpu.VMEM((sizes[name], WIDTH), BF16) for name in names if name in sizes}
    if QUERY in names:
        scratch["held_qkv"] = pltpu.VMEM((3, WIDTH, WIDTH), BF16)
    return scratch


def head_pair(values, left):
    zero = jnp.zeros_like(values)
    return jnp.concatenate([jnp.where(left, values, zero), jnp.where(left, zero, values)], axis=0)


def attention_of(keys, queries):
    scores = [dot_nt(k, q) * (1.0 / math.sqrt(HEAD_DIM)) for k, q in zip(keys, queries)]
    tops = [jnp.max(part, axis=0, keepdims=True) for part in scores]
    weights = [jnp.exp(part - top) for part, top in zip(scores, tops)]
    totals = [1.0 / jnp.sum(part, axis=0, keepdims=True) for part in weights]
    return [part * total for part, total in zip(weights, totals)]


AT_ONCE = 4


def image_groups(images):
    every = [(image, pl.ds(image * PIXELS, PIXELS), pair) for image in range(images) for pair in range(CHUNKS)]
    return [every[start : start + AT_ONCE * CHUNKS] for start in range(0, len(every), AT_ONCE * CHUNKS)]


def by_image(scratch, image, chunk):
    part = scratch[:, image, :, lanes(chunk)]
    return part.reshape(PIXELS, LANE)


def put_image(scratch, image, chunk, values):
    scratch[:, image, :, lanes(chunk)] = values.reshape(SIDE, 8, LANE)


def conv_in_forward(r, decoder, shared, octets):
    rows = r.hidden.shape[0]
    tables = (r.group_of[...], r.group_of_t[...])
    sides = [(r.hidden, r.stat_h, 0)] + ([(r.skipped, r.stat_s, 1)] if decoder else [])
    span = WIDTH * len(sides)
    clear_edges(r.planes, octets)
    for source, stat, which in sides:
        mean, inv = norm_stats(lambda c: source[:, lanes(c)].astype(F32), octets, *tables)
        stat[0] = mean
        stat[1] = inv
        if shared and not which:
            for index, values in enumerate((mean, 1.0 / inv)):
                grouped = dot(values.astype(BF16), tables[0]) * (1.0 / PER_GROUP)
                r.turned[pl.ds(WIDTH + index * GROUPS, GROUPS), :] = over_rows(grouped).T[:GROUPS].astype(BF16)
        for c in range(CHUNKS):
            normed = normed_chunk(source[:, lanes(c)].astype(F32), stat, c)
            value = (
                normed * r.params[pl.ds(GAIN + which, 1), lanes(c)]
                + r.params[pl.ds(BIAS + which, 1), lanes(c)]
            )
            value = value * sigmoid(value)
            put_shifted(r.planes, 3 * which, value, c, octets)
            if not (shared and which):
                r.turned[pl.ds(which * WIDTH + c * LANE, LANE), :] = normed.T.astype(BF16)
    for tap in range(TAPS):
        r.weights.need(CONV_IN, (tap + 1) * span)
        for half in range(len(sides)):
            part = dot(
                r.planes[3 * half + tap % 3, pl.ds(octets * (tap // 3), rows), :],
                r.held_conv_in[pl.ds(tap * span + half * WIDTH, WIDTH), :],
            )
            if tap == 0 and half == 0:
                r.conv_one[...] = part + r.params[pl.ds(BIAS + 2, 1), :]
            else:
                r.conv_one[...] += part
    r.flush(CONV_ONE)
    mean, inv = norm_stats(lambda c: r.conv_one[:, lanes(c)], octets, *tables)
    r.stat_c[0] = mean
    r.stat_c[1] = inv
    for c in range(CHUNKS):
        normed = (
            normed_chunk(r.conv_one[:, lanes(c)], r.stat_c, c) * r.params[pl.ds(GAIN + 2, 1), lanes(c)]
            + r.params[pl.ds(BIAS + 5, 1), lanes(c)]
        )
        scale = over_rows(r.modulation[:, lanes(c)])
        shift = over_rows(r.modulation[:, lanes(CHUNKS + c)])
        value = normed * (1.0 + scale) + shift
        value = value * sigmoid(value)
        r.middle[:, lanes(c)] = value.astype(BF16)
        r.turned_w[lanes(c), :] = value.T.astype(BF16)
    r.flush(MIDDLE, STAT_C)
    r.leave(r.turned, r.fields, r.fields_sems.at[0])
    r.leave(r.turned_w, r.columns_w, r.fields_sems.at[1])


def block_forward(r, decoder, octets):
    rows = r.hidden.shape[0]
    images = octets // 8
    tables = (r.group_of[...], r.group_of_t[...])
    clear_edges(r.planes, octets)
    for c in range(CHUNKS):
        put_shifted(r.planes, 0, r.middle[:, lanes(c)].astype(F32), c, octets)
    for tap in range(TAPS):
        r.weights.need(CONV_OUT, (tap + 1) * WIDTH)
        part = dot(
            r.planes[tap % 3, pl.ds(octets * (tap // 3), rows), :], r.held_conv_out[pl.ds(tap * WIDTH, WIDTH), :]
        )
        if tap == 0:
            r.residual[...] = part + r.params[pl.ds(BIAS + 6, 1), :]
        else:
            r.residual[...] += part
    if decoder:
        r.weights.need(SKIP, 2 * WIDTH)
        r.residual[...] += (
            dot(r.hidden[...], r.held_skip[pl.ds(0, WIDTH), :])
            + dot(r.skipped[...], r.held_skip[pl.ds(WIDTH, WIDTH), :])
            + r.params[pl.ds(BIAS + 7, 1), :]
        )
    else:
        r.residual[...] += r.hidden[...].astype(F32)
    r.flush(RESIDUAL)
    mean, inv = norm_stats(lambda c: r.residual[:, lanes(c)], octets, *tables)
    r.stat_r[0] = mean
    r.stat_r[1] = inv
    for c in range(CHUNKS):
        r.attend[:, lanes(c)] = (
            normed_chunk(r.residual[:, lanes(c)], r.stat_r, c) * r.params[pl.ds(GAIN + 3, 1), lanes(c)]
            + r.params[pl.ds(BIAS + 8, 1), lanes(c)]
        ).astype(BF16)
    r.flush(ATTEND)
    for index, (name, bias) in enumerate(((QUERY, 9), (KEY, None), (VALUE, 10))):
        r.weights.need(name, WIDTH)
        part = dot(r.attend[...], r.held_qkv[index])
        if bias is not None:
            part = part + r.params[pl.ds(BIAS + bias, 1), :]
        part = part.reshape(SIDE, images, 8, WIDTH)
        for image in range(images):
            own = part[:, image].reshape(PIXELS, WIDTH).astype(BF16)
            r.project[pl.ds(image * PIXELS, PIXELS), pl.ds(index * WIDTH, WIDTH)] = own
    r.flush(PROJECT)
    left = lax.broadcasted_iota(jnp.int32, (PIXELS, LANE), 1) < HEAD_DIM
    for group in image_groups(images):
        queries = [head_pair(r.project[span, lanes(pair)], left) for _, span, pair in group]
        keys_h = [r.project[span, lanes(CHUNKS + pair)] for _, span, pair in group]
        values_h = [r.project[span, lanes(2 * CHUNKS + pair)] for _, span, pair in group]
        attention = [part.astype(BF16) for part in attention_of(keys_h, queries)]
        both = [dot_tn(part, values) for part, values in zip(attention, values_h)]
        for (image, _, pair), part in zip(group, both):
            put_image(r.grid, image, pair, jnp.where(left, part[:PIXELS], part[PIXELS:]))
    r.mixed[...] = r.grid[:, :, :, pl.ds(0, WIDTH)].reshape(rows, WIDTH).astype(BF16)
    r.flush(MIXED)
    r.weights.need(OUT_NAME, WIDTH)
    r.result[...] = (
        r.residual[...] + dot(r.mixed[...], r.held_out[...]) + r.params[pl.ds(BIAS + 11, 1), :]
    ).astype(BF16)


def attention_backward(r, decoder, octets, shards, with_skip):
    rows = r.residual.shape[0]
    images = octets // 8
    tables = (r.group_of[...], r.group_of_t[...])

    def put_sum(row, c, values):
        r.sums[pl.ds(row, 1), lanes(c)] = row_total(values)

    def leave(first, width):
        part = pl.ds(first * WIDTH, width * WIDTH)
        r.leave(r.built.at[:, part], r.products.at[:, part], r.built_sems.at[min(first, 2)])

    top = r.grad_out[...].astype(BF16)
    for c in range(CHUNKS):
        put_sum(BIAS + 11, c, r.grad_out[:, lanes(c)].astype(BF16).astype(F32))
    r.built[:, pl.ds(3 * WIDTH, WIDTH)] = dot_tn(r.mixed[...], top).astype(BF16)
    leave(3, 1)
    r.weights.need(OUT_NAME, WIDTH)
    r.grid[:, :, :, pl.ds(0, WIDTH)] = dot_nt(top, r.held_out[...]).reshape(SIDE, images, 8, WIDTH)
    left = lax.broadcasted_iota(jnp.int32, (PIXELS, LANE), 1) < HEAD_DIM
    root = 1.0 / math.sqrt(HEAD_DIM)
    for group in image_groups(images):
        queries = [head_pair(r.project[span, lanes(pair)], left) for _, span, pair in group]
        keys_h = [r.project[span, lanes(CHUNKS + pair)] for _, span, pair in group]
        values_h = [r.project[span, lanes(2 * CHUNKS + pair)] for _, span, pair in group]
        grads_h = [head_pair(by_image(r.grid, image, pair).astype(BF16), left) for image, _, pair in group]
        attention = attention_of(keys_h, queries)
        weighted = [dot_nt(v, g) * part for v, g, part in zip(values_h, grads_h, attention)]
        totals = [jnp.sum(part, axis=0, keepdims=True) for part in weighted]
        scores = [(w - part * total).astype(BF16) for w, part, total in zip(weighted, attention, totals)]
        both = [dot_tn(part, k) * root for part, k in zip(scores, keys_h)]
        grad_keys = [dot(part, q) * root for part, q in zip(scores, queries)]
        grad_values = [dot(part.astype(BF16), g) for part, g in zip(attention, grads_h)]
        for index, (image, _, pair) in enumerate(group):
            put_image(r.grid, image, pair, jnp.where(left, both[index][:PIXELS], both[index][PIXELS:]))
            put_image(r.grid, image, CHUNKS + pair, grad_keys[index])
            put_image(r.grid, image, 2 * CHUNKS + pair, grad_values[index])
    for index in range(3):
        for pair in range(CHUNKS):
            chunk = lanes(index * CHUNKS + pair)
            joined = r.grid[:, :, :, chunk].reshape(rows, LANE).astype(BF16)
            r.grad_project[:, chunk] = joined
            if index == 0:
                put_sum(BIAS + 9, pair, joined.astype(F32))
            if index == 2:
                put_sum(BIAS + 10, pair, joined.astype(F32))
    for index in range(3):
        columns = pl.ds(index * WIDTH, WIDTH)
        r.built[:, columns] = dot_tn(r.attend[...], r.grad_project[:, columns]).astype(BF16)
    leave(0, 3)
    for index, name in enumerate(SMALL[:3]):
        r.weights.need(name, WIDTH)
        part = dot_nt(r.grad_project[:, pl.ds(index * WIDTH, WIDTH)], r.held_qkv[index])
        if index == 0:
            r.work[...] = part
        else:
            r.work[...] += part

    def gain_attend(c):
        return r.params[pl.ds(GAIN + 3, 1), :] if c is None else r.params[pl.ds(GAIN + 3, 1), lanes(c)]

    def sums_attend(first, second):
        r.sums[pl.ds(BIAS + 8, 1), :] = row_total(first) * 0.125
        r.sums[pl.ds(GAIN + 3, 1), :] = row_total(second) * 0.125

    def write_resid(c, grad):
        total = r.grad_out[:, lanes(c)].astype(F32) + grad
        r.grad_resid[:, lanes(c)] = total
        rounded = total.astype(BF16)
        r.grad_resid_b[:, lanes(c)] = rounded
        rounded = rounded.astype(F32)
        put_sum(BIAS + 6, c, rounded)
        if decoder:
            put_sum(BIAS + 7, c, rounded)

    norm_back(
        lambda c: r.work[:, lanes(c)],
        lambda c: normed_chunk(r.residual[:, lanes(c)], r.stat_r, c),
        gain_attend,
        r.stat_r,
        octets,
        tables,
        write_resid,
        sums_attend,
    )
    r.flush(GRAD_RESID, GRAD_RESID_B)
    if with_skip:
        share = WIDTH // shards
        for side, source in enumerate((r.hidden, r.skipped)):
            first = side * shards // 2
            if decoder:
                part = dot_tn(source[...], r.grad_resid_b[...]).astype(BF16)
            else:
                part = jnp.zeros((WIDTH, WIDTH), BF16)
            for index in range(shards // 2):
                target = pl.ds((first + index) * share, share)
                for half in range(2):
                    r.built[target, pl.ds((4 + half) * WIDTH, WIDTH)] = part[
                        (2 * index + half) * share : (2 * index + half + 1) * share
                    ]
        part = pl.ds(4 * WIDTH, 2 * WIDTH)
        r.leave(r.built.at[:, part], r.products.at[:, part], r.built_sems.at[1])


def middle_backward(r, octets):
    rows = r.conv_one.shape[0]
    tables = (r.group_of[...], r.group_of_t[...])
    clear_edges(r.planes, octets)
    r.rows[pl.ds(0, rows), :] = r.grad_resid_b[...]
    for c in range(CHUNKS):
        put_shifted(r.planes, 0, r.grad_resid_b[:, lanes(c)].astype(F32), c, octets)
    for tap in range(TAPS):
        r.weights.need(CONV_OUT, (tap + 1) * WIDTH)
        part = dot_nt(
            r.planes[2 - tap % 3, pl.ds(octets * (2 - tap // 3), rows), :],
            r.held_conv_out[pl.ds(tap * WIDTH, WIDTH), :],
        )
        if tap == 0:
            r.work[...] = part
        else:
            r.work[...] += part
    for c in range(CHUNKS):
        normed = (
            normed_chunk(r.conv_one[:, lanes(c)], r.stat_c, c) * r.params[pl.ds(GAIN + 2, 1), lanes(c)]
            + r.params[pl.ds(BIAS + 5, 1), lanes(c)]
        )
        scale = over_rows(r.modulation[:, lanes(c)])
        shift = over_rows(r.modulation[:, lanes(CHUNKS + c)])
        r.work[:, lanes(c)] = r.work[:, lanes(c)] * silu_slope(normed * (1.0 + scale) + shift)

    def gain_middle(c):
        if c is None:
            return r.params[pl.ds(GAIN + 2, 1), :] * (1.0 + r.modulation[:, pl.ds(0, WIDTH)])
        return over_rows(r.params[pl.ds(GAIN + 2, 1), lanes(c)] * (1.0 + r.modulation[:, lanes(c)]))

    def sums_middle(first, second):
        scaled = 1.0 + r.modulation[:, pl.ds(0, WIDTH)]
        r.sums[pl.ds(BIAS + 5, 1), :] = row_total(first * scaled) * 0.125
        r.sums[pl.ds(GAIN + 2, 1), :] = row_total(second * scaled) * 0.125
        grad_scale = (
            r.params[pl.ds(GAIN + 2, 1), :] * second + r.params[pl.ds(BIAS + 5, 1), :] * first
        ).astype(BF16)
        grad_shift = first.astype(BF16)
        images = octets // 8
        row = lax.broadcasted_iota(jnp.int32, (16, octets), 0)
        column = lax.broadcasted_iota(jnp.int32, (16, octets), 1)
        for index, part in enumerate((grad_scale, grad_shift)):
            taken = ((row - index * images) * 8 == column) & (row >= index * images)
            chosen = dot(jnp.where(taken, 1.0, 0.0).astype(BF16), part)
            compact = chosen if index == 0 else compact + chosen
        r.rows[pl.ds(2 * rows, 16), :] = compact.astype(BF16)
        r.sums[pl.ds(BIAS + 3, 1), :] = row_total(grad_scale.astype(F32)) * 0.125
        r.sums[pl.ds(BIAS + 4, 1), :] = row_total(grad_shift.astype(F32)) * 0.125

    def write_conv(c, grad):
        rounded = grad.astype(BF16)
        r.grad_conv_b[:, lanes(c)] = rounded
        r.rows[pl.ds(rows, rows), lanes(c)] = rounded
        r.sums[pl.ds(BIAS + 2, 1), lanes(c)] = row_total(rounded.astype(F32))

    norm_back(
        lambda c: r.work[:, lanes(c)],
        lambda c: normed_chunk(r.conv_one[:, lanes(c)], r.stat_c, c),
        gain_middle,
        r.stat_c,
        octets,
        tables,
        write_conv,
        sums_middle,
    )
    r.leave(r.rows, r.payload, r.payload_sem)


def conv_in_backward(r, decoder, joined, octets):
    rows = r.hidden.shape[0]
    tables = (r.group_of[...], r.group_of_t[...])
    sides = [(r.hidden, r.stat_h, r.total if joined else r.grad_hidden, 0)]
    if decoder:
        sides.append((r.skipped, r.stat_s, r.total if joined else r.grad_skipped, 1))
    span = WIDTH * len(sides)
    clear_edges(r.planes, octets)
    for c in range(CHUNKS):
        put_shifted(r.planes, 0, r.grad_conv_b[:, lanes(c)].astype(F32), c, octets)
    for tap in range(TAPS):
        r.weights.need(CONV_IN, (tap + 1) * span)
        for _, _, _, half in sides:
            part = dot_nt(
                r.planes[2 - tap % 3, pl.ds(octets * (2 - tap // 3), rows), :],
                r.held_conv_in[pl.ds(tap * span + half * WIDTH, WIDTH), :],
            )
            if tap == 0:
                r.sides[half] = part
            else:
                r.sides[half] += part
    if decoder:
        r.weights.need(SKIP, 2 * WIDTH)
    for source, stat, target, which in sides:

        def normed_of(c, source=source, stat=stat):
            return normed_chunk(source[:, lanes(c)].astype(F32), stat, c)

        def gain_input(c, which=which):
            row = pl.ds(GAIN + which, 1)
            return r.params[row, :] if c is None else r.params[row, lanes(c)]

        for c in range(CHUNKS):
            value = normed_of(c) * gain_input(c) + r.params[pl.ds(BIAS + which, 1), lanes(c)]
            r.sides[which, :, lanes(c)] = r.sides[which, :, lanes(c)] * silu_slope(value)

        def sums_input(first, second, which=which):
            r.sums[pl.ds(BIAS + which, 1), :] = row_total(first) * 0.125
            r.sums[pl.ds(GAIN + which, 1), :] = row_total(second) * 0.125

        if decoder:
            part = dot_nt(r.grad_resid_b[...], r.held_skip[pl.ds(which * WIDTH, WIDTH), :])
            if joined and which:
                target[...] += part
            else:
                target[...] = part

        def write_input(c, grad, target=target):
            if decoder:
                target[:, lanes(c)] += grad
            else:
                target[:, lanes(c)] = grad + r.grad_resid[:, lanes(c)]

        norm_back(
            lambda c, which=which: r.sides[which, :, lanes(c)],
            normed_of,
            gain_input,
            stat,
            octets,
            tables,
            write_input,
            sums_input,
        )
    if joined:
        r.grad_joined[...] = r.total[...].astype(BF16)


def shape(dims, kind):
    return jax.ShapeDtypeStruct(dims, kind)


IN_VMEM = pl.BlockSpec(memory_space=pltpu.VMEM)
IN_HBM = pl.BlockSpec(memory_space=pl.ANY)
IN_SMEM = pl.BlockSpec(memory_space=pltpu.SMEM)


class Refs:
    def __init__(self, refs, targets):
        self.__dict__.update(refs)
        self._targets, self._leaving = targets, []

    def leave(self, source, target, sem):
        self._leaving.append(pltpu.make_async_copy(source, target, sem))
        self._leaving[-1].start()

    def flush(self, *names):
        for name in names:
            if name in self._targets:
                self.leave(getattr(self, name), *self._targets.pop(name))

    def finish(self):
        self.flush(*list(self._targets))
        for copy in self._leaving:
            copy.wait()


def call(body, name, operands, outputs, scratch, weights=None, order=(), active=None, far=(), flops=0, always=False, light=False):
    sources, plan = weights if weights is not None else ([], {})
    scratch = dict(scratch)
    if order:
        scratch["fetched"] = pltpu.SemaphoreType.DMA((sum(len(plan[part]) for part in order),))
    ins = [key for key in operands if key not in far and not key.startswith(BEFORE)]
    outs = [key for key in outputs if key not in far]
    for key in outs:
        scratch[OUT + key] = pltpu.VMEM(outputs[key].shape, outputs[key].dtype)
    scratch[OUT_SEMS] = pltpu.SemaphoreType.DMA((max(len(outs), 1),))
    names = [*operands, *(SOURCE + str(index) for index in range(len(sources)))]
    names += ([ACTIVE] if active is not None else []) + [*outputs, *scratch]
    moved = sum(int(np.prod(v.shape)) * v.dtype.itemsize for v in (*operands.values(), *outputs.values()))

    def kernel(*refs):
        refs = dict(zip(names, refs))

        def run():
            targets = {}
            for index, key in enumerate(outs):
                targets[key] = (refs[key], refs[OUT_SEMS].at[index])
                refs[key] = refs[OUT + key]
            r = Refs(refs, targets)
            if order:
                r.weights = Weights([getattr(r, SOURCE + str(index)) for index in range(len(sources))], plan, r.fetched)
                for part in order:
                    r.weights.fetch(part, held_at(r, part))
            if SUMS in outputs:
                r.sums[...] = jnp.zeros(r.sums.shape, F32)
            body(r)
            r.finish()

        if active is None or always:
            run()
        else:
            pl.when(refs[ACTIVE][0] == 1)(run)

    keys = list(operands)
    results = pl.pallas_call(
        kernel,
        out_shape=list(outputs.values()),
        in_specs=[IN_VMEM if key in ins else IN_HBM for key in keys] + [IN_HBM] * len(sources) + ([IN_SMEM] if active is not None else []),
        out_specs=[IN_HBM] * len(outputs),
        scratch_shapes=list(scratch.values()),
        input_output_aliases={
            index: list(outputs).index(key[len(BEFORE) :])
            for index, key in enumerate(keys)
            if key.startswith(BEFORE)
        },
        compiler_params=pltpu.CompilerParams(vmem_limit_bytes=VMEM_LIMIT),
        cost_estimate=pl.CostEstimate(
            flops=flops // 4 if light else flops, bytes_accessed=moved // 4 if light else moved, transcendentals=0
        ),
        name=name,
    )(*operands.values(), *sources, *([active] if active is not None else []))
    return dict(zip(outputs, results))


def field(rows, kind=BF16, width=WIDTH):
    return shape((rows, width), kind)


def planes_scratch(sides, rows):
    return pltpu.VMEM((3 * sides, rows + 2 * rows // SIDE, WIDTH), BF16)


def run_forward(decoder, shared, hidden, skipped, weights_for, modulation, common, before, active):
    rows = hidden.shape[0]
    octets = rows // SIDE
    inputs = {HIDDEN: hidden, **({SKIPPED: skipped} if decoder else {}), **common}
    inputs.update(before)
    stat = shape((2, octets, WIDTH), F32)
    first_out = {
        CONV_ONE: field(rows, F32),
        STAT_C: stat,
        FIELDS: field(WIDTH + (2 * GROUPS if shared else WIDTH), width=rows),
        COLUMNS_W: field(WIDTH, width=rows),
        STAT_H: stat,
        **({STAT_S: stat} if decoder else {}),
    }
    first_scratch = {
        "turned": pltpu.VMEM(first_out[FIELDS].shape, BF16),
        "turned_w": pltpu.VMEM((WIDTH, rows), BF16),
        "fields_sems": pltpu.SemaphoreType.DMA((2,)),
        PLANES: planes_scratch(1 + decoder, rows),
        **held_scratch(decoder, (CONV_IN,)),
    }
    second_names = (CONV_OUT, *((SKIP,) if decoder else ()), *SMALL)
    second_out = {
        RESULT: field(rows),
        RESIDUAL: field(rows, F32),
        STAT_R: stat,
        ATTEND: field(rows),
        PROJECT: field(rows, width=3 * WIDTH),
        MIXED: field(rows),
    }
    second_scratch = {
        "grid": pltpu.VMEM((SIDE, octets // 8, 8, WIDTH), F32),
        PLANES: planes_scratch(1, rows),
        **held_scratch(decoder, second_names),
    }
    first_flops = 2 * rows * (1 + decoder) * TAPS * WIDTH * WIDTH
    second_flops = 2 * rows * (TAPS + 6) * WIDTH * WIDTH

    def first_body(r):
        conv_in_forward(r, decoder, shared, octets)

    def second_body(r):
        block_forward(r, decoder, octets)

    def both(r):
        first_body(r)
        second_body(r)

    if not decoder:
        names = (CONV_IN, *second_names)
        return call(
            both,
            "encoder_forward",
            {**inputs, MODULATION: modulation},
            {**first_out, **second_out},
            {**second_scratch, **first_scratch, MIDDLE: pltpu.VMEM((rows, WIDTH), BF16)},
            weights_for(decoder, *names),
            names,
            active,
            (FIELDS, COLUMNS_W),
            first_flops + second_flops,
        )
    first = call(
        first_body,
        "conv_in_forward",
        {**inputs, MODULATION: modulation},
        {**first_out, MIDDLE: field(rows)},
        first_scratch,
        weights_for(decoder, CONV_IN),
        (CONV_IN,),
        active,
        (FIELDS, COLUMNS_W),
        first_flops,
    )
    second = call(
        second_body,
        "block_forward",
        {HIDDEN: hidden, SKIPPED: skipped, MIDDLE: first[MIDDLE], **common},
        second_out,
        second_scratch,
        weights_for(decoder, *second_names),
        second_names,
        active,
        (),
        second_flops,
    )
    return {**first, **second}


def run_backward(decoder, joined, shards, with_skip, part, entry, weights_for, modulation, common, before, active):
    rows = entry[HIDDEN].shape[0]
    octets = rows // SIDE
    first, second = part in (0, None), part in (1, None)
    inputs, names = {}, ()
    if first:
        names += (OUT_NAME, *SMALL[:3], CONV_OUT)
        used = [GRAD_OUT, PROJECT, RESIDUAL, STAT_R, ATTEND, MIXED, CONV_ONE, STAT_C]
        inputs.update({name: entry[name] for name in used}, modulation=modulation, **before)
    if second:
        names += (CONV_IN, *((SKIP,) if decoder else ()))
    if second or with_skip:
        inputs[HIDDEN] = entry[HIDDEN]
        if decoder or with_skip:
            inputs[SKIPPED] = entry[SKIPPED]
    if second:
        inputs[STAT_H] = entry[STAT_H]
        if decoder:
            inputs[STAT_S] = entry[STAT_S]
    between = {GRAD_RESID: field(rows, F32), GRAD_RESID_B: field(rows), "grad_conv_b": field(rows)}
    outputs = {SUMS: field(16, F32)}
    scratch = {PLANES: planes_scratch(1, rows), **held_scratch(decoder, names)}
    if first:
        outputs[PRODUCTS] = field(WIDTH, width=(6 if with_skip else 4) * WIDTH)
        outputs[PAYLOAD] = field(2 * rows + 16)
        scratch.update(
            grid=pltpu.VMEM((SIDE, octets // 8, 8, 3 * WIDTH), F32),
            grad_project=pltpu.VMEM((rows, 3 * WIDTH), BF16),
            built=pltpu.VMEM(outputs[PRODUCTS].shape, BF16),
            built_sems=pltpu.SemaphoreType.DMA((3,)),
            rows=pltpu.VMEM(outputs[PAYLOAD].shape, BF16),
            payload_sem=pltpu.SemaphoreType.DMA,
        )
    if part == 0:
        outputs.update(between)
    elif part == 1:
        inputs.update({name: entry[name] for name in between if decoder or name != GRAD_RESID_B})
    else:
        scratch.update({name: pltpu.VMEM(value.shape, value.dtype) for name, value in between.items()})
    scratch["sides"] = pltpu.VMEM((1 + (decoder and second), rows, WIDTH), F32)
    if second:
        if joined:
            outputs[GRAD_JOINED] = field(rows)
            scratch["total"] = pltpu.VMEM((rows, WIDTH), F32)
        else:
            outputs[GRAD_HIDDEN] = field(rows, F32)
            if decoder:
                outputs[GRAD_SKIPPED] = field(rows, F32)

    def body(r):
        r.work = r.sides.at[0]
        if first:
            attention_backward(r, decoder, octets, shards, with_skip)
            middle_backward(r, octets)
        if second:
            conv_in_backward(r, decoder, joined, octets)

    return call(
        body,
        "section_backward" if part is None else ("block_backward", "conv_in_backward")[part],
        {**inputs, **common},
        outputs,
        scratch,
        weights_for(decoder, *names),
        names,
        active,
        (PRODUCTS, PAYLOAD),
        2 * rows * (first * (TAPS + 14) + second * (1 + decoder) * TAPS) * WIDTH * WIDTH,
    )


def tap_at(place, index, rows, channels):
    block = rows // TAPS
    per_tap = channels // block
    position = place * TAPS + index
    tap = lax.div(position, per_tap)
    start = pl.multiple_of(lax.rem(position, per_tap) * block, 16)
    return lax.div(tap, 3) - 1, lax.rem(tap, 3) - 1, start, block


def shifted_field(values, down, across, octets, also=None):
    width = values.shape[1]
    lane = lax.broadcasted_iota(jnp.int32, (1, width), 1)
    row, column = lax.div(lane, octets) + down, (lane & 7) + across
    inside = (row >= 0) & (row < SIDE) & (column >= 0) & (column < 8)
    if also is not None:
        inside = inside & also(lane)
    back = lax.rem(width - (octets * down + across), width)
    return jnp.where(inside, pltpu.roll(values, back, 1), 0.0).astype(BF16)


def columns_in_kernel(octets, shared, place, order, fields, affine, cols_in, *cols_skip):
    width = fields.shape[2]
    rows = cols_in.shape[0]
    for index in range(TAPS):
        down, across, start, block = tap_at(place[0], index, rows, 2 * WIDTH)
        side = lax.div(start, WIDTH)
        spot = pl.multiple_of(start - side * WIDTH if shared else start, 16)
        values = fields[0, pl.ds(spot, block), :].astype(F32)
        values = values * affine[pl.ds(start, block), 0:1] + affine[pl.ds(start, block), 1:2]
        values = values * sigmoid(values)
        kept = lax.mul(side, 1 - place[1]) * width
        cols_in[pl.ds(index * block, block), :] = shifted_field(
            values, down, across, octets, lambda lane: lane >= kept
        )
    if shared:
        rows = cols_skip[0].shape[0]
        start = pl.multiple_of(lax.rem(place[0] * rows, WIDTH), 16)
        channel = lax.broadcasted_iota(jnp.int32, (rows, GROUPS), 0) + start
        group = lax.broadcasted_iota(jnp.int32, (rows, GROUPS), 1) * PER_GROUP
        member = jnp.where((channel >= group) & (channel < group + PER_GROUP), 1.0, 0.0).astype(BF16)
        mean = dot(member, fields[0, pl.ds(WIDTH, GROUPS), :])
        deviation = dot(member, fields[0, pl.ds(WIDTH + GROUPS, GROUPS), :])
        values = fields[0, pl.ds(start, rows), :].astype(F32) * deviation + mean
        lane = lax.broadcasted_iota(jnp.int32, (1, width), 1)
        cols_skip[0][...] = jnp.where(lane < place[1] * width, values, 0.0).astype(BF16)


def tap_slices_plain(fields, rows, channels, place, octets):
    pieces, _, width = fields.shape
    spots = place * rows + jnp.arange(rows)
    taps = spots // channels
    values = jnp.take(fields, spots % channels, axis=1)
    lane = jnp.arange(width)
    total = jnp.zeros_like(values)
    for tap in range(TAPS):
        down, across = tap // 3 - 1, tap % 3 - 1
        row, column = lane // octets + down, lane % 8 + across
        inside = (row >= 0) & (row < SIDE) & (column >= 0) & (column < 8)
        moved = jnp.roll(values, -(octets * down + across), axis=2)
        total = jnp.where((taps == tap)[None, :, None] & inside, moved, total)
    return total.transpose(1, 0, 2).reshape(rows, pieces * width)


def columns_in(fields, order, affine, rows_in, rows_skip, place, decoder, octets, shared):
    _, height, width = fields.shape
    pieces = order.shape[0]
    if not shared and rows_in % (TAPS * 16):
        fields = jnp.take(fields, order, axis=0)
        sides = fields.astype(F32) * affine[:, :1] + affine[:, 1:]
        keep = (jnp.arange(2 * WIDTH)[:, None] < WIDTH) | decoder
        sides = jnp.where(keep, jax.nn.silu(sides), 0.0).astype(BF16)
        return [tap_slices_plain(sides, rows_in, 2 * WIDTH, place, octets)]
    heights = (rows_in, rows_skip) if shared else (rows_in,)
    return pl.pallas_call(
        partial(columns_in_kernel, octets, shared),
        grid_spec=pltpu.PrefetchScalarGridSpec(
            num_scalar_prefetch=2,
            grid=(pieces,),
            in_specs=[
                pl.BlockSpec((1, height, width), lambda piece, place, order: (order[piece], 0, 0)),
                pl.BlockSpec((2 * WIDTH, 2), lambda piece, place, order: (0, 0)),
            ],
            out_specs=[pl.BlockSpec((rows, width), lambda piece, place, order: (0, piece)) for rows in heights],
        ),
        out_shape=[shape((rows, pieces * width), BF16) for rows in heights],
        compiler_params=pltpu.CompilerParams(vmem_limit_bytes=VMEM_LIMIT),
        cost_estimate=pl.CostEstimate(
            flops=0, bytes_accessed=pieces * height * width, transcendentals=0
        ),
        name="columns_in",
    )(jnp.stack([place, decoder.astype(jnp.int32)]).astype(jnp.int32), order, fields, affine)


def columns_out(blocks, rows, place, octets):
    fields = [
        (number, first) for number, block in enumerate(blocks) for first in range(0, block.shape[0], WIDTH)
    ]
    if rows % (TAPS * 16):
        taken = jnp.stack([blocks[number][first : first + WIDTH] for number, first in fields])
        return tap_slices_plain(taken, rows, WIDTH, place, octets)
    width = blocks[0].shape[1]

    def body(r):
        for index in range(TAPS):
            down, across, start, block = tap_at(r.active[0], index, rows, WIDTH)
            for column, (number, first) in enumerate(fields):
                values = getattr(r, BLOCK + str(number))[pl.ds(start + first, block), :].astype(F32)
                r.cols[pl.ds(index * block, block), pl.ds(column * width, width)] = shifted_field(
                    values, down, across, octets
                )

    operands = {BLOCK + str(number): block for number, block in enumerate(blocks)}
    return call(
        body,
        "columns_out",
        operands,
        {COLS_NAME: field(rows, width=len(fields) * width)},
        {},
        active=place.reshape(1).astype(jnp.int32),
        always=True,
        light=True,
    )[COLS_NAME]


def grad_step(cols, blocks, totals):
    sides = len(cols[0])
    count = len(blocks) // len(cols)
    depth = cols[0][0].shape[1] // count

    def body(r):
        for side, part in enumerate(cols[0]):
            target = getattr(r, TOTAL + str(side))
            rows = part.shape[0]
            tile = rows // 3 if rows % 48 == 0 and rows > 128 else rows
            for start in range(0, rows, tile):
                total = getattr(r, PRIOR + str(side))[pl.ds(start, tile), :] if totals else None
                for number in range(len(blocks)):
                    factor = getattr(r, COLS + str(number // count * sides + side))
                    product = dot(
                        factor[pl.ds(start, tile), pl.ds(number % count * depth, depth)],
                        getattr(r, BLOCK + str(number))[pl.ds(depth if side == 1 else 0, depth), :],
                    )
                    total = product if total is None else total + product
                target[pl.ds(start, tile), :] = total
            r.flush(TOTAL + str(side))

    every = [part for step in cols for part in step]
    operands = {COLS + str(index): part for index, part in enumerate(every)}
    operands.update({BLOCK + str(number): block for number, block in enumerate(blocks)})
    if totals:
        operands.update({PRIOR + str(side): total for side, total in enumerate(totals)})
    outputs = {TOTAL + str(side): field(part.shape[0], F32) for side, part in enumerate(cols[0])}
    flops = 2 * sum(part.shape[0] * part.shape[1] for part in every) * WIDTH
    return list(call(body, "grad_step", operands, outputs, {}, flops=flops, light=True).values())


def last_rows(blocks, first):
    def body(r):
        copies = [
            pltpu.make_async_copy(
                getattr(r, BLOCK + str(index)).at[pl.ds(first, r.taken.shape[1])], r.landed.at[index], r.sems.at[index]
            )
            for index in range(len(blocks))
        ]
        for copy in copies:
            copy.start()
        for copy in copies:
            copy.wait()
        r.taken[...] = r.landed[...]

    operands = {BLOCK + str(index): block for index, block in enumerate(blocks)}
    taken = shape((len(blocks), blocks[0].shape[0] - first, blocks[0].shape[1]), blocks[0].dtype)
    scratch = {"sems": pltpu.SemaphoreType.DMA((len(blocks),)), "landed": pltpu.VMEM(taken.shape, taken.dtype)}
    return call(body, "last_rows", operands, {TAKEN: taken}, scratch, far=operands)[TAKEN]


class Doubling:
    def __init__(self, value, axis):
        self.axis, self.value, self.distance = axis, value[None], 1

    def step(self):
        count, index = lax.axis_size(self.axis), lax.axis_index(self.axis)
        if self.distance < count:
            pairs = [(i, i ^ self.distance) for i in range(count)]
            other = lax.ppermute(self.value, self.axis, pairs)
            self.value = jnp.where(
                (index // self.distance) % 2 == 0,
                jnp.concatenate([self.value, other], axis=0),
                jnp.concatenate([other, self.value], axis=0),
            )
            self.distance *= 2

    def finish(self):
        while self.distance < lax.axis_size(self.axis):
            self.step()
        return self.value


class Ring:
    def __init__(self, value, axis):
        self.axis = axis
        self.count = lax.axis_size(axis)
        self.stride = self.count // 4
        self.values, self.rows, self.steps = [value], [], []

    def send(self, value, target):
        return lax.ppermute(value, self.axis, [(i, target(i)) for i in range(self.count)])

    def around(self, value, steps=1):
        return self.send(value, lambda i: (i + steps * self.stride) % self.count)

    def besides(self, value):
        row, stride = [value], self.stride
        for _ in range(stride // 2 - 1):
            row.append(self.send(row[-1], lambda i: i // stride * stride + (i + 2) % stride))
        return row

    def with_core(self, row):
        return row + [self.send(part, lambda i: i ^ 1) for part in row]

    def turn(self):
        self.values.append(self.around(self.values[-1]))

    def spread(self):
        self.rows.append(self.besides(self.values[len(self.rows)]))

    def spread_last(self):
        stride, half = self.stride, self.values[3].shape[0] // 32 * 16
        row = [self.values[3]]
        for index in range(1, stride // 2):
            beside = self.send(row[-1][:half], lambda i: i // stride * stride + (i + 2) % stride)
            turned = self.around(self.rows[2][index][half:])
            row.append(jnp.concatenate([beside, turned], axis=0))
        self.rows.append(row)

    def share(self, step):
        self.steps.append(self.with_core(self.rows[step]))


def ring_order(axis, step):
    index, stride = lax.axis_index(axis), lax.axis_size(axis) // 4
    quarter = (index // stride + 4 - step) % 4 * stride
    sources = []
    for core in range(2):
        for beside in range(stride // 2):
            sources.append(quarter + (index % stride + stride - 2 * beside) % stride // 2 * 2 + (index + core) % 2)
    return jnp.stack(sources).astype(jnp.int32)


def together(*values):
    return lax.optimization_barrier(values)


def moved(value, source, target):
    return lax.ppermute(value, SECTION, [(source, target)])


def to_rows(value):
    micro, images, pixels, channels = value.shape
    count = micro * images
    return (
        value.reshape(count, pixels // 8, 8, channels).transpose(1, 0, 2, 3).reshape(-1, channels)
    )


def from_rows(value, images):
    count = MICRO * images
    channels = value.shape[-1]
    grid_rows = value.shape[0] // (8 * count)
    planes = value.reshape(grid_rows, count, 8, channels).transpose(1, 0, 2, 3)
    return planes.reshape(MICRO, images, grid_rows * 8, channels)


def noise_columns(pair_ids, columns):
    fraction = pair_ids.astype(F32) / (LEVELS - 1)
    top_root = SIGMA_HIGH ** (1.0 / 7.0)
    bottom_root = SIGMA_LOW ** (1.0 / 7.0)
    sigmas = (top_root + fraction * (bottom_root - top_root)) ** 7
    log_scale = 250.0 * jnp.log(sigmas)
    quarter = EMBED // 4
    kind = columns // quarter
    frequency = jnp.exp(-math.log(10000.0) * (columns % quarter).astype(F32) / quarter)
    angles = jnp.where(kind < 2, log_scale[:, :1], log_scale[:, 1:]) * frequency
    return jnp.where(kind % 2 == 0, jnp.cos(angles), jnp.sin(angles))


def block_homes(shards, rows_in):
    block = rows_in // TAPS
    per_tap = 2 * WIDTH // block
    mine = [[i for i in range(TAPS) if (TAPS * d + i) % per_tap < per_tap // 2] for d in range(shards)]
    slots = max(-(-(len(mine[d]) + len(mine[d ^ 1])) // 2) for d in range(shards))
    sent = [mine[d][slots:] for d in range(shards)]
    most = max(1, max(len(part) for part in sent))
    offers, names = [], []
    for d in range(shards):
        kept = mine[d][:slots]
        offer = kept + [TAPS + i for i in range(len(sent[d ^ 1]))]
        names.append([TAPS * d + i for i in kept] + [TAPS * (d ^ 1) + i for i in sent[d ^ 1]])
        offers.append(offer + [0] * (slots - len(offer)))
    sends = [part + [0] * (most - len(part)) for part in sent]
    return np.array(sends, np.int32), np.array(offers, np.int32), names, slots


def spans(name_rows, cuts):
    found, start = {}, 0
    for name, count in name_rows:
        found[name], first, base = [], 0, 0
        for array, height in enumerate(cuts):
            low, high = max(start, base), min(start + count, base + height)
            if low < high:
                found[name].append((array, low - base, low - start, high - low))
            base += height
        start += count
    return found


def section_weights(conv_in, conv_out, skip_proj, qkv_proj, out_proj, is_decoder):
    shards, me = lax.axis_size(DP), lax.axis_index(DP)
    qkv_parts = [qkv_proj[:, part * WIDTH : (part + 1) * WIDTH] for part in range(3)]
    small = dict(zip(SMALL, (*qkv_parts, out_proj)))
    shares = {CONV_IN: conv_in, CONV_OUT: conv_out, **small, SKIP: skip_proj}
    heights = [(name, part.shape[0]) for name, part in shares.items()]
    if any(height % 16 for _, height in heights) or conv_in.shape[0] % (TAPS * 16):
        whole = {name: lax.all_gather(part, DP, axis=0, tiled=True)[None] for name, part in shares.items()}
        sources = list(whole.values())
        plan = {name: [(index, 0, 0, 0, part.shape[1])] for index, (name, part) in enumerate(whole.items())}
        encoder_plan = dict(plan)
        encoder_plan[CONV_IN] = [(0, 0, tap * 2 * WIDTH, tap * WIDTH, WIDTH) for tap in range(TAPS)]
        return sources, encoder_plan, plan
    sends, offers, names, slots = block_homes(shards, conv_in.shape[0])
    blocks = conv_in.reshape(TAPS, -1, WIDTH)
    block = blocks.shape[1]
    other = lax.ppermute(
        jnp.take(blocks, jnp.asarray(sends)[me], axis=0), DP, [(i, i ^ 1) for i in range(shards)]
    )
    chosen = jnp.take(jnp.concatenate([blocks, other], axis=0), jnp.asarray(offers)[me], axis=0)
    encoder_parts = [chosen.reshape(slots * block, WIDTH), conv_out, *small.values()]
    encoder_rows = sum(part.shape[0] for part in encoder_parts)
    first_rows = max(encoder_rows, sum(height for name, height in heights if name not in (OUT_NAME, SKIP)))
    everything = jnp.concatenate(list(shares.values()), axis=0)
    encoder_parts.append(jnp.zeros((first_rows - encoder_rows, WIDTH), BF16))
    first = lax.all_gather(
        jnp.where(is_decoder, everything[:first_rows], jnp.concatenate(encoder_parts, axis=0)), DP, axis=0
    )
    second = lax.all_gather(everything[first_rows:], DP, axis=0)

    def plan_of(found):
        return {
            name: [
                (array, piece, row, piece * height + start, count)
                for piece in range(shards)
                for array, row, start, count in found[name]
            ]
            for name, height in heights
            if name in found
        }

    decoder_plan = plan_of(spans(heights, (first_rows, everything.shape[0] - first_rows)))
    encoder_plan = plan_of(
        spans([("blocks", slots * block)] + [item for item in heights if item[0] in (CONV_OUT, *SMALL)], (encoder_rows,))
    )
    per_tap = 2 * WIDTH // block
    encoder_plan[CONV_IN] = sorted(
        (
            (0, piece, slot * block, name // per_tap * WIDTH + name % per_tap * block, block)
            for piece in range(shards)
            for slot, name in enumerate(names[piece])
        ),
        key=lambda entry: entry[3],
    )
    return [first, second], encoder_plan, decoder_plan


def on_device(
    level_input,
    cotangent,
    class_table,
    conv_in,
    conv_out,
    embed_proj,
    skip_proj,
    qkv_proj,
    out_proj,
    gains,
    biases,
    noise_pairs,
    classes,
):
    sections = lax.axis_size(SECTION)
    section_id = lax.axis_index(SECTION)
    shards = lax.axis_size(DP)
    shard_id = lax.axis_index(DP)
    images = level_input.shape[1]
    count = MICRO * images
    octets = 8 * count
    rows = SIDE * octets

    is_decoder = section_id >= sections // 2
    skip_by_columns = sections == 2
    sources, encoder_plan, decoder_plan = section_weights(
        conv_in[0], conv_out[0], skip_proj[0], qkv_proj[0], out_proj[0], is_decoder
    )

    gain_share, bias_share = gains.shape[1], biases.shape[1]
    small = jnp.concatenate(
        [
            gains[0].astype(F32),
            biases[0].astype(F32),
            noise_pairs.reshape(-1).astype(F32),
            classes.reshape(-1).astype(F32),
        ]
    )
    spare = -small.shape[0] % LANE
    every = Doubling(jnp.pad(small, (0, spare))[None], DP).finish()[:, 0]
    cut = gain_share + bias_share
    params = jnp.concatenate(
        [every[:, :gain_share].reshape(4, WIDTH), every[:, gain_share:cut].reshape(12, WIDTH)],
        axis=0,
    )
    all_images = shards * count
    pair_ids = every[:, cut : cut + 2 * count].reshape(all_images, 2)
    class_ids = every[:, cut + 2 * count : cut + 3 * count].reshape(all_images).astype(jnp.int32)

    slice_width = class_table.shape[1]
    columns = shard_id * slice_width + jnp.arange(slice_width)[None, :]
    onehot = (class_ids[:, None] == jnp.arange(CLASSES)[None, :]).astype(BF16)
    pre = noise_columns(pair_ids, columns) + dot(onehot, class_table)
    embed_b = jax.nn.silu(pre).astype(BF16)
    shares = dot(embed_b, embed_proj[0]).astype(BF16).reshape(shards, count, 2 * WIDTH)
    modulation = lax.all_to_all(shares, DP, 0, 0).astype(F32).sum(axis=0)
    modulation = modulation + params[BIAS + 3 : BIAS + 5].reshape(1, 2 * WIDTH)
    modulation = jnp.repeat(modulation, 8, axis=0)

    level_own, top_own = to_rows(level_input), to_rows(cotangent)
    level_rows = jnp.concatenate(
        [level_own] + [moved(level_own, source, 0) for source in range(1, sections)], axis=0
    )
    top_rows = jnp.concatenate(
        [moved(top_own, source, sections - 1) for source in range(sections - 1)] + [top_own], axis=0
    )

    orders = [ring_order(DP, step) for step in range(4)]
    order = jnp.concatenate(orders)

    def in_order(values):
        return jnp.take(values.reshape(shards, count, -1), order, axis=0).reshape(all_images, -1)

    common = {
        "params": params,
        "group_of": jnp.asarray(GROUP_OF, BF16),
        "group_of_t": jnp.asarray(GROUP_OF.T, BF16),
    }
    level_rows, top_rows, modulation, embed_late, pre_late, onehot_late = together(
        level_rows, top_rows, modulation, in_order(embed_b), in_order(pre), in_order(onehot)
    )

    def weights_for(decoder, *names):
        plan = decoder_plan if decoder else encoder_plan
        used = sorted({entry[0] for name in names for entry in plan[name]})
        return [sources[index] for index in used], {
            name: [(used.index(entry[0]), *entry[1:]) for entry in plan[name]] for name in names
        }

    kept = []
    skips = {}
    hidden = level_rows
    result = None
    before = {}
    for tick in range(sections):
        decoder = tick >= sections // 2
        mirror = sections - 1 - tick
        active = (section_id == tick).astype(jnp.int32).reshape(1)
        skipped = skips[tick] if decoder else hidden
        outs = run_forward(
            decoder, sections == 2, hidden, skipped, weights_for, modulation, common, before, active
        )
        before = {"before_fields": outs[FIELDS], "before_columns_w": outs[COLUMNS_W]}
        result = outs[RESULT]
        entry = {HIDDEN: hidden, SKIPPED: skipped, STAT_S: outs[STAT_H], **outs}
        for name in (FIELDS, COLUMNS_W, RESULT, MIDDLE):
            entry.pop(name, None)
        if sections > 2 and kept:
            entry = {name: jnp.where(section_id == tick, value, kept[-1][name]) for name, value in entry.items()}
            kept = [entry] * (tick + 1)
        else:
            kept.append(entry)
        if tick < sections - 1:
            hidden = moved(result, tick, tick + 1)
            if not decoder:
                skips[mirror] = hidden if mirror == tick + 1 else moved(result, tick, mirror)

    def own(values):
        if sections > 2 and values[0] is values[-1]:
            return values[0]
        chosen = values[0]
        for tick in range(1, sections):
            chosen = jnp.where(section_id == tick, values[tick], chosen)
        return chosen

    fields = lax.all_gather(outs[FIELDS], DP, axis=0)
    circle = Ring(outs[COLUMNS_W], DP)
    turned = {0: outs[COLUMNS_W]}
    w_rows, w_steps = {}, {}

    def beside(stage, *values):
        if stage == 0:
            turned.update({step % 4: circle.around(turned[0], step) for step in (1, -1)})
            w_rows[0] = circle.besides(turned[0])
        if stage == 1:
            turned[2] = circle.around(turned[1])
            w_rows.update({step: circle.besides(turned[step]) for step in (1, 3)})
        if stage == 2:
            w_rows[2] = circle.besides(turned[2])
        for step in ((), (0,), (1, 3), (2,))[stage]:
            other = circle.send(jnp.concatenate(w_rows[step], axis=0), lambda i: i ^ 1)
            w_steps[step] = [*w_rows[step], other]
        state, *values = together((turned, w_rows, w_steps), *values)
        for old, new in zip((turned, w_rows, w_steps), state):
            old.update(new)
        return values

    def to_owners(value, source):
        share = rows // sections
        pieces = [value[index * share : (index + 1) * share] for index in range(sections)]
        total = jnp.where(section_id == source, pieces[source], jnp.zeros_like(pieces[source]))
        for target in range(sections):
            if target != source:
                total = total + moved(pieces[target].astype(BF16), source, target).astype(value.dtype)
        return from_rows(total, images)


    sums_of = [None] * sections
    skip_grads = {}
    grad_out = top_rows
    before = {}
    for tick in reversed(range(sections)):
        decoder = tick >= sections // 2
        mirror = sections - 1 - tick
        entry = kept[tick]
        if not decoder and tick in skip_grads:
            grad_out = grad_out.astype(F32) + skip_grads[tick].astype(F32)
        joined = decoder and mirror == tick - 1
        active = (section_id == tick).astype(jnp.int32).reshape(1)

        def backward(part, entry, decoder=decoder, joined=joined, active=active):
            return run_backward(
                decoder, joined, shards, not skip_by_columns, part, entry, weights_for, modulation, common, before, active
            )

        outs = backward(0 if tick == 0 else None, {**entry, GRAD_OUT: grad_out})
        if tick == sections - 1:
            level_output = to_owners(result, sections - 1)
            outs, level_output = beside(0, outs, level_output)
        if tick == 0:
            (outs,) = beside(1, outs)
        before = {"before_products": outs[PRODUCTS], "before_payload": outs[PAYLOAD]}
        sums_of[tick] = outs[SUMS]
        if joined:
            grad_out = moved(outs[GRAD_JOINED], tick, mirror)
        elif tick:
            if decoder:
                skip_grads[mirror] = moved(outs[GRAD_SKIPPED].astype(BF16), tick, mirror)
            grad_out = moved(outs[GRAD_HIDDEN].astype(BF16), tick, tick - 1)
    products, payload = outs[PRODUCTS], outs[PAYLOAD]

    affine = jnp.stack([params[GAIN : GAIN + 2].reshape(-1), params[BIAS : BIAS + 2].reshape(-1)], axis=1)

    def cols_in_of(step):
        return columns_in(
            fields,
            orders[step],
            affine,
            conv_in.shape[1],
            skip_proj.shape[1],
            shard_id,
            is_decoder,
            octets,
            sections == 2,
        )

    def with_out(step, others):
        return [columns_out(w_steps[step], conv_out.shape[1], shard_id, octets), *others]

    ring = Ring(payload, DP)
    cols = []

    small_grads = lax.psum_scatter(products, DP, scatter_dimension=0, tiled=True)
    ring.turn()
    ring.spread()
    last = backward(1, {**entry, **outs})
    cols.append(cols_in_of(0))
    ring.values, ring.rows, fields, cols, sums_of[0], input_rows = beside(
        2, ring.values, ring.rows, fields, cols, sums_of[0] + last[SUMS], last[GRAD_HIDDEN]
    )
    sums = own(sums_of)
    shares = jnp.concatenate([sums[:4].reshape(shards, gain_share), sums[4:].reshape(shards, bias_share)], axis=1)
    summed = lax.all_to_all(shares, DP, 0, 0, tiled=True).sum(axis=0)
    ring.turn()
    ring.spread()
    ring.share(0)
    cols = [with_out(0, cols[0]), with_out(1, cols_in_of(1))]
    ring.values, ring.rows, ring.steps, cols, fields, input_rows, summed = beside(
        3, ring.values, ring.rows, ring.steps, cols, fields, input_rows, summed
    )
    ring.turn()
    ring.spread()
    ring.share(1)
    cols += [with_out(step, cols_in_of(step)) for step in (2, 3)]
    ring.values, ring.rows, ring.steps, cols, input_rows, small_grads = together(
        ring.values, ring.rows, ring.steps, cols, input_rows, small_grads
    )
    ring.spread_last()
    ring.share(2)
    input_grad = to_owners(input_rows, 0)
    totals = grad_step(cols[:2], ring.steps[0] + ring.steps[1], None)
    small_grads = small_grads.astype(F32)
    qkv_grad = small_grads[:, : 3 * WIDTH]
    out_grad = small_grads[:, 3 * WIDTH : 4 * WIDTH]
    ring.rows, ring.steps, cols, totals, input_grad, qkv_grad, out_grad = together(
        ring.rows, ring.steps, cols, totals, input_grad, qkv_grad, out_grad
    )
    ring.share(3)
    totals = grad_step(cols[2:], ring.steps[2] + ring.steps[3], totals)
    conv_out_grad, conv_in_grad = totals[:2]
    gains_grad, biases_grad = summed[:gain_share], summed[gain_share:]

    mods = last_rows([block for step in ring.steps for block in step], 2 * rows)
    mods = jnp.concatenate(
        [mods[:, start : start + count].reshape(all_images, WIDTH) for start in (0, count)], axis=1
    )
    embed_grad = dot_tn(embed_late, mods)
    grad_embed = dot_nt(mods, embed_proj[0])
    if sections == 2:
        grad_embed = grad_embed + lax.ppermute(grad_embed, SECTION, [(0, 1), (1, 0)])
    else:
        grad_embed = lax.psum(grad_embed, SECTION)
    grad_pre = jax.vjp(jax.nn.silu, pre_late)[1](grad_embed)[0]
    table_grad = lax.dot_general(
        onehot_late.astype(F32),
        grad_pre,
        (((0,), (0,)), ((), ())),
        precision=lax.Precision.HIGHEST,
        preferred_element_type=F32,
    )

    if skip_by_columns:
        skip_grad = totals[2]
    else:
        skip_grad = jnp.concatenate(
            [small_grads[:, 4 * WIDTH : 5 * WIDTH], small_grads[:, 5 * WIDTH :]], axis=0
        )
    return (
        level_output,
        input_grad,
        table_grad,
        conv_in_grad[None],
        conv_out_grad[None],
        embed_grad[None],
        skip_grad[None],
        qkv_grad[None],
        out_grad[None],
        gains_grad[None],
        biases_grad[None],
    )


def solution(mesh):
    placed = (
        P(None, DP, SECTION, None),
        P(None, DP, SECTION, None),
        P(None, DP),
        P(SECTION, DP, None),
        P(SECTION, DP, None),
        P(SECTION, DP, None),
        P(SECTION, DP, None),
        P(SECTION, DP, None),
        P(SECTION, DP, None),
        P(SECTION, DP),
        P(SECTION, DP),
        P(None, DP, None),
        P(None, DP),
    )
    return jax.shard_map(
        on_device,
        mesh=mesh,
        in_specs=placed,
        out_specs=(
            P(None, DP, SECTION, None),
            P(None, DP, SECTION, None),
            P(None, DP),
            P(SECTION, DP, None),
            P(SECTION, DP, None),
            P(SECTION, DP, None),
            P(SECTION, DP, None),
            P(SECTION, DP, None),
            P(SECTION, DP, None),
            P(SECTION, DP),
            P(SECTION, DP),
        ),
        check_vma=False,
    )
```

```python
import math
from functools import partial

import jax
import jax.numpy as jnp
import numpy as np
from jax import lax
from jax.experimental import pallas as pl
from jax.experimental.pallas import tpu as pltpu
from jax.sharding import PartitionSpec as P

WIDTH = 768
EMBED = 768
CLASSES = 1000
HEAD_DIM = 64
GROUPS = 32
SIDE = 8
LEVELS = 40
MICRO = 4
PIXELS = 64
TAPS = 9

EPS = 1e-05
SIGMA_LOW = 0.002
SIGMA_HIGH = 80.0

ACTIVE = "active"
ATTEND = "attend"
BEFORE = "before_"
BLOCK = "block_"
COLS_NAME = "cols"
COLS = "cols_"
COLUMNS_W = "columns_w"
CONV_IN = "conv_in"
CONV_ONE = "conv_one"
CONV_OUT = "conv_out"
DP = "dp"
FIELDS = "fields"
GRAD_HIDDEN = "grad_hidden"
GRAD_JOINED = "grad_joined"
GRAD_OUT = "grad_out"
GRAD_RESID = "grad_resid"
GRAD_RESID_B = "grad_resid_b"
GRAD_SKIPPED = "grad_skipped"
HELD = "held_"
HIDDEN = "hidden"
KEY = "key"
MIDDLE = "middle"
MIXED = "mixed"
MODULATION = "modulation"
OUT_NAME = "out"
OUT = "out_"
OUT_SEMS = "out_sems"
PAYLOAD = "payload"
PLANES = "planes"
PRIOR = "prior_"
PRODUCTS = "products"
PROJECT = "project"
QUERY = "query"
RESIDUAL = "residual"
RESULT = "result"
SECTION = "section"
SKIP = "skip"
SKIPPED = "skipped"
SOURCE = "source_"
STAT_C = "stat_c"
STAT_H = "stat_h"
STAT_R = "stat_r"
STAT_S = "stat_s"
SUMS = "sums"
TAKEN = "taken"
TOTAL = "total_"
VALUE = "value"

F32 = jnp.float32
BF16 = jnp.bfloat16
LANE = 128
CHUNKS = WIDTH // LANE
PER_GROUP = WIDTH // GROUPS
GROUP_SHARE = 1.0 / (PER_GROUP * PIXELS)
VMEM_LIMIT = 60 * 2**20

GAIN = 0
BIAS = 4

GROUP_OF = (np.arange(WIDTH)[:, None] // PER_GROUP == np.arange(LANE)[None, :]).astype(np.float32)


def lanes(chunk):
    return pl.ds(chunk * LANE, LANE)


def dot(left, right):
    return jnp.dot(left, right, preferred_element_type=F32)


def dot_nt(left, right):
    return lax.dot_general(left, right, (((1,), (1,)), ((), ())), preferred_element_type=F32)


def dot_tn(left, right):
    return lax.dot_general(left, right, (((0,), (0,)), ((), ())), preferred_element_type=F32)


def octet_sum(values, octets):
    width = values.shape[-1]
    partial_sums = values.reshape(SIDE, octets, width).sum(axis=0).reshape(octets // 8, 8, width)
    totals = jnp.sum(partial_sums, axis=1, keepdims=True)
    return jnp.broadcast_to(totals, partial_sums.shape).reshape(octets, width)


def over_rows(stat):
    octets, width = stat.shape
    return jnp.broadcast_to(stat[None], (SIDE, octets, width)).reshape(SIDE * octets, width)


def in_parts(values):
    first = values.astype(BF16)
    rest = values - first.astype(F32)
    second = rest.astype(BF16)
    third = (rest - second.astype(F32)).astype(BF16)
    return jnp.concatenate([first, second, third], axis=0)


def group_mean(sums, group_of, group_of_t):
    count = sums.shape[0]
    grouped = dot(in_parts(sums), group_of)
    grouped = (grouped[:count] + grouped[count : 2 * count] + grouped[2 * count :]) * GROUP_SHARE
    spread = dot(in_parts(grouped), group_of_t)
    return spread[:count] + spread[count : 2 * count] + spread[2 * count :]


def norm_stats(read, octets, group_of, group_of_t):
    sums = jnp.concatenate([octet_sum(read(c), octets) for c in range(CHUNKS)], axis=1)
    mean = group_mean(sums, group_of, group_of_t)
    squares = []
    for c in range(CHUNKS):
        centered = read(c) - over_rows(mean[:, c * LANE : (c + 1) * LANE])
        squares.append(octet_sum(centered * centered, octets))
    spread = group_mean(jnp.concatenate(squares, axis=1), group_of, group_of_t)
    return mean, lax.rsqrt(spread + EPS)


def normed_chunk(values, stat_ref, c):
    mean = stat_ref[0, :, lanes(c)]
    inv = stat_ref[1, :, lanes(c)]
    return (values - over_rows(mean)) * over_rows(inv)


def sigmoid(values):
    return 1.0 / (1.0 + jnp.exp(-values))


def silu_slope(values):
    gate = sigmoid(values)
    return gate * (1.0 + values * (1.0 - gate))


def put_shifted(planes, base, values, c, octets):
    rows = values.shape[0]
    column = lax.broadcasted_iota(jnp.int32, values.shape, 0) & 7
    before = jnp.where(column != 0, pltpu.roll(values, 1, 0), 0.0)
    after = jnp.where(column != 7, pltpu.roll(values, rows - 1, 0), 0.0)
    planes[base, pl.ds(octets, rows), lanes(c)] = before.astype(BF16)
    planes[base + 1, pl.ds(octets, rows), lanes(c)] = values.astype(BF16)
    planes[base + 2, pl.ds(octets, rows), lanes(c)] = after.astype(BF16)


def clear_edges(planes, octets):
    count, rows, width = planes.shape
    edge = jnp.zeros((count, octets, width), BF16)
    planes[:, pl.ds(0, octets), :] = edge
    planes[:, pl.ds(rows - octets, octets), :] = edge


def row_total(values):
    return jnp.sum(values, axis=0, keepdims=True)


def norm_back(read_grad, read_normed, gain_of, stat_ref, octets, tables, write, sums_out):
    group_of, group_of_t = tables
    first, second = [], []
    for c in range(CHUNKS):
        grad = read_grad(c)
        first.append(octet_sum(grad, octets))
        second.append(octet_sum(grad * read_normed(c), octets))
    first = jnp.concatenate(first, axis=1)
    second = jnp.concatenate(second, axis=1)
    sums_out(first, second)
    gain = gain_of(None)
    both = group_mean(jnp.concatenate([first * gain, second * gain], axis=0), group_of, group_of_t)
    for c in range(CHUNKS):
        part = slice(c * LANE, (c + 1) * LANE)
        inv = over_rows(stat_ref[1, :, lanes(c)])
        mean_one = over_rows(both[:octets, part])
        mean_two = over_rows(both[octets:, part])
        write(c, inv * (gain_of(c) * read_grad(c) - mean_one - read_normed(c) * mean_two))


class Weights:
    def __init__(self, sources, plan, sems):
        self.sources, self.plan, self.sems, self.waits, self.used = sources, plan, sems, {}, 0

    def fetch(self, name, held):
        self.waits[name] = []
        for source, piece, row, target, count in self.plan[name]:
            copy = pltpu.make_async_copy(
                self.sources[source].at[piece, pl.ds(row, count)],
                held.at[pl.ds(target, count)],
                self.sems.at[self.used],
            )
            copy.start()
            self.used += 1
            self.waits[name].append([target, copy])

    def need(self, name, stop):
        for entry in self.waits[name]:
            if entry[0] < stop and entry[1] is not None:
                entry[1].wait()
                entry[1] = None


def copies_of(plan, *names):
    return pltpu.SemaphoreType.DMA((sum(len(plan[name]) for name in names),))


SMALL = (QUERY, KEY, VALUE, OUT_NAME)


def held_at(r, name):
    if name in SMALL[:3]:
        return r.held_qkv.at[SMALL.index(name)]
    return getattr(r, HELD + name)


def held_scratch(decoder, names):
    sizes = {CONV_IN: (1 + decoder) * TAPS * WIDTH, CONV_OUT: TAPS * WIDTH, OUT_NAME: WIDTH, SKIP: 2 * WIDTH}
    scratch = {HELD + name: pltpu.VMEM((sizes[name], WIDTH), BF16) for name in names if name in sizes}
    if QUERY in names:
        scratch["held_qkv"] = pltpu.VMEM((3, WIDTH, WIDTH), BF16)
    return scratch


def tap_loop(body):
    def one(tap, carry):
        body(tap, lax.div(tap, 3), lax.rem(tap, 3))
        return carry

    lax.fori_loop(0, TAPS, one, 0)


def plane_rows(planes, plane, down, octets, rows):
    return planes[plane, pl.ds(pl.multiple_of(octets * down, 16), rows), :]


def head_pair(values, left):
    zero = jnp.zeros_like(values)
    return jnp.concatenate([jnp.where(left, values, zero), jnp.where(left, zero, values)], axis=0)


def attention_of(keys, queries):
    scores = [dot_nt(k, q) * (1.0 / math.sqrt(HEAD_DIM)) for k, q in zip(keys, queries)]
    tops = [jnp.max(part, axis=0, keepdims=True) for part in scores]
    weights = [jnp.exp(part - top) for part, top in zip(scores, tops)]
    totals = [1.0 / jnp.sum(part, axis=0, keepdims=True) for part in weights]
    return [part * total for part, total in zip(weights, totals)]


AT_ONCE = 4


def image_groups(images):
    every = [(image, pl.ds(image * PIXELS, PIXELS), pair) for image in range(images) for pair in range(CHUNKS)]
    return [every[start : start + AT_ONCE * CHUNKS] for start in range(0, len(every), AT_ONCE * CHUNKS)]


def by_image(scratch, image, chunk):
    part = scratch[:, image, :, lanes(chunk)]
    return part.reshape(PIXELS, LANE)


def put_image(scratch, image, chunk, values):
    scratch[:, image, :, lanes(chunk)] = values.reshape(SIDE, 8, LANE)


def conv_in_forward(r, decoder, shared, octets):
    rows = r.hidden.shape[0]
    tables = (r.group_of[...], r.group_of_t[...])
    sides = [(r.hidden, r.stat_h, 0)] + ([(r.skipped, r.stat_s, 1)] if decoder else [])
    span = WIDTH * len(sides)
    clear_edges(r.planes, octets)
    for source, stat, which in sides:
        mean, inv = norm_stats(lambda c: source[:, lanes(c)].astype(F32), octets, *tables)
        stat[0] = mean
        stat[1] = inv
        if shared and not which:
            for index, values in enumerate((mean, 1.0 / inv)):
                grouped = dot(values.astype(BF16), tables[0]) * (1.0 / PER_GROUP)
                r.turned[pl.ds(WIDTH + index * GROUPS, GROUPS), :] = over_rows(grouped).T[:GROUPS].astype(BF16)
        for c in range(CHUNKS):
            normed = normed_chunk(source[:, lanes(c)].astype(F32), stat, c)
            value = (
                normed * r.params[pl.ds(GAIN + which, 1), lanes(c)]
                + r.params[pl.ds(BIAS + which, 1), lanes(c)]
            )
            value = value * sigmoid(value)
            put_shifted(r.planes, 3 * which, value, c, octets)
            if not (shared and which):
                r.turned[pl.ds(which * WIDTH + c * LANE, LANE), :] = normed.T.astype(BF16)
    if decoder:
        r.conv_one[...] = jnp.broadcast_to(r.params[pl.ds(BIAS + 2, 1), :], r.conv_one.shape)
    for down in range(3 if decoder else 0):
        r.weights.need(CONV_IN, 3 * (down + 1) * span)

        def one_tap(across, carry, down=down):
            for half in range(len(sides)):
                first = pl.multiple_of((3 * down + across) * span + half * WIDTH, WIDTH)
                values = r.planes[3 * half + across, pl.ds(octets * down, rows), :]
                r.conv_one[...] += dot(values, r.held_conv_in[pl.ds(first, WIDTH), :])
            return carry

        lax.fori_loop(0, 3, one_tap, 0)
    for tap in range(0 if decoder else TAPS):
        r.weights.need(CONV_IN, (tap + 1) * span)
        for half in range(len(sides)):
            part = dot(
                r.planes[3 * half + tap % 3, pl.ds(octets * (tap // 3), rows), :],
                r.held_conv_in[pl.ds(tap * span + half * WIDTH, WIDTH), :],
            )
            if tap == 0 and half == 0:
                r.conv_one[...] = part + r.params[pl.ds(BIAS + 2, 1), :]
            else:
                r.conv_one[...] += part
    r.flush(CONV_ONE)
    mean, inv = norm_stats(lambda c: r.conv_one[:, lanes(c)], octets, *tables)
    r.stat_c[0] = mean
    r.stat_c[1] = inv
    for c in range(CHUNKS):
        normed = (
            normed_chunk(r.conv_one[:, lanes(c)], r.stat_c, c) * r.params[pl.ds(GAIN + 2, 1), lanes(c)]
            + r.params[pl.ds(BIAS + 5, 1), lanes(c)]
        )
        scale = over_rows(r.modulation[:, lanes(c)])
        shift = over_rows(r.modulation[:, lanes(CHUNKS + c)])
        value = normed * (1.0 + scale) + shift
        value = value * sigmoid(value)
        r.middle[:, lanes(c)] = value.astype(BF16)
        r.turned_w[lanes(c), :] = value.T.astype(BF16)
    r.flush(MIDDLE, STAT_C)
    r.leave(r.turned, r.fields, r.fields_sems.at[0])
    r.leave(r.turned_w, r.columns_w, r.fields_sems.at[1])


def block_forward(r, decoder, octets):
    rows = r.hidden.shape[0]
    images = octets // 8
    tables = (r.group_of[...], r.group_of_t[...])
    clear_edges(r.planes, octets)
    for c in range(CHUNKS):
        put_shifted(r.planes, 0, r.middle[:, lanes(c)].astype(F32), c, octets)
    if not decoder:
        r.weights.need(CONV_OUT, TAPS * WIDTH)
        r.residual[...] = jnp.broadcast_to(r.params[pl.ds(BIAS + 6, 1), :], r.residual.shape)

        def one_tap(tap, down, across):
            weights = r.held_conv_out[pl.ds(pl.multiple_of(tap * WIDTH, WIDTH), WIDTH), :]
            r.residual[...] += dot(plane_rows(r.planes, across, down, octets, rows), weights)

        tap_loop(one_tap)
    for tap in range(TAPS if decoder else 0):
        r.weights.need(CONV_OUT, (tap + 1) * WIDTH)
        part = dot(
            r.planes[tap % 3, pl.ds(octets * (tap // 3), rows), :], r.held_conv_out[pl.ds(tap * WIDTH, WIDTH), :]
        )
        if tap == 0:
            r.residual[...] = part + r.params[pl.ds(BIAS + 6, 1), :]
        else:
            r.residual[...] += part
    if decoder:
        r.weights.need(SKIP, 2 * WIDTH)
        r.residual[...] += (
            dot(r.hidden[...], r.held_skip[pl.ds(0, WIDTH), :])
            + dot(r.skipped[...], r.held_skip[pl.ds(WIDTH, WIDTH), :])
            + r.params[pl.ds(BIAS + 7, 1), :]
        )
    else:
        r.residual[...] += r.hidden[...].astype(F32)
    r.flush(RESIDUAL)
    mean, inv = norm_stats(lambda c: r.residual[:, lanes(c)], octets, *tables)
    r.stat_r[0] = mean
    r.stat_r[1] = inv
    for c in range(CHUNKS):
        r.attend[:, lanes(c)] = (
            normed_chunk(r.residual[:, lanes(c)], r.stat_r, c) * r.params[pl.ds(GAIN + 3, 1), lanes(c)]
            + r.params[pl.ds(BIAS + 8, 1), lanes(c)]
        ).astype(BF16)
    r.flush(ATTEND)
    for index, (name, bias) in enumerate(((QUERY, 9), (KEY, None), (VALUE, 10))):
        r.weights.need(name, WIDTH)
        part = dot(r.attend[...], r.held_qkv[index])
        if bias is not None:
            part = part + r.params[pl.ds(BIAS + bias, 1), :]
        part = part.reshape(SIDE, images, 8, WIDTH)
        for image in range(images):
            own = part[:, image].reshape(PIXELS, WIDTH).astype(BF16)
            r.project[pl.ds(image * PIXELS, PIXELS), pl.ds(index * WIDTH, WIDTH)] = own
    r.flush(PROJECT)
    left = lax.broadcasted_iota(jnp.int32, (PIXELS, LANE), 1) < HEAD_DIM
    for group in image_groups(images):
        queries = [head_pair(r.project[span, lanes(pair)], left) for _, span, pair in group]
        keys_h = [r.project[span, lanes(CHUNKS + pair)] for _, span, pair in group]
        values_h = [r.project[span, lanes(2 * CHUNKS + pair)] for _, span, pair in group]
        attention = [part.astype(BF16) for part in attention_of(keys_h, queries)]
        both = [dot_tn(part, values) for part, values in zip(attention, values_h)]
        for (image, _, pair), part in zip(group, both):
            put_image(r.grid, image, pair, jnp.where(left, part[:PIXELS], part[PIXELS:]))
    r.mixed[...] = r.grid[:, :, :, pl.ds(0, WIDTH)].reshape(rows, WIDTH).astype(BF16)
    r.flush(MIXED)
    r.weights.need(OUT_NAME, WIDTH)
    r.result[...] = (
        r.residual[...] + dot(r.mixed[...], r.held_out[...]) + r.params[pl.ds(BIAS + 11, 1), :]
    ).astype(BF16)


def attention_backward(r, decoder, octets, shards, with_skip):
    rows = r.residual.shape[0]
    images = octets // 8
    tables = (r.group_of[...], r.group_of_t[...])

    def put_sum(row, c, values):
        r.sums[pl.ds(row, 1), lanes(c)] = row_total(values)

    def leave(first, width):
        part = pl.ds(first * WIDTH, width * WIDTH)
        r.leave(r.built.at[:, part], r.products.at[:, part], r.built_sems.at[min(first, 2)])

    top = r.grad_out[...].astype(BF16)
    for c in range(CHUNKS):
        put_sum(BIAS + 11, c, r.grad_out[:, lanes(c)].astype(BF16).astype(F32))
    r.built[:, pl.ds(3 * WIDTH, WIDTH)] = dot_tn(r.mixed[...], top).astype(BF16)
    leave(3, 1)
    r.weights.need(OUT_NAME, WIDTH)
    r.grid[:, :, :, pl.ds(0, WIDTH)] = dot_nt(top, r.held_out[...]).reshape(SIDE, images, 8, WIDTH)
    left = lax.broadcasted_iota(jnp.int32, (PIXELS, LANE), 1) < HEAD_DIM
    root = 1.0 / math.sqrt(HEAD_DIM)
    for group in image_groups(images):
        queries = [head_pair(r.project[span, lanes(pair)], left) for _, span, pair in group]
        keys_h = [r.project[span, lanes(CHUNKS + pair)] for _, span, pair in group]
        values_h = [r.project[span, lanes(2 * CHUNKS + pair)] for _, span, pair in group]
        grads_h = [head_pair(by_image(r.grid, image, pair).astype(BF16), left) for image, _, pair in group]
        attention = attention_of(keys_h, queries)
        weighted = [dot_nt(v, g) * part for v, g, part in zip(values_h, grads_h, attention)]
        totals = [jnp.sum(part, axis=0, keepdims=True) for part in weighted]
        scores = [(w - part * total).astype(BF16) for w, part, total in zip(weighted, attention, totals)]
        both = [dot_tn(part, k) * root for part, k in zip(scores, keys_h)]
        grad_keys = [dot(part, q) * root for part, q in zip(scores, queries)]
        grad_values = [dot(part.astype(BF16), g) for part, g in zip(attention, grads_h)]
        for index, (image, _, pair) in enumerate(group):
            put_image(r.grid, image, pair, jnp.where(left, both[index][:PIXELS], both[index][PIXELS:]))
            put_image(r.grid, image, CHUNKS + pair, grad_keys[index])
            put_image(r.grid, image, 2 * CHUNKS + pair, grad_values[index])
    for index in range(3):
        for pair in range(CHUNKS):
            chunk = lanes(index * CHUNKS + pair)
            joined = r.grid[:, :, :, chunk].reshape(rows, LANE).astype(BF16)
            r.grad_project[:, chunk] = joined
            if index == 0:
                put_sum(BIAS + 9, pair, joined.astype(F32))
            if index == 2:
                put_sum(BIAS + 10, pair, joined.astype(F32))
    for index in range(3):
        columns = pl.ds(index * WIDTH, WIDTH)
        r.built[:, columns] = dot_tn(r.attend[...], r.grad_project[:, columns]).astype(BF16)
    leave(0, 3)
    for index, name in enumerate(SMALL[:3]):
        r.weights.need(name, WIDTH)
        part = dot_nt(r.grad_project[:, pl.ds(index * WIDTH, WIDTH)], r.held_qkv[index])
        if index == 0:
            r.work[...] = part
        else:
            r.work[...] += part

    def gain_attend(c):
        return r.params[pl.ds(GAIN + 3, 1), :] if c is None else r.params[pl.ds(GAIN + 3, 1), lanes(c)]

    def sums_attend(first, second):
        r.sums[pl.ds(BIAS + 8, 1), :] = row_total(first) * 0.125
        r.sums[pl.ds(GAIN + 3, 1), :] = row_total(second) * 0.125

    def write_resid(c, grad):
        total = r.grad_out[:, lanes(c)].astype(F32) + grad
        r.grad_resid[:, lanes(c)] = total
        rounded = total.astype(BF16)
        r.grad_resid_b[:, lanes(c)] = rounded
        rounded = rounded.astype(F32)
        put_sum(BIAS + 6, c, rounded)
        if decoder:
            put_sum(BIAS + 7, c, rounded)

    norm_back(
        lambda c: r.work[:, lanes(c)],
        lambda c: normed_chunk(r.residual[:, lanes(c)], r.stat_r, c),
        gain_attend,
        r.stat_r,
        octets,
        tables,
        write_resid,
        sums_attend,
    )
    r.flush(GRAD_RESID, GRAD_RESID_B)
    if with_skip:
        share = WIDTH // shards
        for side, source in enumerate((r.hidden, r.skipped)):
            first = side * shards // 2
            if decoder:
                part = dot_tn(source[...], r.grad_resid_b[...]).astype(BF16)
            else:
                part = jnp.zeros((WIDTH, WIDTH), BF16)
            for index in range(shards // 2):
                target = pl.ds((first + index) * share, share)
                for half in range(2):
                    r.built[target, pl.ds((4 + half) * WIDTH, WIDTH)] = part[
                        (2 * index + half) * share : (2 * index + half + 1) * share
                    ]
        part = pl.ds(4 * WIDTH, 2 * WIDTH)
        r.leave(r.built.at[:, part], r.products.at[:, part], r.built_sems.at[1])


def middle_backward(r, octets):
    rows = r.conv_one.shape[0]
    tables = (r.group_of[...], r.group_of_t[...])
    clear_edges(r.planes, octets)
    r.rows[pl.ds(0, rows), :] = r.grad_resid_b[...]
    for c in range(CHUNKS):
        put_shifted(r.planes, 0, r.grad_resid_b[:, lanes(c)].astype(F32), c, octets)
    r.weights.need(CONV_OUT, TAPS * WIDTH)
    r.work[...] = jnp.zeros(r.work.shape, F32)

    def one_tap(tap, down, across):
        weights = r.held_conv_out[pl.ds(pl.multiple_of(tap * WIDTH, WIDTH), WIDTH), :]
        r.work[...] += dot_nt(plane_rows(r.planes, 2 - across, 2 - down, octets, rows), weights)

    tap_loop(one_tap)
    for c in range(CHUNKS):
        normed = (
            normed_chunk(r.conv_one[:, lanes(c)], r.stat_c, c) * r.params[pl.ds(GAIN + 2, 1), lanes(c)]
            + r.params[pl.ds(BIAS + 5, 1), lanes(c)]
        )
        scale = over_rows(r.modulation[:, lanes(c)])
        shift = over_rows(r.modulation[:, lanes(CHUNKS + c)])
        r.work[:, lanes(c)] = r.work[:, lanes(c)] * silu_slope(normed * (1.0 + scale) + shift)

    def gain_middle(c):
        if c is None:
            return r.params[pl.ds(GAIN + 2, 1), :] * (1.0 + r.modulation[:, pl.ds(0, WIDTH)])
        return over_rows(r.params[pl.ds(GAIN + 2, 1), lanes(c)] * (1.0 + r.modulation[:, lanes(c)]))

    def sums_middle(first, second):
        scaled = 1.0 + r.modulation[:, pl.ds(0, WIDTH)]
        r.sums[pl.ds(BIAS + 5, 1), :] = row_total(first * scaled) * 0.125
        r.sums[pl.ds(GAIN + 2, 1), :] = row_total(second * scaled) * 0.125
        grad_scale = (
            r.params[pl.ds(GAIN + 2, 1), :] * second + r.params[pl.ds(BIAS + 5, 1), :] * first
        ).astype(BF16)
        grad_shift = first.astype(BF16)
        images = octets // 8
        row = lax.broadcasted_iota(jnp.int32, (16, octets), 0)
        column = lax.broadcasted_iota(jnp.int32, (16, octets), 1)
        for index, part in enumerate((grad_scale, grad_shift)):
            taken = ((row - index * images) * 8 == column) & (row >= index * images)
            chosen = dot(jnp.where(taken, 1.0, 0.0).astype(BF16), part)
            compact = chosen if index == 0 else compact + chosen
        r.rows[pl.ds(2 * rows, 16), :] = compact.astype(BF16)
        r.sums[pl.ds(BIAS + 3, 1), :] = row_total(grad_scale.astype(F32)) * 0.125
        r.sums[pl.ds(BIAS + 4, 1), :] = row_total(grad_shift.astype(F32)) * 0.125

    def write_conv(c, grad):
        rounded = grad.astype(BF16)
        r.grad_conv_b[:, lanes(c)] = rounded
        r.rows[pl.ds(rows, rows), lanes(c)] = rounded
        r.sums[pl.ds(BIAS + 2, 1), lanes(c)] = row_total(rounded.astype(F32))

    norm_back(
        lambda c: r.work[:, lanes(c)],
        lambda c: normed_chunk(r.conv_one[:, lanes(c)], r.stat_c, c),
        gain_middle,
        r.stat_c,
        octets,
        tables,
        write_conv,
        sums_middle,
    )
    r.leave(r.rows, r.payload, r.payload_sem)


def conv_in_backward(r, decoder, joined, octets, prefetched):
    rows = r.hidden.shape[0]
    tables = (r.group_of[...], r.group_of_t[...])
    sides = [(r.hidden, r.stat_h, r.total if joined else r.grad_hidden, 0)]
    if decoder:
        sides.append((r.skipped, r.stat_s, r.total if joined else r.grad_skipped, 1))
    span = WIDTH * len(sides)
    clear_edges(r.planes, octets)
    for c in range(CHUNKS):
        put_shifted(r.planes, 0, r.grad_conv_b[:, lanes(c)].astype(F32), c, octets)
    if prefetched:
        r.weights.need(CONV_IN, TAPS * span)
        r.sides[...] = jnp.zeros(r.sides.shape, F32)

        def one_tap(tap, down, across):
            values = plane_rows(r.planes, 2 - across, 2 - down, octets, rows)
            for half in range(len(sides)):
                first = pl.multiple_of(tap * span + half * WIDTH, WIDTH)
                r.sides[half] += dot_nt(values, r.held_conv_in[pl.ds(first, WIDTH), :])

        tap_loop(one_tap)
    for tap in range(0 if prefetched else TAPS):
        r.weights.need(CONV_IN, (tap + 1) * span)
        for _, _, _, half in sides:
            part = dot_nt(
                r.planes[2 - tap % 3, pl.ds(octets * (2 - tap // 3), rows), :],
                r.held_conv_in[pl.ds(tap * span + half * WIDTH, WIDTH), :],
            )
            if tap == 0:
                r.sides[half] = part
            else:
                r.sides[half] += part
    if decoder:
        r.weights.need(SKIP, 2 * WIDTH)
    for source, stat, target, which in sides:

        def normed_of(c, source=source, stat=stat):
            return normed_chunk(source[:, lanes(c)].astype(F32), stat, c)

        def gain_input(c, which=which):
            row = pl.ds(GAIN + which, 1)
            return r.params[row, :] if c is None else r.params[row, lanes(c)]

        for c in range(CHUNKS):
            value = normed_of(c) * gain_input(c) + r.params[pl.ds(BIAS + which, 1), lanes(c)]
            r.sides[which, :, lanes(c)] = r.sides[which, :, lanes(c)] * silu_slope(value)

        def sums_input(first, second, which=which):
            r.sums[pl.ds(BIAS + which, 1), :] = row_total(first) * 0.125
            r.sums[pl.ds(GAIN + which, 1), :] = row_total(second) * 0.125

        if decoder:
            part = dot_nt(r.grad_resid_b[...], r.held_skip[pl.ds(which * WIDTH, WIDTH), :])
            if joined and which:
                target[...] += part
            else:
                target[...] = part

        def write_input(c, grad, target=target):
            if decoder:
                target[:, lanes(c)] += grad
            else:
                target[:, lanes(c)] = grad + r.grad_resid[:, lanes(c)]

        norm_back(
            lambda c, which=which: r.sides[which, :, lanes(c)],
            normed_of,
            gain_input,
            stat,
            octets,
            tables,
            write_input,
            sums_input,
        )
    if joined:
        r.grad_joined[...] = r.total[...].astype(BF16)


def shape(dims, kind):
    return jax.ShapeDtypeStruct(dims, kind)


IN_VMEM = pl.BlockSpec(memory_space=pltpu.VMEM)
IN_HBM = pl.BlockSpec(memory_space=pl.ANY)
IN_SMEM = pl.BlockSpec(memory_space=pltpu.SMEM)


class Refs:
    def __init__(self, refs, targets):
        self.__dict__.update(refs)
        self._targets, self._leaving = targets, []

    def leave(self, source, target, sem):
        self._leaving.append(pltpu.make_async_copy(source, target, sem))
        self._leaving[-1].start()

    def flush(self, *names):
        for name in names:
            if name in self._targets:
                self.leave(getattr(self, name), *self._targets.pop(name))

    def finish(self):
        self.flush(*list(self._targets))
        for copy in self._leaving:
            copy.wait()


def call(body, name, operands, outputs, scratch, weights=None, order=(), active=None, far=(), flops=0, always=False, light=False):
    sources, plan = weights if weights is not None else ([], {})
    scratch = dict(scratch)
    if order:
        scratch["fetched"] = pltpu.SemaphoreType.DMA((sum(len(plan[part]) for part in order),))
    ins = [key for key in operands if key not in far and not key.startswith(BEFORE)]
    outs = [key for key in outputs if key not in far]
    for key in outs:
        scratch[OUT + key] = pltpu.VMEM(outputs[key].shape, outputs[key].dtype)
    scratch[OUT_SEMS] = pltpu.SemaphoreType.DMA((max(len(outs), 1),))
    names = [*operands, *(SOURCE + str(index) for index in range(len(sources)))]
    names += ([ACTIVE] if active is not None else []) + [*outputs, *scratch]
    moved = sum(int(np.prod(v.shape)) * v.dtype.itemsize for v in (*operands.values(), *outputs.values()))

    def kernel(*refs):
        refs = dict(zip(names, refs))

        def run():
            targets = {}
            for index, key in enumerate(outs):
                targets[key] = (refs[key], refs[OUT_SEMS].at[index])
                refs[key] = refs[OUT + key]
            r = Refs(refs, targets)
            if order:
                r.weights = Weights([getattr(r, SOURCE + str(index)) for index in range(len(sources))], plan, r.fetched)
                for part in order:
                    r.weights.fetch(part, held_at(r, part))
            if SUMS in outputs:
                r.sums[...] = jnp.zeros(r.sums.shape, F32)
            body(r)
            r.finish()

        if active is None or always:
            run()
        else:
            pl.when(refs[ACTIVE][0] == 1)(run)

    keys = list(operands)
    results = pl.pallas_call(
        kernel,
        out_shape=list(outputs.values()),
        in_specs=[IN_VMEM if key in ins else IN_HBM for key in keys] + [IN_HBM] * len(sources) + ([IN_SMEM] if active is not None else []),
        out_specs=[IN_HBM] * len(outputs),
        scratch_shapes=list(scratch.values()),
        input_output_aliases={
            index: list(outputs).index(key[len(BEFORE) :])
            for index, key in enumerate(keys)
            if key.startswith(BEFORE)
        },
        compiler_params=pltpu.CompilerParams(vmem_limit_bytes=VMEM_LIMIT),
        cost_estimate=pl.CostEstimate(
            flops=flops // 4 if light else flops, bytes_accessed=moved // 4 if light else moved, transcendentals=0
        ),
        name=name,
    )(*operands.values(), *sources, *([active] if active is not None else []))
    return dict(zip(outputs, results))


def field(rows, kind=BF16, width=WIDTH):
    return shape((rows, width), kind)


def planes_scratch(sides, rows):
    return pltpu.VMEM((3 * sides, rows + 2 * rows // SIDE, WIDTH), BF16)


def run_forward(decoder, shared, hidden, skipped, weights_for, modulation, common, before, active):
    rows = hidden.shape[0]
    octets = rows // SIDE
    inputs = {HIDDEN: hidden, **({SKIPPED: skipped} if decoder else {}), **common}
    inputs.update(before)
    stat = shape((2, octets, WIDTH), F32)
    first_out = {
        CONV_ONE: field(rows, F32),
        STAT_C: stat,
        FIELDS: field(WIDTH + (2 * GROUPS if shared else WIDTH), width=rows),
        COLUMNS_W: field(WIDTH, width=rows),
        STAT_H: stat,
        **({STAT_S: stat} if decoder else {}),
    }
    first_scratch = {
        "turned": pltpu.VMEM(first_out[FIELDS].shape, BF16),
        "turned_w": pltpu.VMEM((WIDTH, rows), BF16),
        "fields_sems": pltpu.SemaphoreType.DMA((2,)),
        PLANES: planes_scratch(1 + decoder, rows),
        **held_scratch(decoder, (CONV_IN,)),
    }
    second_names = (CONV_OUT, *((SKIP,) if decoder else ()), *SMALL)
    second_out = {
        RESULT: field(rows),
        RESIDUAL: field(rows, F32),
        STAT_R: stat,
        ATTEND: field(rows),
        PROJECT: field(rows, width=3 * WIDTH),
        MIXED: field(rows),
    }
    second_scratch = {
        "grid": pltpu.VMEM((SIDE, octets // 8, 8, WIDTH), F32),
        PLANES: planes_scratch(1, rows),
        **held_scratch(decoder, second_names),
    }
    first_flops = 2 * rows * (1 + decoder) * TAPS * WIDTH * WIDTH
    second_flops = 2 * rows * (TAPS + 6) * WIDTH * WIDTH

    def first_body(r):
        conv_in_forward(r, decoder, shared, octets)

    def second_body(r):
        block_forward(r, decoder, octets)

    def both(r):
        first_body(r)
        second_body(r)

    if not decoder:
        names = (CONV_IN, *second_names)
        return call(
            both,
            "encoder_forward",
            {**inputs, MODULATION: modulation},
            {**first_out, **second_out},
            {**second_scratch, **first_scratch, MIDDLE: pltpu.VMEM((rows, WIDTH), BF16)},
            weights_for(decoder, *names),
            names,
            active,
            (FIELDS, COLUMNS_W),
            first_flops + second_flops,
        )
    first = call(
        first_body,
        "conv_in_forward",
        {**inputs, MODULATION: modulation},
        {**first_out, MIDDLE: field(rows)},
        first_scratch,
        weights_for(decoder, CONV_IN),
        (CONV_IN,),
        active,
        (FIELDS, COLUMNS_W),
        first_flops,
    )
    second = call(
        second_body,
        "block_forward",
        {HIDDEN: hidden, SKIPPED: skipped, MIDDLE: first[MIDDLE], **common},
        second_out,
        second_scratch,
        weights_for(decoder, *second_names),
        second_names,
        active,
        (),
        second_flops,
    )
    return {**first, **second}


def run_backward(decoder, joined, shards, with_skip, part, entry, weights_for, modulation, common, before, active):
    rows = entry[HIDDEN].shape[0]
    octets = rows // SIDE
    first, second = part in (0, None), part in (1, None)
    inputs, names = {}, ()
    if first:
        names += (OUT_NAME, *SMALL[:3], CONV_OUT)
        used = [GRAD_OUT, PROJECT, RESIDUAL, STAT_R, ATTEND, MIXED, CONV_ONE, STAT_C]
        inputs.update({name: entry[name] for name in used}, modulation=modulation, **before)
    if second:
        names += (CONV_IN, *((SKIP,) if decoder else ()))
    if second or with_skip:
        inputs[HIDDEN] = entry[HIDDEN]
        if decoder or with_skip:
            inputs[SKIPPED] = entry[SKIPPED]
    if second:
        inputs[STAT_H] = entry[STAT_H]
        if decoder:
            inputs[STAT_S] = entry[STAT_S]
    between = {GRAD_RESID: field(rows, F32), GRAD_RESID_B: field(rows), "grad_conv_b": field(rows)}
    outputs = {SUMS: field(16, F32)}
    scratch = {PLANES: planes_scratch(1, rows), **held_scratch(decoder, names)}
    if first:
        outputs[PRODUCTS] = field(WIDTH, width=(6 if with_skip else 4) * WIDTH)
        outputs[PAYLOAD] = field(2 * rows + 16)
        scratch.update(
            grid=pltpu.VMEM((SIDE, octets // 8, 8, 3 * WIDTH), F32),
            grad_project=pltpu.VMEM((rows, 3 * WIDTH), BF16),
            built=pltpu.VMEM(outputs[PRODUCTS].shape, BF16),
            built_sems=pltpu.SemaphoreType.DMA((3,)),
            rows=pltpu.VMEM(outputs[PAYLOAD].shape, BF16),
            payload_sem=pltpu.SemaphoreType.DMA,
        )
    if part == 0:
        outputs.update(between)
    elif part == 1:
        inputs.update({name: entry[name] for name in between if decoder or name != GRAD_RESID_B})
    else:
        scratch.update({name: pltpu.VMEM(value.shape, value.dtype) for name, value in between.items()})
    scratch["sides"] = pltpu.VMEM((1 + (decoder and second), rows, WIDTH), F32)
    if second:
        if joined:
            outputs[GRAD_JOINED] = field(rows)
            scratch["total"] = pltpu.VMEM((rows, WIDTH), F32)
        else:
            outputs[GRAD_HIDDEN] = field(rows, F32)
            if decoder:
                outputs[GRAD_SKIPPED] = field(rows, F32)

    def body(r):
        r.work = r.sides.at[0]
        if first:
            attention_backward(r, decoder, octets, shards, with_skip)
            middle_backward(r, octets)
        if second:
            conv_in_backward(r, decoder, joined, octets, first)

    return call(
        body,
        "section_backward" if part is None else ("block_backward", "conv_in_backward")[part],
        {**inputs, **common},
        outputs,
        scratch,
        weights_for(decoder, *names),
        names,
        active,
        (PRODUCTS, PAYLOAD),
        2 * rows * (first * (TAPS + 14) + second * (1 + decoder) * TAPS) * WIDTH * WIDTH,
    )


def tap_at(place, index, rows, channels):
    block = rows // TAPS
    per_tap = channels // block
    position = place * TAPS + index
    tap = lax.div(position, per_tap)
    start = pl.multiple_of(lax.rem(position, per_tap) * block, 16)
    return lax.div(tap, 3) - 1, lax.rem(tap, 3) - 1, start, block


def shifted_field(values, down, across, octets, also=None):
    width = values.shape[1]
    lane = lax.broadcasted_iota(jnp.int32, (1, width), 1)
    row, column = lax.div(lane, octets) + down, (lane & 7) + across
    inside = (row >= 0) & (row < SIDE) & (column >= 0) & (column < 8)
    if also is not None:
        inside = inside & also(lane)
    back = lax.rem(width - (octets * down + across), width)
    return jnp.where(inside, pltpu.roll(values, back, 1), 0.0).astype(BF16)


def columns_in_kernel(octets, shared, place, order, fields, affine, cols_in, *cols_skip):
    width = fields.shape[2]
    rows = cols_in.shape[0]
    for index in range(TAPS):
        down, across, start, block = tap_at(place[0], index, rows, 2 * WIDTH)
        side = lax.div(start, WIDTH)
        spot = pl.multiple_of(start - side * WIDTH if shared else start, 16)
        values = fields[0, pl.ds(spot, block), :].astype(F32)
        values = values * affine[pl.ds(start, block), 0:1] + affine[pl.ds(start, block), 1:2]
        values = values * sigmoid(values)
        kept = lax.mul(side, 1 - place[1]) * width
        cols_in[pl.ds(index * block, block), :] = shifted_field(
            values, down, across, octets, lambda lane: lane >= kept
        )
    if shared:
        rows = cols_skip[0].shape[0]
        start = pl.multiple_of(lax.rem(place[0] * rows, WIDTH), 16)
        channel = lax.broadcasted_iota(jnp.int32, (rows, GROUPS), 0) + start
        group = lax.broadcasted_iota(jnp.int32, (rows, GROUPS), 1) * PER_GROUP
        member = jnp.where((channel >= group) & (channel < group + PER_GROUP), 1.0, 0.0).astype(BF16)
        mean = dot(member, fields[0, pl.ds(WIDTH, GROUPS), :])
        deviation = dot(member, fields[0, pl.ds(WIDTH + GROUPS, GROUPS), :])
        values = fields[0, pl.ds(start, rows), :].astype(F32) * deviation + mean
        lane = lax.broadcasted_iota(jnp.int32, (1, width), 1)
        cols_skip[0][...] = jnp.where(lane < place[1] * width, values, 0.0).astype(BF16)


def tap_slices_plain(fields, rows, channels, place, octets):
    pieces, _, width = fields.shape
    spots = place * rows + jnp.arange(rows)
    taps = spots // channels
    values = jnp.take(fields, spots % channels, axis=1)
    lane = jnp.arange(width)
    total = jnp.zeros_like(values)
    for tap in range(TAPS):
        down, across = tap // 3 - 1, tap % 3 - 1
        row, column = lane // octets + down, lane % 8 + across
        inside = (row >= 0) & (row < SIDE) & (column >= 0) & (column < 8)
        moved = jnp.roll(values, -(octets * down + across), axis=2)
        total = jnp.where((taps == tap)[None, :, None] & inside, moved, total)
    return total.transpose(1, 0, 2).reshape(rows, pieces * width)


def columns_in(fields, order, affine, rows_in, rows_skip, place, decoder, octets, shared):
    _, height, width = fields.shape
    pieces = order.shape[0]
    if not shared and rows_in % (TAPS * 16):
        fields = jnp.take(fields, order, axis=0)
        sides = fields.astype(F32) * affine[:, :1] + affine[:, 1:]
        keep = (jnp.arange(2 * WIDTH)[:, None] < WIDTH) | decoder
        sides = jnp.where(keep, jax.nn.silu(sides), 0.0).astype(BF16)
        return [tap_slices_plain(sides, rows_in, 2 * WIDTH, place, octets)]
    heights = (rows_in, rows_skip) if shared else (rows_in,)
    return pl.pallas_call(
        partial(columns_in_kernel, octets, shared),
        grid_spec=pltpu.PrefetchScalarGridSpec(
            num_scalar_prefetch=2,
            grid=(pieces,),
            in_specs=[
                pl.BlockSpec((1, height, width), lambda piece, place, order: (order[piece], 0, 0)),
                pl.BlockSpec((2 * WIDTH, 2), lambda piece, place, order: (0, 0)),
            ],
            out_specs=[pl.BlockSpec((rows, width), lambda piece, place, order: (0, piece)) for rows in heights],
        ),
        out_shape=[shape((rows, pieces * width), BF16) for rows in heights],
        compiler_params=pltpu.CompilerParams(vmem_limit_bytes=VMEM_LIMIT),
        cost_estimate=pl.CostEstimate(
            flops=0, bytes_accessed=pieces * height * width, transcendentals=0
        ),
        name="columns_in",
    )(jnp.stack([place, decoder.astype(jnp.int32)]).astype(jnp.int32), order, fields, affine)


def columns_out(blocks, rows, place, octets):
    fields = [
        (number, first) for number, block in enumerate(blocks) for first in range(0, block.shape[0], WIDTH)
    ]
    if rows % (TAPS * 16):
        taken = jnp.stack([blocks[number][first : first + WIDTH] for number, first in fields])
        return tap_slices_plain(taken, rows, WIDTH, place, octets)
    width = blocks[0].shape[1]

    def body(r):
        for index in range(TAPS):
            down, across, start, block = tap_at(r.active[0], index, rows, WIDTH)
            for column, (number, first) in enumerate(fields):
                values = getattr(r, BLOCK + str(number))[pl.ds(start + first, block), :].astype(F32)
                r.cols[pl.ds(index * block, block), pl.ds(column * width, width)] = shifted_field(
                    values, down, across, octets
                )

    operands = {BLOCK + str(number): block for number, block in enumerate(blocks)}
    return call(
        body,
        "columns_out",
        operands,
        {COLS_NAME: field(rows, width=len(fields) * width)},
        {},
        active=place.reshape(1).astype(jnp.int32),
        always=True,
        light=True,
    )[COLS_NAME]


def grad_step(cols, blocks, totals):
    sides = len(cols[0])
    count = len(blocks) // len(cols)
    depth = cols[0][0].shape[1] // count

    def body(r):
        for side, part in enumerate(cols[0]):
            target = getattr(r, TOTAL + str(side))
            rows = part.shape[0]
            tile = rows // 3 if rows % 48 == 0 and rows > 128 else rows
            for start in range(0, rows, tile):
                total = getattr(r, PRIOR + str(side))[pl.ds(start, tile), :] if totals else None
                for number in range(len(blocks)):
                    factor = getattr(r, COLS + str(number // count * sides + side))
                    product = dot(
                        factor[pl.ds(start, tile), pl.ds(number % count * depth, depth)],
                        getattr(r, BLOCK + str(number))[pl.ds(depth if side == 1 else 0, depth), :],
                    )
                    total = product if total is None else total + product
                target[pl.ds(start, tile), :] = total
            r.flush(TOTAL + str(side))

    every = [part for step in cols for part in step]
    operands = {COLS + str(index): part for index, part in enumerate(every)}
    operands.update({BLOCK + str(number): block for number, block in enumerate(blocks)})
    if totals:
        operands.update({PRIOR + str(side): total for side, total in enumerate(totals)})
    outputs = {TOTAL + str(side): field(part.shape[0], F32) for side, part in enumerate(cols[0])}
    flops = 2 * sum(part.shape[0] * part.shape[1] for part in every) * WIDTH
    return list(call(body, "grad_step", operands, outputs, {}, flops=flops, light=True).values())


def last_rows(blocks, first):
    def body(r):
        copies = [
            pltpu.make_async_copy(
                getattr(r, BLOCK + str(index)).at[pl.ds(first, r.taken.shape[1])], r.landed.at[index], r.sems.at[index]
            )
            for index in range(len(blocks))
        ]
        for copy in copies:
            copy.start()
        for copy in copies:
            copy.wait()
        r.taken[...] = r.landed[...]

    operands = {BLOCK + str(index): block for index, block in enumerate(blocks)}
    taken = shape((len(blocks), blocks[0].shape[0] - first, blocks[0].shape[1]), blocks[0].dtype)
    scratch = {"sems": pltpu.SemaphoreType.DMA((len(blocks),)), "landed": pltpu.VMEM(taken.shape, taken.dtype)}
    return call(body, "last_rows", operands, {TAKEN: taken}, scratch, far=operands)[TAKEN]


class Doubling:
    def __init__(self, value, axis):
        self.axis, self.value, self.distance = axis, value[None], 1

    def step(self):
        count, index = lax.axis_size(self.axis), lax.axis_index(self.axis)
        if self.distance < count:
            pairs = [(i, i ^ self.distance) for i in range(count)]
            other = lax.ppermute(self.value, self.axis, pairs)
            self.value = jnp.where(
                (index // self.distance) % 2 == 0,
                jnp.concatenate([self.value, other], axis=0),
                jnp.concatenate([other, self.value], axis=0),
            )
            self.distance *= 2

    def finish(self):
        while self.distance < lax.axis_size(self.axis):
            self.step()
        return self.value


class Ring:
    def __init__(self, value, axis):
        self.axis = axis
        self.count = lax.axis_size(axis)
        self.stride = self.count // 4
        self.values, self.rows, self.steps = [value], [], []

    def send(self, value, target):
        return lax.ppermute(value, self.axis, [(i, target(i)) for i in range(self.count)])

    def around(self, value, steps=1):
        return self.send(value, lambda i: (i + steps * self.stride) % self.count)

    def besides(self, value):
        row, stride = [value], self.stride
        for _ in range(stride // 2 - 1):
            row.append(self.send(row[-1], lambda i: i // stride * stride + (i + 2) % stride))
        return row

    def with_core(self, row):
        return row + [self.send(part, lambda i: i ^ 1) for part in row]

    def turn(self):
        self.values.append(self.around(self.values[-1]))

    def spread(self):
        self.rows.append(self.besides(self.values[len(self.rows)]))

    def spread_last(self):
        stride, half = self.stride, self.values[3].shape[0] // 32 * 16
        row = [self.values[3]]
        for index in range(1, stride // 2):
            beside = self.send(row[-1][:half], lambda i: i // stride * stride + (i + 2) % stride)
            turned = self.around(self.rows[2][index][half:])
            row.append(jnp.concatenate([beside, turned], axis=0))
        self.rows.append(row)

    def share(self, step):
        self.steps.append(self.with_core(self.rows[step]))


def ring_order(axis, step):
    index, stride = lax.axis_index(axis), lax.axis_size(axis) // 4
    quarter = (index // stride + 4 - step) % 4 * stride
    sources = []
    for core in range(2):
        for beside in range(stride // 2):
            sources.append(quarter + (index % stride + stride - 2 * beside) % stride // 2 * 2 + (index + core) % 2)
    return jnp.stack(sources).astype(jnp.int32)


def together(*values):
    return lax.optimization_barrier(values)


def moved(value, source, target):
    return lax.ppermute(value, SECTION, [(source, target)])


def to_rows(value):
    micro, images, pixels, channels = value.shape
    count = micro * images
    return (
        value.reshape(count, pixels // 8, 8, channels).transpose(1, 0, 2, 3).reshape(-1, channels)
    )


def from_rows(value, images):
    count = MICRO * images
    channels = value.shape[-1]
    grid_rows = value.shape[0] // (8 * count)
    planes = value.reshape(grid_rows, count, 8, channels).transpose(1, 0, 2, 3)
    return planes.reshape(MICRO, images, grid_rows * 8, channels)


def noise_columns(pair_ids, columns):
    fraction = pair_ids.astype(F32) / (LEVELS - 1)
    top_root = SIGMA_HIGH ** (1.0 / 7.0)
    bottom_root = SIGMA_LOW ** (1.0 / 7.0)
    sigmas = (top_root + fraction * (bottom_root - top_root)) ** 7
    log_scale = 250.0 * jnp.log(sigmas)
    quarter = EMBED // 4
    kind = columns // quarter
    frequency = jnp.exp(-math.log(10000.0) * (columns % quarter).astype(F32) / quarter)
    angles = jnp.where(kind < 2, log_scale[:, :1], log_scale[:, 1:]) * frequency
    return jnp.where(kind % 2 == 0, jnp.cos(angles), jnp.sin(angles))


def block_homes(shards, rows_in):
    block = rows_in // TAPS
    per_tap = 2 * WIDTH // block
    mine = [[i for i in range(TAPS) if (TAPS * d + i) % per_tap < per_tap // 2] for d in range(shards)]
    slots = max(-(-(len(mine[d]) + len(mine[d ^ 1])) // 2) for d in range(shards))
    sent = [mine[d][slots:] for d in range(shards)]
    most = max(1, max(len(part) for part in sent))
    offers, names = [], []
    for d in range(shards):
        kept = mine[d][:slots]
        offer = kept + [TAPS + i for i in range(len(sent[d ^ 1]))]
        names.append([TAPS * d + i for i in kept] + [TAPS * (d ^ 1) + i for i in sent[d ^ 1]])
        offers.append(offer + [0] * (slots - len(offer)))
    sends = [part + [0] * (most - len(part)) for part in sent]
    return np.array(sends, np.int32), np.array(offers, np.int32), names, slots


def spans(name_rows, cuts):
    found, start = {}, 0
    for name, count in name_rows:
        found[name], first, base = [], 0, 0
        for array, height in enumerate(cuts):
            low, high = max(start, base), min(start + count, base + height)
            if low < high:
                found[name].append((array, low - base, low - start, high - low))
            base += height
        start += count
    return found


def section_weights(conv_in, conv_out, skip_proj, qkv_proj, out_proj, is_decoder):
    shards, me = lax.axis_size(DP), lax.axis_index(DP)
    qkv_parts = [qkv_proj[:, part * WIDTH : (part + 1) * WIDTH] for part in range(3)]
    small = dict(zip(SMALL, (*qkv_parts, out_proj)))
    shares = {CONV_IN: conv_in, CONV_OUT: conv_out, **small, SKIP: skip_proj}
    heights = [(name, part.shape[0]) for name, part in shares.items()]
    if any(height % 16 for _, height in heights) or conv_in.shape[0] % (TAPS * 16):
        whole = {name: lax.all_gather(part, DP, axis=0, tiled=True)[None] for name, part in shares.items()}
        sources = list(whole.values())
        plan = {name: [(index, 0, 0, 0, part.shape[1])] for index, (name, part) in enumerate(whole.items())}
        encoder_plan = dict(plan)
        encoder_plan[CONV_IN] = [(0, 0, tap * 2 * WIDTH, tap * WIDTH, WIDTH) for tap in range(TAPS)]
        return sources, encoder_plan, plan
    sends, offers, names, slots = block_homes(shards, conv_in.shape[0])
    blocks = conv_in.reshape(TAPS, -1, WIDTH)
    block = blocks.shape[1]
    other = lax.ppermute(
        jnp.take(blocks, jnp.asarray(sends)[me], axis=0), DP, [(i, i ^ 1) for i in range(shards)]
    )
    chosen = jnp.take(jnp.concatenate([blocks, other], axis=0), jnp.asarray(offers)[me], axis=0)
    encoder_parts = [chosen.reshape(slots * block, WIDTH), conv_out, *small.values()]
    encoder_rows = sum(part.shape[0] for part in encoder_parts)
    first_rows = max(encoder_rows, sum(height for name, height in heights if name not in (OUT_NAME, SKIP)))
    everything = jnp.concatenate(list(shares.values()), axis=0)
    encoder_parts.append(jnp.zeros((first_rows - encoder_rows, WIDTH), BF16))
    first = lax.all_gather(
        jnp.where(is_decoder, everything[:first_rows], jnp.concatenate(encoder_parts, axis=0)), DP, axis=0
    )
    second = lax.all_gather(everything[first_rows:], DP, axis=0)

    def plan_of(found):
        return {
            name: [
                (array, piece, row, piece * height + start, count)
                for piece in range(shards)
                for array, row, start, count in found[name]
            ]
            for name, height in heights
            if name in found
        }

    decoder_plan = plan_of(spans(heights, (first_rows, everything.shape[0] - first_rows)))
    encoder_plan = plan_of(
        spans([("blocks", slots * block)] + [item for item in heights if item[0] in (CONV_OUT, *SMALL)], (encoder_rows,))
    )
    per_tap = 2 * WIDTH // block
    encoder_plan[CONV_IN] = sorted(
        (
            (0, piece, slot * block, name // per_tap * WIDTH + name % per_tap * block, block)
            for piece in range(shards)
            for slot, name in enumerate(names[piece])
        ),
        key=lambda entry: entry[3],
    )
    return [first, second], encoder_plan, decoder_plan


def on_device(
    level_input,
    cotangent,
    class_table,
    conv_in,
    conv_out,
    embed_proj,
    skip_proj,
    qkv_proj,
    out_proj,
    gains,
    biases,
    noise_pairs,
    classes,
):
    sections = lax.axis_size(SECTION)
    section_id = lax.axis_index(SECTION)
    shards = lax.axis_size(DP)
    shard_id = lax.axis_index(DP)
    images = level_input.shape[1]
    count = MICRO * images
    octets = 8 * count
    rows = SIDE * octets

    is_decoder = section_id >= sections // 2
    skip_by_columns = sections == 2
    sources, encoder_plan, decoder_plan = section_weights(
        conv_in[0], conv_out[0], skip_proj[0], qkv_proj[0], out_proj[0], is_decoder
    )

    gain_share, bias_share = gains.shape[1], biases.shape[1]
    small = jnp.concatenate(
        [
            gains[0].astype(F32),
            biases[0].astype(F32),
            noise_pairs.reshape(-1).astype(F32),
            classes.reshape(-1).astype(F32),
        ]
    )
    spare = -small.shape[0] % LANE
    every = Doubling(jnp.pad(small, (0, spare))[None], DP).finish()[:, 0]
    cut = gain_share + bias_share
    params = jnp.concatenate(
        [every[:, :gain_share].reshape(4, WIDTH), every[:, gain_share:cut].reshape(12, WIDTH)],
        axis=0,
    )
    all_images = shards * count
    pair_ids = every[:, cut : cut + 2 * count].reshape(all_images, 2)
    class_ids = every[:, cut + 2 * count : cut + 3 * count].reshape(all_images).astype(jnp.int32)

    slice_width = class_table.shape[1]
    columns = shard_id * slice_width + jnp.arange(slice_width)[None, :]
    onehot = (class_ids[:, None] == jnp.arange(CLASSES)[None, :]).astype(BF16)
    pre = noise_columns(pair_ids, columns) + dot(onehot, class_table)
    embed_b = jax.nn.silu(pre).astype(BF16)
    shares = dot(embed_b, embed_proj[0]).astype(BF16).reshape(shards, count, 2 * WIDTH)
    modulation = lax.all_to_all(shares, DP, 0, 0).astype(F32).sum(axis=0)
    modulation = modulation + params[BIAS + 3 : BIAS + 5].reshape(1, 2 * WIDTH)
    modulation = jnp.repeat(modulation, 8, axis=0)

    level_own, top_own = to_rows(level_input), to_rows(cotangent)
    level_rows = jnp.concatenate(
        [level_own] + [moved(level_own, source, 0) for source in range(1, sections)], axis=0
    )
    top_rows = jnp.concatenate(
        [moved(top_own, source, sections - 1) for source in range(sections - 1)] + [top_own], axis=0
    )

    orders = [ring_order(DP, step) for step in range(4)]
    order = jnp.concatenate(orders)

    def in_order(values):
        return jnp.take(values.reshape(shards, count, -1), order, axis=0).reshape(all_images, -1)

    common = {
        "params": params,
        "group_of": jnp.asarray(GROUP_OF, BF16),
        "group_of_t": jnp.asarray(GROUP_OF.T, BF16),
    }
    level_rows, top_rows, modulation, embed_late, pre_late, onehot_late = together(
        level_rows, top_rows, modulation, in_order(embed_b), in_order(pre), in_order(onehot)
    )

    def weights_for(decoder, *names):
        plan = decoder_plan if decoder else encoder_plan
        used = sorted({entry[0] for name in names for entry in plan[name]})
        return [sources[index] for index in used], {
            name: [(used.index(entry[0]), *entry[1:]) for entry in plan[name]] for name in names
        }

    kept = []
    skips = {}
    hidden = level_rows
    result = None
    before = {}
    for tick in range(sections):
        decoder = tick >= sections // 2
        mirror = sections - 1 - tick
        active = (section_id == tick).astype(jnp.int32).reshape(1)
        skipped = skips[tick] if decoder else hidden
        outs = run_forward(
            decoder, sections == 2, hidden, skipped, weights_for, modulation, common, before, active
        )
        before = {"before_fields": outs[FIELDS], "before_columns_w": outs[COLUMNS_W]}
        result = outs[RESULT]
        entry = {HIDDEN: hidden, SKIPPED: skipped, STAT_S: outs[STAT_H], **outs}
        for name in (FIELDS, COLUMNS_W, RESULT, MIDDLE):
            entry.pop(name, None)
        if sections > 2 and kept:
            entry = {name: jnp.where(section_id == tick, value, kept[-1][name]) for name, value in entry.items()}
            kept = [entry] * (tick + 1)
        else:
            kept.append(entry)
        if tick < sections - 1:
            hidden = moved(result, tick, tick + 1)
            if not decoder:
                skips[mirror] = hidden if mirror == tick + 1 else moved(result, tick, mirror)

    def own(values):
        if sections > 2 and values[0] is values[-1]:
            return values[0]
        chosen = values[0]
        for tick in range(1, sections):
            chosen = jnp.where(section_id == tick, values[tick], chosen)
        return chosen

    fields = lax.all_gather(outs[FIELDS], DP, axis=0)
    circle = Ring(outs[COLUMNS_W], DP)
    columns_w, kept[-1] = together(outs[COLUMNS_W], kept[-1])
    turned = {0: columns_w}
    w_rows, w_steps = {}, {}

    def beside(stage, *values):
        if stage == 0:
            turned.update({step % 4: circle.around(turned[0], step) for step in (1, -1)})
            w_rows[0] = circle.besides(turned[0])
        if stage == 1:
            turned[2] = circle.around(turned[1])
            w_rows.update({step: circle.besides(turned[step]) for step in (1, 3)})
        if stage == 2:
            w_rows[2] = circle.besides(turned[2])
        for step in ((), (0,), (1, 3), (2,))[stage]:
            other = circle.send(jnp.concatenate(w_rows[step], axis=0), lambda i: i ^ 1)
            w_steps[step] = [*w_rows[step], other]
        state, *values = together((turned, w_rows, w_steps), *values)
        for old, new in zip((turned, w_rows, w_steps), state):
            old.update(new)
        return values

    def to_owners(value, source):
        share = rows // sections
        pieces = [value[index * share : (index + 1) * share] for index in range(sections)]
        total = jnp.where(section_id == source, pieces[source], jnp.zeros_like(pieces[source]))
        for target in range(sections):
            if target != source:
                total = total + moved(pieces[target].astype(BF16), source, target).astype(value.dtype)
        return from_rows(total, images)


    sums_of = [None] * sections
    skip_grads = {}
    grad_out = top_rows
    before = {}
    for tick in reversed(range(sections)):
        decoder = tick >= sections // 2
        mirror = sections - 1 - tick
        entry = kept[tick]
        if not decoder and tick in skip_grads:
            grad_out = grad_out.astype(F32) + skip_grads[tick].astype(F32)
        joined = decoder and mirror == tick - 1
        active = (section_id == tick).astype(jnp.int32).reshape(1)

        def backward(part, entry, decoder=decoder, joined=joined, active=active):
            return run_backward(
                decoder, joined, shards, not skip_by_columns, part, entry, weights_for, modulation, common, before, active
            )

        outs = backward(0 if tick == 0 else None, {**entry, GRAD_OUT: grad_out})
        if tick == sections - 1:
            level_output = to_owners(result, sections - 1)
            outs, level_output = beside(0, outs, level_output)
        if tick == 0:
            (outs,) = beside(1, outs)
        before = {"before_products": outs[PRODUCTS], "before_payload": outs[PAYLOAD]}
        sums_of[tick] = outs[SUMS]
        if joined:
            grad_out = moved(outs[GRAD_JOINED], tick, mirror)
        elif tick:
            if decoder:
                skip_grads[mirror] = moved(outs[GRAD_SKIPPED].astype(BF16), tick, mirror)
            grad_out = moved(outs[GRAD_HIDDEN].astype(BF16), tick, tick - 1)
    products, payload = outs[PRODUCTS], outs[PAYLOAD]

    affine = jnp.stack([params[GAIN : GAIN + 2].reshape(-1), params[BIAS : BIAS + 2].reshape(-1)], axis=1)

    def cols_in_of(step):
        return columns_in(
            fields,
            orders[step],
            affine,
            conv_in.shape[1],
            skip_proj.shape[1],
            shard_id,
            is_decoder,
            octets,
            sections == 2,
        )

    def with_out(step, others):
        return [columns_out(w_steps[step], conv_out.shape[1], shard_id, octets), *others]

    ring = Ring(payload, DP)
    cols = []

    small_grads = lax.psum_scatter(products, DP, scatter_dimension=0, tiled=True)
    ring.turn()
    ring.spread()
    last = backward(1, {**entry, **outs})
    cols.append(cols_in_of(0))
    ring.values, ring.rows, fields, cols, sums_of[0], input_rows = beside(
        2, ring.values, ring.rows, fields, cols, sums_of[0] + last[SUMS], last[GRAD_HIDDEN]
    )
    sums = own(sums_of)
    shares = jnp.concatenate([sums[:4].reshape(shards, gain_share), sums[4:].reshape(shards, bias_share)], axis=1)
    summed = lax.all_to_all(shares, DP, 0, 0, tiled=True).sum(axis=0)
    ring.turn()
    ring.spread()
    ring.share(0)
    cols = [with_out(0, cols[0]), with_out(1, cols_in_of(1))]
    ring.values, ring.rows, ring.steps, cols, fields, input_rows, summed = beside(
        3, ring.values, ring.rows, ring.steps, cols, fields, input_rows, summed
    )
    ring.turn()
    ring.spread()
    ring.share(1)
    cols += [with_out(step, cols_in_of(step)) for step in (2, 3)]
    ring.values, ring.rows, ring.steps, cols, input_rows = together(
        ring.values, ring.rows, ring.steps, cols, input_rows
    )
    ring.spread_last()
    ring.share(2)
    input_grad = to_owners(input_rows, 0)
    totals = grad_step(cols[:2], ring.steps[0] + ring.steps[1], None)
    ring.rows, ring.steps, cols, totals, input_grad, small_grads = together(
        ring.rows, ring.steps, cols, totals, input_grad, small_grads
    )
    small_grads = small_grads.astype(F32)
    qkv_grad = small_grads[:, : 3 * WIDTH]
    out_grad = small_grads[:, 3 * WIDTH : 4 * WIDTH]
    ring.share(3)
    totals = grad_step(cols[2:], ring.steps[2] + ring.steps[3], totals)
    conv_out_grad, conv_in_grad = totals[:2]
    gains_grad, biases_grad = summed[:gain_share], summed[gain_share:]

    mods = last_rows([block for step in ring.steps for block in step], 2 * rows)
    mods = jnp.concatenate(
        [mods[:, start : start + count].reshape(all_images, WIDTH) for start in (0, count)], axis=1
    )
    embed_grad = dot_tn(embed_late, mods)
    grad_embed = dot_nt(mods, embed_proj[0])
    if sections == 2:
        grad_embed = grad_embed + lax.ppermute(grad_embed, SECTION, [(0, 1), (1, 0)])
    else:
        grad_embed = lax.psum(grad_embed, SECTION)
    grad_pre = jax.vjp(jax.nn.silu, pre_late)[1](grad_embed)[0]
    table_grad = lax.dot_general(
        onehot_late.astype(F32),
        grad_pre,
        (((0,), (0,)), ((), ())),
        precision=lax.Precision.HIGHEST,
        preferred_element_type=F32,
    )

    if skip_by_columns:
        skip_grad = totals[2]
    else:
        skip_grad = jnp.concatenate(
            [small_grads[:, 4 * WIDTH : 5 * WIDTH], small_grads[:, 5 * WIDTH :]], axis=0
        )
    return (
        level_output,
        input_grad,
        table_grad,
        conv_in_grad[None],
        conv_out_grad[None],
        embed_grad[None],
        skip_grad[None],
        qkv_grad[None],
        out_grad[None],
        gains_grad[None],
        biases_grad[None],
    )


def solution(mesh):
    placed = (
        P(None, DP, SECTION, None),
        P(None, DP, SECTION, None),
        P(None, DP),
        P(SECTION, DP, None),
        P(SECTION, DP, None),
        P(SECTION, DP, None),
        P(SECTION, DP, None),
        P(SECTION, DP, None),
        P(SECTION, DP, None),
        P(SECTION, DP),
        P(SECTION, DP),
        P(None, DP, None),
        P(None, DP),
    )
    return jax.shard_map(
        on_device,
        mesh=mesh,
        in_specs=placed,
        out_specs=(
            P(None, DP, SECTION, None),
            P(None, DP, SECTION, None),
            P(None, DP),
            P(SECTION, DP, None),
            P(SECTION, DP, None),
            P(SECTION, DP, None),
            P(SECTION, DP, None),
            P(SECTION, DP, None),
            P(SECTION, DP, None),
            P(SECTION, DP),
            P(SECTION, DP),
        ),
        check_vma=False,
    )
```

```python
import math
from functools import partial

import jax
import jax.numpy as jnp
import numpy as np
from jax import lax
from jax.experimental import pallas as pl
from jax.experimental.pallas import tpu as pltpu
from jax.sharding import PartitionSpec as P

WIDTH = 768
EMBED = 768
CLASSES = 1000
HEAD_DIM = 64
GROUPS = 32
SIDE = 8
LEVELS = 40
MICRO = 4
PIXELS = 64
TAPS = 9

EPS = 1e-05
SIGMA_LOW = 0.002
SIGMA_HIGH = 80.0

ACTIVE = "active"
ATTEND = "attend"
BEFORE = "before_"
BLOCK = "block_"
COLS_NAME = "cols"
COLS = "cols_"
COLUMNS_W = "columns_w"
CONV_IN = "conv_in"
CONV_ONE = "conv_one"
CONV_OUT = "conv_out"
DP = "dp"
FIELDS = "fields"
GRAD_HIDDEN = "grad_hidden"
GRAD_JOINED = "grad_joined"
GRAD_OUT = "grad_out"
GRAD_RESID = "grad_resid"
GRAD_RESID_B = "grad_resid_b"
GRAD_SKIPPED = "grad_skipped"
HELD = "held_"
HIDDEN = "hidden"
KEY = "key"
MIDDLE = "middle"
MIXED = "mixed"
MODULATION = "modulation"
OUT_NAME = "out"
OUT = "out_"
OUT_SEMS = "out_sems"
PAYLOAD = "payload"
PLANES = "planes"
PRIOR = "prior_"
PRODUCTS = "products"
PROJECT = "project"
QUERY = "query"
RESIDUAL = "residual"
RESULT = "result"
SECTION = "section"
SKIP = "skip"
SKIPPED = "skipped"
SOURCE = "source_"
STAT_C = "stat_c"
STAT_H = "stat_h"
STAT_R = "stat_r"
STAT_S = "stat_s"
SUMS = "sums"
TAKEN = "taken"
TOTAL = "total_"
VALUE = "value"

F32 = jnp.float32
BF16 = jnp.bfloat16
LANE = 128
CHUNKS = WIDTH // LANE
PER_GROUP = WIDTH // GROUPS
GROUP_SHARE = 1.0 / (PER_GROUP * PIXELS)
VMEM_LIMIT = 60 * 2**20

GAIN = 0
BIAS = 4

GROUP_OF = (np.arange(WIDTH)[:, None] // PER_GROUP == np.arange(LANE)[None, :]).astype(np.float32)


def lanes(chunk):
    return pl.ds(chunk * LANE, LANE)


def dot(left, right):
    return jnp.dot(left, right, preferred_element_type=F32)


def dot_nt(left, right):
    return lax.dot_general(left, right, (((1,), (1,)), ((), ())), preferred_element_type=F32)


def dot_tn(left, right):
    return lax.dot_general(left, right, (((0,), (0,)), ((), ())), preferred_element_type=F32)


def octet_sum(values, octets):
    width = values.shape[-1]
    partial_sums = values.reshape(SIDE, octets, width).sum(axis=0).reshape(octets // 8, 8, width)
    totals = jnp.sum(partial_sums, axis=1, keepdims=True)
    return jnp.broadcast_to(totals, partial_sums.shape).reshape(octets, width)


def over_rows(stat):
    octets, width = stat.shape
    return jnp.broadcast_to(stat[None], (SIDE, octets, width)).reshape(SIDE * octets, width)


def in_parts(values):
    first = values.astype(BF16)
    rest = values - first.astype(F32)
    second = rest.astype(BF16)
    third = (rest - second.astype(F32)).astype(BF16)
    return jnp.concatenate([first, second, third], axis=0)


def group_mean(sums, group_of, group_of_t):
    count = sums.shape[0]
    grouped = dot(in_parts(sums), group_of)
    grouped = (grouped[:count] + grouped[count : 2 * count] + grouped[2 * count :]) * GROUP_SHARE
    spread = dot(in_parts(grouped), group_of_t)
    return spread[:count] + spread[count : 2 * count] + spread[2 * count :]


def norm_stats(read, octets, group_of, group_of_t):
    sums = jnp.concatenate([octet_sum(read(c), octets) for c in range(CHUNKS)], axis=1)
    mean = group_mean(sums, group_of, group_of_t)
    squares = []
    for c in range(CHUNKS):
        centered = read(c) - over_rows(mean[:, c * LANE : (c + 1) * LANE])
        squares.append(octet_sum(centered * centered, octets))
    spread = group_mean(jnp.concatenate(squares, axis=1), group_of, group_of_t)
    return mean, lax.rsqrt(spread + EPS)


def normed_chunk(values, stat_ref, c):
    mean = stat_ref[0, :, lanes(c)]
    inv = stat_ref[1, :, lanes(c)]
    return (values - over_rows(mean)) * over_rows(inv)


def sigmoid(values):
    return 1.0 / (1.0 + jnp.exp(-values))


def silu_slope(values):
    gate = sigmoid(values)
    return gate * (1.0 + values * (1.0 - gate))


def put_shifted(planes, base, values, c, octets):
    rows = values.shape[0]
    column = lax.broadcasted_iota(jnp.int32, values.shape, 0) & 7
    before = jnp.where(column != 0, pltpu.roll(values, 1, 0), 0.0)
    after = jnp.where(column != 7, pltpu.roll(values, rows - 1, 0), 0.0)
    planes[base, pl.ds(octets, rows), lanes(c)] = before.astype(BF16)
    planes[base + 1, pl.ds(octets, rows), lanes(c)] = values.astype(BF16)
    planes[base + 2, pl.ds(octets, rows), lanes(c)] = after.astype(BF16)


def clear_edges(planes, octets):
    count, rows, width = planes.shape
    edge = jnp.zeros((count, octets, width), BF16)
    planes[:, pl.ds(0, octets), :] = edge
    planes[:, pl.ds(rows - octets, octets), :] = edge


def row_total(values):
    return jnp.sum(values, axis=0, keepdims=True)


def norm_back(read_grad, read_normed, gain_of, stat_ref, octets, tables, write, sums_out):
    group_of, group_of_t = tables
    first, second = [], []
    for c in range(CHUNKS):
        grad = read_grad(c)
        first.append(octet_sum(grad, octets))
        second.append(octet_sum(grad * read_normed(c), octets))
    first = jnp.concatenate(first, axis=1)
    second = jnp.concatenate(second, axis=1)
    sums_out(first, second)
    gain = gain_of(None)
    both = group_mean(jnp.concatenate([first * gain, second * gain], axis=0), group_of, group_of_t)
    for c in range(CHUNKS):
        part = slice(c * LANE, (c + 1) * LANE)
        inv = over_rows(stat_ref[1, :, lanes(c)])
        mean_one = over_rows(both[:octets, part])
        mean_two = over_rows(both[octets:, part])
        write(c, inv * (gain_of(c) * read_grad(c) - mean_one - read_normed(c) * mean_two))


class Weights:
    def __init__(self, sources, plan, sems):
        self.sources, self.plan, self.sems, self.waits, self.used = sources, plan, sems, {}, 0

    def fetch(self, name, held):
        self.waits[name] = []
        for source, piece, row, target, count in self.plan[name]:
            copy = pltpu.make_async_copy(
                self.sources[source].at[piece, pl.ds(row, count)],
                held.at[pl.ds(target, count)],
                self.sems.at[self.used],
            )
            copy.start()
            self.used += 1
            self.waits[name].append([target, copy])

    def need(self, name, stop):
        for entry in self.waits[name]:
            if entry[0] < stop and entry[1] is not None:
                entry[1].wait()
                entry[1] = None


def copies_of(plan, *names):
    return pltpu.SemaphoreType.DMA((sum(len(plan[name]) for name in names),))


SMALL = (QUERY, KEY, VALUE, OUT_NAME)


def held_at(r, name):
    if name in SMALL[:3]:
        return r.held_qkv.at[SMALL.index(name)]
    return getattr(r, HELD + name)


def held_scratch(decoder, names):
    sizes = {CONV_IN: (1 + decoder) * TAPS * WIDTH, CONV_OUT: TAPS * WIDTH, OUT_NAME: WIDTH, SKIP: 2 * WIDTH}
    scratch = {HELD + name: pltpu.VMEM((sizes[name], WIDTH), BF16) for name in names if name in sizes}
    if QUERY in names:
        scratch["held_qkv"] = pltpu.VMEM((3, WIDTH, WIDTH), BF16)
    return scratch


def tap_loop(body):
    def one(tap, carry):
        body(tap, lax.div(tap, 3), lax.rem(tap, 3))
        return carry

    lax.fori_loop(0, TAPS, one, 0)


def plane_rows(planes, plane, down, octets, rows):
    return planes[plane, pl.ds(pl.multiple_of(octets * down, 16), rows), :]


def head_pair(values, left):
    zero = jnp.zeros_like(values)
    return jnp.concatenate([jnp.where(left, values, zero), jnp.where(left, zero, values)], axis=0)


def attention_of(keys, queries):
    scores = [dot_nt(k, q) * (1.0 / math.sqrt(HEAD_DIM)) for k, q in zip(keys, queries)]
    tops = [jnp.max(part, axis=0, keepdims=True) for part in scores]
    weights = [jnp.exp(part - top) for part, top in zip(scores, tops)]
    totals = [1.0 / jnp.sum(part, axis=0, keepdims=True) for part in weights]
    return [part * total for part, total in zip(weights, totals)]


AT_ONCE = 4


def image_groups(images):
    every = [(image, pl.ds(image * PIXELS, PIXELS), pair) for image in range(images) for pair in range(CHUNKS)]
    return [every[start : start + AT_ONCE * CHUNKS] for start in range(0, len(every), AT_ONCE * CHUNKS)]


def by_image(scratch, image, chunk):
    part = scratch[:, image, :, lanes(chunk)]
    return part.reshape(PIXELS, LANE)


def put_image(scratch, image, chunk, values):
    scratch[:, image, :, lanes(chunk)] = values.reshape(SIDE, 8, LANE)


def conv_in_forward(r, decoder, shared, octets):
    rows = r.hidden.shape[0]
    tables = (r.group_of[...], r.group_of_t[...])
    sides = [(r.hidden, r.stat_h, 0)] + ([(r.skipped, r.stat_s, 1)] if decoder else [])
    span = WIDTH * len(sides)
    clear_edges(r.planes, octets)
    for source, stat, which in sides:
        mean, inv = norm_stats(lambda c: source[:, lanes(c)].astype(F32), octets, *tables)
        stat[0] = mean
        stat[1] = inv
        if shared and not which:
            for index, values in enumerate((mean, 1.0 / inv)):
                grouped = dot(values.astype(BF16), tables[0]) * (1.0 / PER_GROUP)
                r.turned[pl.ds(WIDTH + index * GROUPS, GROUPS), :] = over_rows(grouped).T[:GROUPS].astype(BF16)
        for c in range(CHUNKS):
            normed = normed_chunk(source[:, lanes(c)].astype(F32), stat, c)
            value = (
                normed * r.params[pl.ds(GAIN + which, 1), lanes(c)]
                + r.params[pl.ds(BIAS + which, 1), lanes(c)]
            )
            value = value * sigmoid(value)
            put_shifted(r.planes, 3 * which, value, c, octets)
            if not (shared and which):
                r.turned[pl.ds(which * WIDTH + c * LANE, LANE), :] = normed.T.astype(BF16)
    if decoder:
        r.conv_one[...] = jnp.broadcast_to(r.params[pl.ds(BIAS + 2, 1), :], r.conv_one.shape)
    for down in range(3 if decoder else 0):
        r.weights.need(CONV_IN, 3 * (down + 1) * span)

        def one_tap(across, carry, down=down):
            for half in range(len(sides)):
                first = pl.multiple_of((3 * down + across) * span + half * WIDTH, WIDTH)
                values = r.planes[3 * half + across, pl.ds(octets * down, rows), :]
                r.conv_one[...] += dot(values, r.held_conv_in[pl.ds(first, WIDTH), :])
            return carry

        lax.fori_loop(0, 3, one_tap, 0)
    for tap in range(0 if decoder else TAPS):
        r.weights.need(CONV_IN, (tap + 1) * span)
        for half in range(len(sides)):
            part = dot(
                r.planes[3 * half + tap % 3, pl.ds(octets * (tap // 3), rows), :],
                r.held_conv_in[pl.ds(tap * span + half * WIDTH, WIDTH), :],
            )
            if tap == 0 and half == 0:
                r.conv_one[...] = part + r.params[pl.ds(BIAS + 2, 1), :]
            else:
                r.conv_one[...] += part
    r.flush(CONV_ONE)
    mean, inv = norm_stats(lambda c: r.conv_one[:, lanes(c)], octets, *tables)
    r.stat_c[0] = mean
    r.stat_c[1] = inv
    for c in range(CHUNKS):
        normed = (
            normed_chunk(r.conv_one[:, lanes(c)], r.stat_c, c) * r.params[pl.ds(GAIN + 2, 1), lanes(c)]
            + r.params[pl.ds(BIAS + 5, 1), lanes(c)]
        )
        scale = over_rows(r.modulation[:, lanes(c)])
        shift = over_rows(r.modulation[:, lanes(CHUNKS + c)])
        value = normed * (1.0 + scale) + shift
        value = value * sigmoid(value)
        r.middle[:, lanes(c)] = value.astype(BF16)
        r.turned_w[lanes(c), :] = value.T.astype(BF16)
    r.flush(MIDDLE, STAT_C)
    r.leave(r.turned, r.fields, r.fields_sems.at[0])
    r.leave(r.turned_w, r.columns_w, r.fields_sems.at[1])


def block_forward(r, decoder, octets):
    rows = r.hidden.shape[0]
    images = octets // 8
    tables = (r.group_of[...], r.group_of_t[...])
    clear_edges(r.planes, octets)
    for c in range(CHUNKS):
        put_shifted(r.planes, 0, r.middle[:, lanes(c)].astype(F32), c, octets)
    if not decoder:
        r.weights.need(CONV_OUT, TAPS * WIDTH)
        r.residual[...] = jnp.broadcast_to(r.params[pl.ds(BIAS + 6, 1), :], r.residual.shape)

        def one_tap(tap, down, across):
            weights = r.held_conv_out[pl.ds(pl.multiple_of(tap * WIDTH, WIDTH), WIDTH), :]
            r.residual[...] += dot(plane_rows(r.planes, across, down, octets, rows), weights)

        tap_loop(one_tap)
    for tap in range(TAPS if decoder else 0):
        r.weights.need(CONV_OUT, (tap + 1) * WIDTH)
        part = dot(
            r.planes[tap % 3, pl.ds(octets * (tap // 3), rows), :], r.held_conv_out[pl.ds(tap * WIDTH, WIDTH), :]
        )
        if tap == 0:
            r.residual[...] = part + r.params[pl.ds(BIAS + 6, 1), :]
        else:
            r.residual[...] += part
    if decoder:
        r.weights.need(SKIP, 2 * WIDTH)
        r.residual[...] += (
            dot(r.hidden[...], r.held_skip[pl.ds(0, WIDTH), :])
            + dot(r.skipped[...], r.held_skip[pl.ds(WIDTH, WIDTH), :])
            + r.params[pl.ds(BIAS + 7, 1), :]
        )
    else:
        r.residual[...] += r.hidden[...].astype(F32)
    r.flush(RESIDUAL)
    mean, inv = norm_stats(lambda c: r.residual[:, lanes(c)], octets, *tables)
    r.stat_r[0] = mean
    r.stat_r[1] = inv
    for c in range(CHUNKS):
        r.attend[:, lanes(c)] = (
            normed_chunk(r.residual[:, lanes(c)], r.stat_r, c) * r.params[pl.ds(GAIN + 3, 1), lanes(c)]
            + r.params[pl.ds(BIAS + 8, 1), lanes(c)]
        ).astype(BF16)
    r.flush(ATTEND)
    for index, (name, bias) in enumerate(((QUERY, 9), (KEY, None), (VALUE, 10))):
        r.weights.need(name, WIDTH)
        part = dot(r.attend[...], r.held_qkv[index])
        if bias is not None:
            part = part + r.params[pl.ds(BIAS + bias, 1), :]
        part = part.reshape(SIDE, images, 8, WIDTH)
        for image in range(images):
            own = part[:, image].reshape(PIXELS, WIDTH).astype(BF16)
            r.project[pl.ds(image * PIXELS, PIXELS), pl.ds(index * WIDTH, WIDTH)] = own
    r.flush(PROJECT)
    left = lax.broadcasted_iota(jnp.int32, (PIXELS, LANE), 1) < HEAD_DIM
    for group in image_groups(images):
        queries = [head_pair(r.project[span, lanes(pair)], left) for _, span, pair in group]
        keys_h = [r.project[span, lanes(CHUNKS + pair)] for _, span, pair in group]
        values_h = [r.project[span, lanes(2 * CHUNKS + pair)] for _, span, pair in group]
        attention = [part.astype(BF16) for part in attention_of(keys_h, queries)]
        both = [dot_tn(part, values) for part, values in zip(attention, values_h)]
        for (image, _, pair), part in zip(group, both):
            put_image(r.grid, image, pair, jnp.where(left, part[:PIXELS], part[PIXELS:]))
    r.mixed[...] = r.grid[:, :, :, pl.ds(0, WIDTH)].reshape(rows, WIDTH).astype(BF16)
    r.flush(MIXED)
    r.weights.need(OUT_NAME, WIDTH)
    r.result[...] = (
        r.residual[...] + dot(r.mixed[...], r.held_out[...]) + r.params[pl.ds(BIAS + 11, 1), :]
    ).astype(BF16)


def attention_backward(r, decoder, octets, shards, with_skip):
    rows = r.residual.shape[0]
    images = octets // 8
    tables = (r.group_of[...], r.group_of_t[...])

    def put_sum(row, c, values):
        r.sums[pl.ds(row, 1), lanes(c)] = row_total(values)

    def leave(first, width):
        part = pl.ds(first * WIDTH, width * WIDTH)
        r.leave(r.built.at[:, part], r.products.at[:, part], r.built_sems.at[min(first, 2)])

    top = r.grad_out[...].astype(BF16)
    for c in range(CHUNKS):
        put_sum(BIAS + 11, c, r.grad_out[:, lanes(c)].astype(BF16).astype(F32))
    r.built[:, pl.ds(3 * WIDTH, WIDTH)] = dot_tn(r.mixed[...], top).astype(BF16)
    leave(3, 1)
    r.weights.need(OUT_NAME, WIDTH)
    r.grid[:, :, :, pl.ds(0, WIDTH)] = dot_nt(top, r.held_out[...]).reshape(SIDE, images, 8, WIDTH)
    left = lax.broadcasted_iota(jnp.int32, (PIXELS, LANE), 1) < HEAD_DIM
    root = 1.0 / math.sqrt(HEAD_DIM)
    for group in image_groups(images):
        queries = [head_pair(r.project[span, lanes(pair)], left) for _, span, pair in group]
        keys_h = [r.project[span, lanes(CHUNKS + pair)] for _, span, pair in group]
        values_h = [r.project[span, lanes(2 * CHUNKS + pair)] for _, span, pair in group]
        grads_h = [head_pair(by_image(r.grid, image, pair).astype(BF16), left) for image, _, pair in group]
        attention = attention_of(keys_h, queries)
        weighted = [dot_nt(v, g) * part for v, g, part in zip(values_h, grads_h, attention)]
        totals = [jnp.sum(part, axis=0, keepdims=True) for part in weighted]
        scores = [(w - part * total).astype(BF16) for w, part, total in zip(weighted, attention, totals)]
        both = [dot_tn(part, k) * root for part, k in zip(scores, keys_h)]
        grad_keys = [dot(part, q) * root for part, q in zip(scores, queries)]
        grad_values = [dot(part.astype(BF16), g) for part, g in zip(attention, grads_h)]
        for index, (image, _, pair) in enumerate(group):
            put_image(r.grid, image, pair, jnp.where(left, both[index][:PIXELS], both[index][PIXELS:]))
            put_image(r.grid, image, CHUNKS + pair, grad_keys[index])
            put_image(r.grid, image, 2 * CHUNKS + pair, grad_values[index])
    for index in range(3):
        for pair in range(CHUNKS):
            chunk = lanes(index * CHUNKS + pair)
            joined = r.grid[:, :, :, chunk].reshape(rows, LANE).astype(BF16)
            r.grad_project[:, chunk] = joined
            if index == 0:
                put_sum(BIAS + 9, pair, joined.astype(F32))
            if index == 2:
                put_sum(BIAS + 10, pair, joined.astype(F32))
    for index in range(3):
        columns = pl.ds(index * WIDTH, WIDTH)
        r.built[:, columns] = dot_tn(r.attend[...], r.grad_project[:, columns]).astype(BF16)
    leave(0, 3)
    for index, name in enumerate(SMALL[:3]):
        r.weights.need(name, WIDTH)
        part = dot_nt(r.grad_project[:, pl.ds(index * WIDTH, WIDTH)], r.held_qkv[index])
        if index == 0:
            r.work[...] = part
        else:
            r.work[...] += part

    def gain_attend(c):
        return r.params[pl.ds(GAIN + 3, 1), :] if c is None else r.params[pl.ds(GAIN + 3, 1), lanes(c)]

    def sums_attend(first, second):
        r.sums[pl.ds(BIAS + 8, 1), :] = row_total(first) * 0.125
        r.sums[pl.ds(GAIN + 3, 1), :] = row_total(second) * 0.125

    def write_resid(c, grad):
        total = r.grad_out[:, lanes(c)].astype(F32) + grad
        r.grad_resid[:, lanes(c)] = total
        rounded = total.astype(BF16)
        r.grad_resid_b[:, lanes(c)] = rounded
        rounded = rounded.astype(F32)
        put_sum(BIAS + 6, c, rounded)
        if decoder:
            put_sum(BIAS + 7, c, rounded)

    norm_back(
        lambda c: r.work[:, lanes(c)],
        lambda c: normed_chunk(r.residual[:, lanes(c)], r.stat_r, c),
        gain_attend,
        r.stat_r,
        octets,
        tables,
        write_resid,
        sums_attend,
    )
    r.flush(GRAD_RESID, GRAD_RESID_B)
    if with_skip:
        share = WIDTH // shards
        for side, source in enumerate((r.hidden, r.skipped)):
            first = side * shards // 2
            if decoder:
                part = dot_tn(source[...], r.grad_resid_b[...]).astype(BF16)
            else:
                part = jnp.zeros((WIDTH, WIDTH), BF16)
            for index in range(shards // 2):
                target = pl.ds((first + index) * share, share)
                for half in range(2):
                    r.built[target, pl.ds((4 + half) * WIDTH, WIDTH)] = part[
                        (2 * index + half) * share : (2 * index + half + 1) * share
                    ]
        part = pl.ds(4 * WIDTH, 2 * WIDTH)
        r.leave(r.built.at[:, part], r.products.at[:, part], r.built_sems.at[1])


def middle_backward(r, octets):
    rows = r.conv_one.shape[0]
    tables = (r.group_of[...], r.group_of_t[...])
    clear_edges(r.planes, octets)
    r.rows[pl.ds(0, rows), :] = r.grad_resid_b[...]
    for c in range(CHUNKS):
        put_shifted(r.planes, 0, r.grad_resid_b[:, lanes(c)].astype(F32), c, octets)
    r.weights.need(CONV_OUT, TAPS * WIDTH)
    r.work[...] = jnp.zeros(r.work.shape, F32)

    def one_tap(tap, down, across):
        weights = r.held_conv_out[pl.ds(pl.multiple_of(tap * WIDTH, WIDTH), WIDTH), :]
        r.work[...] += dot_nt(plane_rows(r.planes, 2 - across, 2 - down, octets, rows), weights)

    tap_loop(one_tap)
    for c in range(CHUNKS):
        normed = (
            normed_chunk(r.conv_one[:, lanes(c)], r.stat_c, c) * r.params[pl.ds(GAIN + 2, 1), lanes(c)]
            + r.params[pl.ds(BIAS + 5, 1), lanes(c)]
        )
        scale = over_rows(r.modulation[:, lanes(c)])
        shift = over_rows(r.modulation[:, lanes(CHUNKS + c)])
        r.work[:, lanes(c)] = r.work[:, lanes(c)] * silu_slope(normed * (1.0 + scale) + shift)

    def gain_middle(c):
        if c is None:
            return r.params[pl.ds(GAIN + 2, 1), :] * (1.0 + r.modulation[:, pl.ds(0, WIDTH)])
        return over_rows(r.params[pl.ds(GAIN + 2, 1), lanes(c)] * (1.0 + r.modulation[:, lanes(c)]))

    def sums_middle(first, second):
        scaled = 1.0 + r.modulation[:, pl.ds(0, WIDTH)]
        r.sums[pl.ds(BIAS + 5, 1), :] = row_total(first * scaled) * 0.125
        r.sums[pl.ds(GAIN + 2, 1), :] = row_total(second * scaled) * 0.125
        grad_scale = (
            r.params[pl.ds(GAIN + 2, 1), :] * second + r.params[pl.ds(BIAS + 5, 1), :] * first
        ).astype(BF16)
        grad_shift = first.astype(BF16)
        images = octets // 8
        row = lax.broadcasted_iota(jnp.int32, (16, octets), 0)
        column = lax.broadcasted_iota(jnp.int32, (16, octets), 1)
        for index, part in enumerate((grad_scale, grad_shift)):
            taken = ((row - index * images) * 8 == column) & (row >= index * images)
            chosen = dot(jnp.where(taken, 1.0, 0.0).astype(BF16), part)
            compact = chosen if index == 0 else compact + chosen
        r.rows[pl.ds(2 * rows, 16), :] = compact.astype(BF16)
        r.sums[pl.ds(BIAS + 3, 1), :] = row_total(grad_scale.astype(F32)) * 0.125
        r.sums[pl.ds(BIAS + 4, 1), :] = row_total(grad_shift.astype(F32)) * 0.125

    def write_conv(c, grad):
        rounded = grad.astype(BF16)
        r.grad_conv_b[:, lanes(c)] = rounded
        r.rows[pl.ds(rows, rows), lanes(c)] = rounded
        r.sums[pl.ds(BIAS + 2, 1), lanes(c)] = row_total(rounded.astype(F32))

    norm_back(
        lambda c: r.work[:, lanes(c)],
        lambda c: normed_chunk(r.conv_one[:, lanes(c)], r.stat_c, c),
        gain_middle,
        r.stat_c,
        octets,
        tables,
        write_conv,
        sums_middle,
    )
    r.leave(r.rows, r.payload, r.payload_sem)


def conv_in_backward(r, decoder, joined, octets, prefetched):
    rows = r.hidden.shape[0]
    tables = (r.group_of[...], r.group_of_t[...])
    sides = [(r.hidden, r.stat_h, r.total if joined else r.grad_hidden, 0)]
    if decoder:
        sides.append((r.skipped, r.stat_s, r.total if joined else r.grad_skipped, 1))
    span = WIDTH * len(sides)
    clear_edges(r.planes, octets)
    for c in range(CHUNKS):
        put_shifted(r.planes, 0, r.grad_conv_b[:, lanes(c)].astype(F32), c, octets)
    if prefetched:
        r.weights.need(CONV_IN, TAPS * span)
        r.sides[...] = jnp.zeros(r.sides.shape, F32)

        def one_tap(tap, down, across):
            values = plane_rows(r.planes, 2 - across, 2 - down, octets, rows)
            for half in range(len(sides)):
                first = pl.multiple_of(tap * span + half * WIDTH, WIDTH)
                r.sides[half] += dot_nt(values, r.held_conv_in[pl.ds(first, WIDTH), :])

        tap_loop(one_tap)
    for tap in range(0 if prefetched else TAPS):
        r.weights.need(CONV_IN, (tap + 1) * span)
        for _, _, _, half in sides:
            part = dot_nt(
                r.planes[2 - tap % 3, pl.ds(octets * (2 - tap // 3), rows), :],
                r.held_conv_in[pl.ds(tap * span + half * WIDTH, WIDTH), :],
            )
            if tap == 0:
                r.sides[half] = part
            else:
                r.sides[half] += part
    if decoder:
        r.weights.need(SKIP, 2 * WIDTH)
    for source, stat, target, which in sides:

        def normed_of(c, source=source, stat=stat):
            return normed_chunk(source[:, lanes(c)].astype(F32), stat, c)

        def gain_input(c, which=which):
            row = pl.ds(GAIN + which, 1)
            return r.params[row, :] if c is None else r.params[row, lanes(c)]

        for c in range(CHUNKS):
            value = normed_of(c) * gain_input(c) + r.params[pl.ds(BIAS + which, 1), lanes(c)]
            r.sides[which, :, lanes(c)] = r.sides[which, :, lanes(c)] * silu_slope(value)

        def sums_input(first, second, which=which):
            r.sums[pl.ds(BIAS + which, 1), :] = row_total(first) * 0.125
            r.sums[pl.ds(GAIN + which, 1), :] = row_total(second) * 0.125

        if decoder:
            part = dot_nt(r.grad_resid_b[...], r.held_skip[pl.ds(which * WIDTH, WIDTH), :])
            if joined and which:
                target[...] += part
            else:
                target[...] = part

        def write_input(c, grad, target=target):
            if decoder:
                target[:, lanes(c)] += grad
            else:
                target[:, lanes(c)] = grad + r.grad_resid[:, lanes(c)]

        norm_back(
            lambda c, which=which: r.sides[which, :, lanes(c)],
            normed_of,
            gain_input,
            stat,
            octets,
            tables,
            write_input,
            sums_input,
        )
    if joined:
        r.grad_joined[...] = r.total[...].astype(BF16)


def shape(dims, kind):
    return jax.ShapeDtypeStruct(dims, kind)


IN_VMEM = pl.BlockSpec(memory_space=pltpu.VMEM)
IN_HBM = pl.BlockSpec(memory_space=pl.ANY)
IN_SMEM = pl.BlockSpec(memory_space=pltpu.SMEM)


class Refs:
    def __init__(self, refs, targets):
        self.__dict__.update(refs)
        self._targets, self._leaving = targets, []

    def leave(self, source, target, sem):
        self._leaving.append(pltpu.make_async_copy(source, target, sem))
        self._leaving[-1].start()

    def flush(self, *names):
        for name in names:
            if name in self._targets:
                self.leave(getattr(self, name), *self._targets.pop(name))

    def finish(self):
        self.flush(*list(self._targets))
        for copy in self._leaving:
            copy.wait()


def call(body, name, operands, outputs, scratch, weights=None, order=(), active=None, far=(), flops=0, always=False, light=False):
    sources, plan = weights if weights is not None else ([], {})
    scratch = dict(scratch)
    if order:
        scratch["fetched"] = pltpu.SemaphoreType.DMA((sum(len(plan[part]) for part in order),))
    ins = [key for key in operands if key not in far and not key.startswith(BEFORE)]
    outs = [key for key in outputs if key not in far]
    for key in outs:
        scratch[OUT + key] = pltpu.VMEM(outputs[key].shape, outputs[key].dtype)
    scratch[OUT_SEMS] = pltpu.SemaphoreType.DMA((max(len(outs), 1),))
    names = [*operands, *(SOURCE + str(index) for index in range(len(sources)))]
    names += ([ACTIVE] if active is not None else []) + [*outputs, *scratch]
    moved = sum(int(np.prod(v.shape)) * v.dtype.itemsize for v in (*operands.values(), *outputs.values()))

    def kernel(*refs):
        refs = dict(zip(names, refs))

        def run():
            targets = {}
            for index, key in enumerate(outs):
                targets[key] = (refs[key], refs[OUT_SEMS].at[index])
                refs[key] = refs[OUT + key]
            r = Refs(refs, targets)
            if order:
                r.weights = Weights([getattr(r, SOURCE + str(index)) for index in range(len(sources))], plan, r.fetched)
                for part in order:
                    r.weights.fetch(part, held_at(r, part))
            if SUMS in outputs:
                r.sums[...] = jnp.zeros(r.sums.shape, F32)
            body(r)
            r.finish()

        if active is None or always:
            run()
        else:
            pl.when(refs[ACTIVE][0] == 1)(run)

    keys = list(operands)
    results = pl.pallas_call(
        kernel,
        out_shape=list(outputs.values()),
        in_specs=[IN_VMEM if key in ins else IN_HBM for key in keys] + [IN_HBM] * len(sources) + ([IN_SMEM] if active is not None else []),
        out_specs=[IN_HBM] * len(outputs),
        scratch_shapes=list(scratch.values()),
        input_output_aliases={
            index: list(outputs).index(key[len(BEFORE) :])
            for index, key in enumerate(keys)
            if key.startswith(BEFORE)
        },
        compiler_params=pltpu.CompilerParams(vmem_limit_bytes=VMEM_LIMIT),
        cost_estimate=pl.CostEstimate(
            flops=flops // 4 if light else flops, bytes_accessed=moved // 4 if light else moved, transcendentals=0
        ),
        name=name,
    )(*operands.values(), *sources, *([active] if active is not None else []))
    return dict(zip(outputs, results))


def field(rows, kind=BF16, width=WIDTH):
    return shape((rows, width), kind)


def planes_scratch(sides, rows):
    return pltpu.VMEM((3 * sides, rows + 2 * rows // SIDE, WIDTH), BF16)


def run_forward(decoder, shared, hidden, skipped, weights_for, modulation, common, before, active):
    rows = hidden.shape[0]
    octets = rows // SIDE
    inputs = {HIDDEN: hidden, **({SKIPPED: skipped} if decoder else {}), **common}
    inputs.update(before)
    stat = shape((2, octets, WIDTH), F32)
    first_out = {
        CONV_ONE: field(rows, F32),
        STAT_C: stat,
        FIELDS: field(WIDTH + (2 * GROUPS if shared else WIDTH), width=rows),
        COLUMNS_W: field(WIDTH, width=rows),
        STAT_H: stat,
        **({STAT_S: stat} if decoder else {}),
    }
    first_scratch = {
        "turned": pltpu.VMEM(first_out[FIELDS].shape, BF16),
        "turned_w": pltpu.VMEM((WIDTH, rows), BF16),
        "fields_sems": pltpu.SemaphoreType.DMA((2,)),
        PLANES: planes_scratch(1 + decoder, rows),
        **held_scratch(decoder, (CONV_IN,)),
    }
    second_names = (CONV_OUT, *((SKIP,) if decoder else ()), *SMALL)
    second_out = {
        RESULT: field(rows),
        RESIDUAL: field(rows, F32),
        STAT_R: stat,
        ATTEND: field(rows),
        PROJECT: field(rows, width=3 * WIDTH),
        MIXED: field(rows),
    }
    second_scratch = {
        "grid": pltpu.VMEM((SIDE, octets // 8, 8, WIDTH), F32),
        PLANES: planes_scratch(1, rows),
        **held_scratch(decoder, second_names),
    }
    first_flops = 2 * rows * (1 + decoder) * TAPS * WIDTH * WIDTH
    second_flops = 2 * rows * (TAPS + 6) * WIDTH * WIDTH

    def first_body(r):
        conv_in_forward(r, decoder, shared, octets)

    def second_body(r):
        block_forward(r, decoder, octets)

    def both(r):
        first_body(r)
        second_body(r)

    if not decoder:
        names = (CONV_IN, *second_names)
        return call(
            both,
            "encoder_forward",
            {**inputs, MODULATION: modulation},
            {**first_out, **second_out},
            {**second_scratch, **first_scratch, MIDDLE: pltpu.VMEM((rows, WIDTH), BF16)},
            weights_for(decoder, *names),
            names,
            active,
            (FIELDS, COLUMNS_W),
            first_flops + second_flops,
        )
    first = call(
        first_body,
        "conv_in_forward",
        {**inputs, MODULATION: modulation},
        {**first_out, MIDDLE: field(rows)},
        first_scratch,
        weights_for(decoder, CONV_IN),
        (CONV_IN,),
        active,
        (FIELDS, COLUMNS_W),
        first_flops,
    )
    second = call(
        second_body,
        "block_forward",
        {HIDDEN: hidden, SKIPPED: skipped, MIDDLE: first[MIDDLE], **common},
        second_out,
        second_scratch,
        weights_for(decoder, *second_names),
        second_names,
        active,
        (),
        second_flops,
    )
    return {**first, **second}


def run_backward(decoder, joined, shards, with_skip, part, entry, weights_for, modulation, common, before, active):
    rows = entry[HIDDEN].shape[0]
    octets = rows // SIDE
    first, second = part in (0, None), part in (1, None)
    inputs, names = {}, ()
    if first:
        names += (OUT_NAME, *SMALL[:3], CONV_OUT)
        used = [GRAD_OUT, PROJECT, RESIDUAL, STAT_R, ATTEND, MIXED, CONV_ONE, STAT_C]
        inputs.update({name: entry[name] for name in used}, modulation=modulation, **before)
    if second:
        names += (CONV_IN, *((SKIP,) if decoder else ()))
    if second or with_skip:
        inputs[HIDDEN] = entry[HIDDEN]
        if decoder or with_skip:
            inputs[SKIPPED] = entry[SKIPPED]
    if second:
        inputs[STAT_H] = entry[STAT_H]
        if decoder:
            inputs[STAT_S] = entry[STAT_S]
    between = {GRAD_RESID: field(rows, F32), GRAD_RESID_B: field(rows), "grad_conv_b": field(rows)}
    outputs = {SUMS: field(16, F32)}
    scratch = {PLANES: planes_scratch(1, rows), **held_scratch(decoder, names)}
    if first:
        outputs[PRODUCTS] = field(WIDTH, width=(6 if with_skip else 4) * WIDTH)
        outputs[PAYLOAD] = field(2 * rows + 16)
        scratch.update(
            grid=pltpu.VMEM((SIDE, octets // 8, 8, 3 * WIDTH), F32),
            grad_project=pltpu.VMEM((rows, 3 * WIDTH), BF16),
            built=pltpu.VMEM(outputs[PRODUCTS].shape, BF16),
            built_sems=pltpu.SemaphoreType.DMA((3,)),
            rows=pltpu.VMEM(outputs[PAYLOAD].shape, BF16),
            payload_sem=pltpu.SemaphoreType.DMA,
        )
    if part == 0:
        outputs.update(between)
    elif part == 1:
        inputs.update({name: entry[name] for name in between if decoder or name != GRAD_RESID_B})
    else:
        scratch.update({name: pltpu.VMEM(value.shape, value.dtype) for name, value in between.items()})
    scratch["sides"] = pltpu.VMEM((1 + (decoder and second), rows, WIDTH), F32)
    if second:
        if joined:
            outputs[GRAD_JOINED] = field(rows)
            scratch["total"] = pltpu.VMEM((rows, WIDTH), F32)
        else:
            outputs[GRAD_HIDDEN] = field(rows, F32)
            if decoder:
                outputs[GRAD_SKIPPED] = field(rows, F32)

    def body(r):
        r.work = r.sides.at[0]
        if first:
            attention_backward(r, decoder, octets, shards, with_skip)
            middle_backward(r, octets)
        if second:
            conv_in_backward(r, decoder, joined, octets, first)

    return call(
        body,
        "section_backward" if part is None else ("block_backward", "conv_in_backward")[part],
        {**inputs, **common},
        outputs,
        scratch,
        weights_for(decoder, *names),
        names,
        active,
        (PRODUCTS, PAYLOAD),
        2 * rows * (first * (TAPS + 14) + second * (1 + decoder) * TAPS) * WIDTH * WIDTH,
    )


def tap_at(place, index, rows, channels):
    block = rows // TAPS
    per_tap = channels // block
    position = place * TAPS + index
    tap = lax.div(position, per_tap)
    start = pl.multiple_of(lax.rem(position, per_tap) * block, 16)
    return lax.div(tap, 3) - 1, lax.rem(tap, 3) - 1, start, block


def shifted_field(values, down, across, octets, also=None):
    width = values.shape[1]
    lane = lax.broadcasted_iota(jnp.int32, (1, width), 1)
    row, column = lax.div(lane, octets) + down, (lane & 7) + across
    inside = (row >= 0) & (row < SIDE) & (column >= 0) & (column < 8)
    if also is not None:
        inside = inside & also(lane)
    back = lax.rem(width - (octets * down + across), width)
    return jnp.where(inside, pltpu.roll(values, back, 1), 0.0).astype(BF16)


def columns_in_kernel(octets, shared, place, order, fields, affine, cols_in, *cols_skip):
    width = fields.shape[2]
    rows = cols_in.shape[0]
    for index in range(TAPS):
        down, across, start, block = tap_at(place[0], index, rows, 2 * WIDTH)
        side = lax.div(start, WIDTH)
        spot = pl.multiple_of(start - side * WIDTH if shared else start, 16)
        values = fields[0, pl.ds(spot, block), :].astype(F32)
        values = values * affine[pl.ds(start, block), 0:1] + affine[pl.ds(start, block), 1:2]
        values = values * sigmoid(values)
        kept = lax.mul(side, 1 - place[1]) * width
        cols_in[pl.ds(index * block, block), :] = shifted_field(
            values, down, across, octets, lambda lane: lane >= kept
        )
    if shared:
        rows = cols_skip[0].shape[0]
        start = pl.multiple_of(lax.rem(place[0] * rows, WIDTH), 16)
        channel = lax.broadcasted_iota(jnp.int32, (rows, GROUPS), 0) + start
        group = lax.broadcasted_iota(jnp.int32, (rows, GROUPS), 1) * PER_GROUP
        member = jnp.where((channel >= group) & (channel < group + PER_GROUP), 1.0, 0.0).astype(BF16)
        mean = dot(member, fields[0, pl.ds(WIDTH, GROUPS), :])
        deviation = dot(member, fields[0, pl.ds(WIDTH + GROUPS, GROUPS), :])
        values = fields[0, pl.ds(start, rows), :].astype(F32) * deviation + mean
        lane = lax.broadcasted_iota(jnp.int32, (1, width), 1)
        cols_skip[0][...] = jnp.where(lane < place[1] * width, values, 0.0).astype(BF16)


def tap_slices_plain(fields, rows, channels, place, octets):
    pieces, _, width = fields.shape
    spots = place * rows + jnp.arange(rows)
    taps = spots // channels
    values = jnp.take(fields, spots % channels, axis=1)
    lane = jnp.arange(width)
    total = jnp.zeros_like(values)
    for tap in range(TAPS):
        down, across = tap // 3 - 1, tap % 3 - 1
        row, column = lane // octets + down, lane % 8 + across
        inside = (row >= 0) & (row < SIDE) & (column >= 0) & (column < 8)
        moved = jnp.roll(values, -(octets * down + across), axis=2)
        total = jnp.where((taps == tap)[None, :, None] & inside, moved, total)
    return total.transpose(1, 0, 2).reshape(rows, pieces * width)


def columns_in(fields, order, affine, rows_in, rows_skip, place, decoder, octets, shared):
    _, height, width = fields.shape
    pieces = order.shape[0]
    if not shared and rows_in % (TAPS * 16):
        fields = jnp.take(fields, order, axis=0)
        sides = fields.astype(F32) * affine[:, :1] + affine[:, 1:]
        keep = (jnp.arange(2 * WIDTH)[:, None] < WIDTH) | decoder
        sides = jnp.where(keep, jax.nn.silu(sides), 0.0).astype(BF16)
        return [tap_slices_plain(sides, rows_in, 2 * WIDTH, place, octets)]
    heights = (rows_in, rows_skip) if shared else (rows_in,)
    return pl.pallas_call(
        partial(columns_in_kernel, octets, shared),
        grid_spec=pltpu.PrefetchScalarGridSpec(
            num_scalar_prefetch=2,
            grid=(pieces,),
            in_specs=[
                pl.BlockSpec((1, height, width), lambda piece, place, order: (order[piece], 0, 0)),
                pl.BlockSpec((2 * WIDTH, 2), lambda piece, place, order: (0, 0)),
            ],
            out_specs=[pl.BlockSpec((rows, width), lambda piece, place, order: (0, piece)) for rows in heights],
        ),
        out_shape=[shape((rows, pieces * width), BF16) for rows in heights],
        compiler_params=pltpu.CompilerParams(vmem_limit_bytes=VMEM_LIMIT),
        cost_estimate=pl.CostEstimate(
            flops=0, bytes_accessed=pieces * height * width, transcendentals=0
        ),
        name="columns_in",
    )(jnp.stack([place, decoder.astype(jnp.int32)]).astype(jnp.int32), order, fields, affine)


def columns_out(blocks, rows, place, octets):
    fields = [
        (number, first) for number, block in enumerate(blocks) for first in range(0, block.shape[0], WIDTH)
    ]
    if rows % (TAPS * 16):
        taken = jnp.stack([blocks[number][first : first + WIDTH] for number, first in fields])
        return tap_slices_plain(taken, rows, WIDTH, place, octets)
    width = blocks[0].shape[1]

    def body(r):
        for index in range(TAPS):
            down, across, start, block = tap_at(r.active[0], index, rows, WIDTH)
            for column, (number, first) in enumerate(fields):
                values = getattr(r, BLOCK + str(number))[pl.ds(start + first, block), :].astype(F32)
                r.cols[pl.ds(index * block, block), pl.ds(column * width, width)] = shifted_field(
                    values, down, across, octets
                )

    operands = {BLOCK + str(number): block for number, block in enumerate(blocks)}
    return call(
        body,
        "columns_out",
        operands,
        {COLS_NAME: field(rows, width=len(fields) * width)},
        {},
        active=place.reshape(1).astype(jnp.int32),
        always=True,
        light=True,
    )[COLS_NAME]


def grad_step(cols, blocks, totals):
    sides = len(cols[0])
    count = len(blocks) // len(cols)
    depth = cols[0][0].shape[1] // count

    def body(r):
        for side, part in enumerate(cols[0]):
            target = getattr(r, TOTAL + str(side))
            rows = part.shape[0]
            tile = rows // 3 if rows % 48 == 0 and rows > 128 else rows
            for start in range(0, rows, tile):
                total = getattr(r, PRIOR + str(side))[pl.ds(start, tile), :] if totals else None
                for number in range(len(blocks)):
                    factor = getattr(r, COLS + str(number // count * sides + side))
                    product = dot(
                        factor[pl.ds(start, tile), pl.ds(number % count * depth, depth)],
                        getattr(r, BLOCK + str(number))[pl.ds(depth if side == 1 else 0, depth), :],
                    )
                    total = product if total is None else total + product
                target[pl.ds(start, tile), :] = total
            r.flush(TOTAL + str(side))

    every = [part for step in cols for part in step]
    operands = {COLS + str(index): part for index, part in enumerate(every)}
    operands.update({BLOCK + str(number): block for number, block in enumerate(blocks)})
    if totals:
        operands.update({PRIOR + str(side): total for side, total in enumerate(totals)})
    outputs = {TOTAL + str(side): field(part.shape[0], F32) for side, part in enumerate(cols[0])}
    flops = 2 * sum(part.shape[0] * part.shape[1] for part in every) * WIDTH
    return list(call(body, "grad_step", operands, outputs, {}, flops=flops, light=True).values())


def last_rows(blocks, first):
    def body(r):
        copies = [
            pltpu.make_async_copy(
                getattr(r, BLOCK + str(index)).at[pl.ds(first, r.taken.shape[1])], r.landed.at[index], r.sems.at[index]
            )
            for index in range(len(blocks))
        ]
        for copy in copies:
            copy.start()
        for copy in copies:
            copy.wait()
        r.taken[...] = r.landed[...]

    operands = {BLOCK + str(index): block for index, block in enumerate(blocks)}
    taken = shape((len(blocks), blocks[0].shape[0] - first, blocks[0].shape[1]), blocks[0].dtype)
    scratch = {"sems": pltpu.SemaphoreType.DMA((len(blocks),)), "landed": pltpu.VMEM(taken.shape, taken.dtype)}
    return call(body, "last_rows", operands, {TAKEN: taken}, scratch, far=operands)[TAKEN]


class Doubling:
    def __init__(self, value, axis):
        self.axis, self.value, self.distance = axis, value[None], 1

    def step(self):
        count, index = lax.axis_size(self.axis), lax.axis_index(self.axis)
        if self.distance < count:
            pairs = [(i, i ^ self.distance) for i in range(count)]
            other = lax.ppermute(self.value, self.axis, pairs)
            self.value = jnp.where(
                (index // self.distance) % 2 == 0,
                jnp.concatenate([self.value, other], axis=0),
                jnp.concatenate([other, self.value], axis=0),
            )
            self.distance *= 2

    def finish(self):
        while self.distance < lax.axis_size(self.axis):
            self.step()
        return self.value


class Ring:
    def __init__(self, value, axis):
        self.axis = axis
        self.count = lax.axis_size(axis)
        self.stride = self.count // 4
        self.values, self.rows, self.steps = [value], [], []

    def send(self, value, target):
        return lax.ppermute(value, self.axis, [(i, target(i)) for i in range(self.count)])

    def around(self, value, steps=1):
        return self.send(value, lambda i: (i + steps * self.stride) % self.count)

    def besides(self, value):
        row, stride = [value], self.stride
        for _ in range(stride // 2 - 1):
            row.append(self.send(row[-1], lambda i: i // stride * stride + (i + 2) % stride))
        return row

    def with_core(self, row):
        return row + [self.send(part, lambda i: i ^ 1) for part in row]

    def turn(self):
        self.values.append(self.around(self.values[-1]))

    def spread(self):
        self.rows.append(self.besides(self.values[len(self.rows)]))

    def spread_last(self):
        stride, half = self.stride, self.values[3].shape[0] // 32 * 16
        row = [self.values[3]]
        for index in range(1, stride // 2):
            beside = self.send(row[-1][:half], lambda i: i // stride * stride + (i + 2) % stride)
            turned = self.around(self.rows[2][index][half:])
            row.append(jnp.concatenate([beside, turned], axis=0))
        self.rows.append(row)

    def share(self, step):
        self.steps.append(self.with_core(self.rows[step]))


def ring_order(axis, step):
    index, stride = lax.axis_index(axis), lax.axis_size(axis) // 4
    quarter = (index // stride + 4 - step) % 4 * stride
    sources = []
    for core in range(2):
        for beside in range(stride // 2):
            sources.append(quarter + (index % stride + stride - 2 * beside) % stride // 2 * 2 + (index + core) % 2)
    return jnp.stack(sources).astype(jnp.int32)


def together(*values):
    return lax.optimization_barrier(values)


def moved(value, source, target):
    return lax.ppermute(value, SECTION, [(source, target)])


def to_rows(value):
    micro, images, pixels, channels = value.shape
    count = micro * images
    return (
        value.reshape(count, pixels // 8, 8, channels).transpose(1, 0, 2, 3).reshape(-1, channels)
    )


def from_rows(value, images):
    count = MICRO * images
    channels = value.shape[-1]
    grid_rows = value.shape[0] // (8 * count)
    planes = value.reshape(grid_rows, count, 8, channels).transpose(1, 0, 2, 3)
    return planes.reshape(MICRO, images, grid_rows * 8, channels)


def noise_columns(pair_ids, columns):
    fraction = pair_ids.astype(F32) / (LEVELS - 1)
    top_root = SIGMA_HIGH ** (1.0 / 7.0)
    bottom_root = SIGMA_LOW ** (1.0 / 7.0)
    sigmas = (top_root + fraction * (bottom_root - top_root)) ** 7
    log_scale = 250.0 * jnp.log(sigmas)
    quarter = EMBED // 4
    kind = columns // quarter
    frequency = jnp.exp(-math.log(10000.0) * (columns % quarter).astype(F32) / quarter)
    angles = jnp.where(kind < 2, log_scale[:, :1], log_scale[:, 1:]) * frequency
    return jnp.where(kind % 2 == 0, jnp.cos(angles), jnp.sin(angles))


def block_homes(shards, rows_in):
    block = rows_in // TAPS
    per_tap = 2 * WIDTH // block
    mine = [[i for i in range(TAPS) if (TAPS * d + i) % per_tap < per_tap // 2] for d in range(shards)]
    slots = max(-(-(len(mine[d]) + len(mine[d ^ 1])) // 2) for d in range(shards))
    sent = [mine[d][slots:] for d in range(shards)]
    most = max(1, max(len(part) for part in sent))
    offers, names = [], []
    for d in range(shards):
        kept = mine[d][:slots]
        offer = kept + [TAPS + i for i in range(len(sent[d ^ 1]))]
        names.append([TAPS * d + i for i in kept] + [TAPS * (d ^ 1) + i for i in sent[d ^ 1]])
        offers.append(offer + [0] * (slots - len(offer)))
    sends = [part + [0] * (most - len(part)) for part in sent]
    return np.array(sends, np.int32), np.array(offers, np.int32), names, slots


def spans(name_rows, cuts):
    found, start = {}, 0
    for name, count in name_rows:
        found[name], first, base = [], 0, 0
        for array, height in enumerate(cuts):
            low, high = max(start, base), min(start + count, base + height)
            if low < high:
                found[name].append((array, low - base, low - start, high - low))
            base += height
        start += count
    return found


def section_weights(conv_in, conv_out, skip_proj, qkv_proj, out_proj, is_decoder):
    shards, me = lax.axis_size(DP), lax.axis_index(DP)
    qkv_parts = [qkv_proj[:, part * WIDTH : (part + 1) * WIDTH] for part in range(3)]
    small = dict(zip(SMALL, (*qkv_parts, out_proj)))
    shares = {CONV_IN: conv_in, CONV_OUT: conv_out, **small, SKIP: skip_proj}
    heights = [(name, part.shape[0]) for name, part in shares.items()]
    if any(height % 16 for _, height in heights) or conv_in.shape[0] % (TAPS * 16):
        whole = {name: lax.all_gather(part, DP, axis=0, tiled=True)[None] for name, part in shares.items()}
        sources = list(whole.values())
        plan = {name: [(index, 0, 0, 0, part.shape[1])] for index, (name, part) in enumerate(whole.items())}
        encoder_plan = dict(plan)
        encoder_plan[CONV_IN] = [(0, 0, tap * 2 * WIDTH, tap * WIDTH, WIDTH) for tap in range(TAPS)]
        return sources, encoder_plan, plan
    sends, offers, names, slots = block_homes(shards, conv_in.shape[0])
    blocks = conv_in.reshape(TAPS, -1, WIDTH)
    block = blocks.shape[1]
    other = lax.ppermute(
        jnp.take(blocks, jnp.asarray(sends)[me], axis=0), DP, [(i, i ^ 1) for i in range(shards)]
    )
    chosen = jnp.take(jnp.concatenate([blocks, other], axis=0), jnp.asarray(offers)[me], axis=0)
    encoder_parts = [chosen.reshape(slots * block, WIDTH), conv_out, *small.values()]
    encoder_rows = sum(part.shape[0] for part in encoder_parts)
    first_rows = max(encoder_rows, sum(height for name, height in heights if name not in (OUT_NAME, SKIP)))
    everything = jnp.concatenate(list(shares.values()), axis=0)
    encoder_parts.append(jnp.zeros((first_rows - encoder_rows, WIDTH), BF16))
    first = lax.all_gather(
        jnp.where(is_decoder, everything[:first_rows], jnp.concatenate(encoder_parts, axis=0)), DP, axis=0
    )
    second = lax.all_gather(everything[first_rows:], DP, axis=0)

    def plan_of(found):
        return {
            name: [
                (array, piece, row, piece * height + start, count)
                for piece in range(shards)
                for array, row, start, count in found[name]
            ]
            for name, height in heights
            if name in found
        }

    decoder_plan = plan_of(spans(heights, (first_rows, everything.shape[0] - first_rows)))
    encoder_plan = plan_of(
        spans([("blocks", slots * block)] + [item for item in heights if item[0] in (CONV_OUT, *SMALL)], (encoder_rows,))
    )
    per_tap = 2 * WIDTH // block
    encoder_plan[CONV_IN] = sorted(
        (
            (0, piece, slot * block, name // per_tap * WIDTH + name % per_tap * block, block)
            for piece in range(shards)
            for slot, name in enumerate(names[piece])
        ),
        key=lambda entry: entry[3],
    )
    return [first, second], encoder_plan, decoder_plan


def on_device(
    level_input,
    cotangent,
    class_table,
    conv_in,
    conv_out,
    embed_proj,
    skip_proj,
    qkv_proj,
    out_proj,
    gains,
    biases,
    noise_pairs,
    classes,
):
    sections = lax.axis_size(SECTION)
    section_id = lax.axis_index(SECTION)
    shards = lax.axis_size(DP)
    shard_id = lax.axis_index(DP)
    images = level_input.shape[1]
    count = MICRO * images
    octets = 8 * count
    rows = SIDE * octets

    is_decoder = section_id >= sections // 2
    skip_by_columns = sections == 2
    sources, encoder_plan, decoder_plan = section_weights(
        conv_in[0], conv_out[0], skip_proj[0], qkv_proj[0], out_proj[0], is_decoder
    )

    gain_share, bias_share = gains.shape[1], biases.shape[1]
    small = jnp.concatenate(
        [
            gains[0].astype(F32),
            biases[0].astype(F32),
            noise_pairs.reshape(-1).astype(F32),
            classes.reshape(-1).astype(F32),
        ]
    )
    spare = -small.shape[0] % LANE
    every = Doubling(jnp.pad(small, (0, spare))[None], DP).finish()[:, 0]
    cut = gain_share + bias_share
    params = jnp.concatenate(
        [every[:, :gain_share].reshape(4, WIDTH), every[:, gain_share:cut].reshape(12, WIDTH)],
        axis=0,
    )
    all_images = shards * count
    pair_ids = every[:, cut : cut + 2 * count].reshape(all_images, 2)
    class_ids = every[:, cut + 2 * count : cut + 3 * count].reshape(all_images).astype(jnp.int32)

    slice_width = class_table.shape[1]
    columns = shard_id * slice_width + jnp.arange(slice_width)[None, :]
    onehot = (class_ids[:, None] == jnp.arange(CLASSES)[None, :]).astype(BF16)
    pre = noise_columns(pair_ids, columns) + dot(onehot, class_table)
    embed_b = jax.nn.silu(pre).astype(BF16)
    shares = dot(embed_b, embed_proj[0]).astype(BF16).reshape(shards, count, 2 * WIDTH)
    modulation = lax.all_to_all(shares, DP, 0, 0).astype(F32).sum(axis=0)
    modulation = modulation + params[BIAS + 3 : BIAS + 5].reshape(1, 2 * WIDTH)
    modulation = jnp.repeat(modulation, 8, axis=0)

    level_own, top_own = to_rows(level_input), to_rows(cotangent)
    level_rows = jnp.concatenate(
        [level_own] + [moved(level_own, source, 0) for source in range(1, sections)], axis=0
    )
    top_rows = jnp.concatenate(
        [moved(top_own, source, sections - 1) for source in range(sections - 1)] + [top_own], axis=0
    )

    orders = [ring_order(DP, step) for step in range(4)]
    order = jnp.concatenate(orders)

    def in_order(values):
        return jnp.take(values.reshape(shards, count, -1), order, axis=0).reshape(all_images, -1)

    common = {
        "params": params,
        "group_of": jnp.asarray(GROUP_OF, BF16),
        "group_of_t": jnp.asarray(GROUP_OF.T, BF16),
    }
    level_rows, top_rows, modulation, embed_late, pre_late, onehot_late = together(
        level_rows, top_rows, modulation, in_order(embed_b), in_order(pre), in_order(onehot)
    )

    def weights_for(decoder, *names):
        plan = decoder_plan if decoder else encoder_plan
        used = sorted({entry[0] for name in names for entry in plan[name]})
        return [sources[index] for index in used], {
            name: [(used.index(entry[0]), *entry[1:]) for entry in plan[name]] for name in names
        }

    kept = []
    skips = {}
    hidden = level_rows
    result = None
    before = {}
    for tick in range(sections):
        decoder = tick >= sections // 2
        mirror = sections - 1 - tick
        active = (section_id == tick).astype(jnp.int32).reshape(1)
        skipped = skips[tick] if decoder else hidden
        outs = run_forward(
            decoder, sections == 2, hidden, skipped, weights_for, modulation, common, before, active
        )
        before = {"before_fields": outs[FIELDS], "before_columns_w": outs[COLUMNS_W]}
        result = outs[RESULT]
        entry = {HIDDEN: hidden, SKIPPED: skipped, STAT_S: outs[STAT_H], **outs}
        for name in (FIELDS, COLUMNS_W, RESULT, MIDDLE):
            entry.pop(name, None)
        if sections > 2 and kept:
            entry = {name: jnp.where(section_id == tick, value, kept[-1][name]) for name, value in entry.items()}
            kept = [entry] * (tick + 1)
        else:
            kept.append(entry)
        if tick < sections - 1:
            hidden = moved(result, tick, tick + 1)
            if not decoder:
                skips[mirror] = hidden if mirror == tick + 1 else moved(result, tick, mirror)

    def own(values):
        if sections > 2 and values[0] is values[-1]:
            return values[0]
        chosen = values[0]
        for tick in range(1, sections):
            chosen = jnp.where(section_id == tick, values[tick], chosen)
        return chosen

    fields = lax.all_gather(outs[FIELDS], DP, axis=0)
    circle = Ring(outs[COLUMNS_W], DP)
    columns_w, kept[-1] = together(outs[COLUMNS_W], kept[-1])
    turned = {0: columns_w}
    w_rows, w_steps = {}, {}

    def beside(stage, *values):
        if stage == 0:
            turned.update({step % 4: circle.around(turned[0], step) for step in (1, -1)})
            w_rows[0] = circle.besides(turned[0])
        if stage == 1:
            turned[2] = circle.around(turned[1])
            w_rows.update({step: circle.besides(turned[step]) for step in (1, 3)})
        if stage == 2:
            w_rows[2] = circle.besides(turned[2])
        for step in ((), (0,), (1, 3), (2,))[stage]:
            other = circle.send(jnp.concatenate(w_rows[step], axis=0), lambda i: i ^ 1)
            w_steps[step] = [*w_rows[step], other]
        state, *values = together((turned, w_rows, w_steps), *values)
        for old, new in zip((turned, w_rows, w_steps), state):
            old.update(new)
        return values

    def to_owners(value, source):
        share = rows // sections
        pieces = [value[index * share : (index + 1) * share] for index in range(sections)]
        total = jnp.where(section_id == source, pieces[source], jnp.zeros_like(pieces[source]))
        for target in range(sections):
            if target != source:
                total = total + moved(pieces[target].astype(BF16), source, target).astype(value.dtype)
        return from_rows(total, images)


    sums_of = [None] * sections
    skip_grads = {}
    grad_out = top_rows
    before = {}
    for tick in reversed(range(sections)):
        decoder = tick >= sections // 2
        mirror = sections - 1 - tick
        entry = kept[tick]
        if not decoder and tick in skip_grads:
            grad_out = grad_out.astype(F32) + skip_grads[tick].astype(F32)
        joined = decoder and mirror == tick - 1
        active = (section_id == tick).astype(jnp.int32).reshape(1)

        def backward(part, entry, decoder=decoder, joined=joined, active=active):
            return run_backward(
                decoder, joined, shards, not skip_by_columns, part, entry, weights_for, modulation, common, before, active
            )

        outs = backward(0 if tick == 0 else None, {**entry, GRAD_OUT: grad_out})
        if tick == sections - 1:
            level_output = to_owners(result, sections - 1)
            outs, level_output = beside(0, outs, level_output)
        if tick == 0:
            (outs,) = beside(1, outs)
        before = {"before_products": outs[PRODUCTS], "before_payload": outs[PAYLOAD]}
        sums_of[tick] = outs[SUMS]
        if joined:
            grad_out = moved(outs[GRAD_JOINED], tick, mirror)
        elif tick:
            if decoder:
                skip_grads[mirror] = moved(outs[GRAD_SKIPPED].astype(BF16), tick, mirror)
            grad_out = moved(outs[GRAD_HIDDEN].astype(BF16), tick, tick - 1)
    products, payload = outs[PRODUCTS], outs[PAYLOAD]

    affine = jnp.stack([params[GAIN : GAIN + 2].reshape(-1), params[BIAS : BIAS + 2].reshape(-1)], axis=1)

    def cols_in_of(step):
        return columns_in(
            fields,
            orders[step],
            affine,
            conv_in.shape[1],
            skip_proj.shape[1],
            shard_id,
            is_decoder,
            octets,
            sections == 2,
        )

    def with_out(step, others):
        return [columns_out(w_steps[step], conv_out.shape[1], shard_id, octets), *others]

    ring = Ring(payload, DP)
    cols = []

    small_grads = lax.psum_scatter(products, DP, scatter_dimension=0, tiled=True)
    ring.turn()
    ring.spread()
    last = backward(1, {**entry, **outs})
    cols.append(cols_in_of(0))
    ring.values, ring.rows, fields, cols, sums_of[0], input_rows = beside(
        2, ring.values, ring.rows, fields, cols, sums_of[0] + last[SUMS], last[GRAD_HIDDEN]
    )
    sums = own(sums_of)
    shares = jnp.concatenate([sums[:4].reshape(shards, gain_share), sums[4:].reshape(shards, bias_share)], axis=1)
    summed = lax.all_to_all(shares, DP, 0, 0, tiled=True).sum(axis=0)
    ring.turn()
    ring.spread()
    ring.share(0)
    cols = [with_out(0, cols[0]), with_out(1, cols_in_of(1))]
    ring.values, ring.rows, ring.steps, cols, fields, input_rows, summed = beside(
        3, ring.values, ring.rows, ring.steps, cols, fields, input_rows, summed
    )
    ring.turn()
    ring.spread()
    ring.share(1)
    cols += [with_out(step, cols_in_of(step)) for step in (2, 3)]
    totals = grad_step(cols[:1], ring.steps[0], None)
    ring.values, ring.rows, ring.steps, cols, input_rows, totals = together(
        ring.values, ring.rows, ring.steps, cols, input_rows, totals
    )
    ring.spread_last()
    ring.share(2)
    input_grad = to_owners(input_rows, 0)
    totals = grad_step(cols[1:3], ring.steps[1] + ring.steps[2], totals)
    ring.rows, ring.steps, cols, totals, input_grad, small_grads = together(
        ring.rows, ring.steps, cols, totals, input_grad, small_grads
    )
    small_grads = small_grads.astype(F32)
    qkv_grad = small_grads[:, : 3 * WIDTH]
    out_grad = small_grads[:, 3 * WIDTH : 4 * WIDTH]
    ring.share(3)
    totals = grad_step(cols[3:], ring.steps[3], totals)
    conv_out_grad, conv_in_grad = totals[:2]
    gains_grad, biases_grad = summed[:gain_share], summed[gain_share:]

    mods = last_rows([block for step in ring.steps for block in step], 2 * rows)
    mods = jnp.concatenate(
        [mods[:, start : start + count].reshape(all_images, WIDTH) for start in (0, count)], axis=1
    )
    embed_grad = dot_tn(embed_late, mods)
    grad_embed = dot_nt(mods, embed_proj[0])
    if sections == 2:
        grad_embed = grad_embed + lax.ppermute(grad_embed, SECTION, [(0, 1), (1, 0)])
    else:
        grad_embed = lax.psum(grad_embed, SECTION)
    grad_pre = jax.vjp(jax.nn.silu, pre_late)[1](grad_embed)[0]
    table_grad = lax.dot_general(
        onehot_late.astype(F32),
        grad_pre,
        (((0,), (0,)), ((), ())),
        precision=lax.Precision.HIGHEST,
        preferred_element_type=F32,
    )

    if skip_by_columns:
        skip_grad = totals[2]
    else:
        skip_grad = jnp.concatenate(
            [small_grads[:, 4 * WIDTH : 5 * WIDTH], small_grads[:, 5 * WIDTH :]], axis=0
        )
    return (
        level_output,
        input_grad,
        table_grad,
        conv_in_grad[None],
        conv_out_grad[None],
        embed_grad[None],
        skip_grad[None],
        qkv_grad[None],
        out_grad[None],
        gains_grad[None],
        biases_grad[None],
    )


def solution(mesh):
    placed = (
        P(None, DP, SECTION, None),
        P(None, DP, SECTION, None),
        P(None, DP),
        P(SECTION, DP, None),
        P(SECTION, DP, None),
        P(SECTION, DP, None),
        P(SECTION, DP, None),
        P(SECTION, DP, None),
        P(SECTION, DP, None),
        P(SECTION, DP),
        P(SECTION, DP),
        P(None, DP, None),
        P(None, DP),
    )
    return jax.shard_map(
        on_device,
        mesh=mesh,
        in_specs=placed,
        out_specs=(
            P(None, DP, SECTION, None),
            P(None, DP, SECTION, None),
            P(None, DP),
            P(SECTION, DP, None),
            P(SECTION, DP, None),
            P(SECTION, DP, None),
            P(SECTION, DP, None),
            P(SECTION, DP, None),
            P(SECTION, DP, None),
            P(SECTION, DP),
            P(SECTION, DP),
        ),
        check_vma=False,
    )
```
